128 devices in a mesh: seq: 16 (over x, z_hi, core), batch: 8 (over y, z_lo).
Axes of the slice: x: 4, y: 4, z: 4 (z_hi: 2, z_lo: 2; z = z_hi * 2 + z_lo), core: 2. Of those that a mesh axis runs over, the one named last changes fastest.
Arguments:
- inputs: float32 [8, 4096, 768], P('batch', 'seq'), may hold values from -6 to 6
- query_weight: float32 [768, 768], P(('seq', 'batch')), may hold values from -0.21875 to 0.21875
- key_weight: float32 [768, 768], P(('seq', 'batch')), may hold values from -0.21875 to 0.21875
- value_weight: float32 [768, 768], P(('seq', 'batch')), may hold values from -0.21875 to 0.21875
- out_weight: float32 [768, 768], P(('seq', 'batch')), may hold values from -2.5 to 2.5
- up_weight: float32 [768, 3072], P(('seq', 'batch')), may hold values from -0.21875 to 0.21875
- down_weight: float32 [3072, 768], P(('seq', 'batch')), may hold values from -0.109375 to 0.109375
- gain_one: float32 [768], P(('seq', 'batch')), may hold values from 0.1 to 1.9
- offset_one: float32 [768], P(('seq', 'batch')), may hold values from -3 to 3
- gain_two: float32 [768], P(('seq', 'batch')), may hold values from 0.1 to 1.9
- offset_two: float32 [768], P(('seq', 'batch')), may hold values from -3 to 3
- pos_bias: float32 [256], P(('seq', 'batch')), may hold values from -4 to 4
- prefix_len: int32 [8], P('batch'), may hold values from 0 to 3840, as said below
- cotangent: float32 [8, 4096, 768], P('batch', 'seq'), may hold values from -6 to 6
Outputs:
- output: float32 [8, 4096, 768], P('batch', 'seq')
- input_grad: float32 [8, 4096, 768], P('batch', 'seq')
- query_weight_grad: float32 [768, 768], P(('seq', 'batch'))
- key_weight_grad: float32 [768, 768], P(('seq', 'batch'))
- value_weight_grad: float32 [768, 768], P(('seq', 'batch'))
- out_weight_grad: float32 [768, 768], P(('seq', 'batch'))
- up_weight_grad: float32 [768, 3072], P(('seq', 'batch'))
- down_weight_grad: float32 [3072, 768], P(('seq', 'batch'))
- gain_one_grad: float32 [768], P(('seq', 'batch'))
- offset_one_grad: float32 [768], P(('seq', 'batch'))
- gain_two_grad: float32 [768], P(('seq', 'batch'))
- offset_two_grad: float32 [768], P(('seq', 'batch'))
- pos_bias_grad: float32 [256], P(('seq', 'batch'))
The draws below stay inside these ranges and needn't reach their ends.
Inputs may be any that keep to these rules, and one draw needn't show every extreme that they name: `prefix_len`: in every draw one row has no unscored positions and one row has exactly 3840 of them.
All inputs are finite; a program needn't handle non-finite values.
Results may differ from the reference program's by a relative error of at most 0.0003.
Values sent between devices are 32-bit elements; how exact they have to be, the bound alone decides.
No kernel may reach another device: no remote copies, remote signals or barrier semaphores. Data moves between devices by JAX's collectives and lax.ppermute only.
A program may use at most 192 MiB of HBM per device.

```python
import jax
import jax.numpy as jnp
from jax import lax

D = 768
FF = 3072
WINDOW = 256
TOK_DEV = 256
ROW_LEN = 4096
ROWS = 8


def draw_prefix_len(key, part):
    key = jax.random.fold_in(key, 11)
    order = jax.random.permutation(jax.random.fold_in(key, 1), ROWS)
    largest = ROW_LEN - TOK_DEV
    values = jax.random.randint(jax.random.fold_in(key, 2), (ROWS,), 0, largest + 1)
    values = jnp.where(order == 0, 0, values)
    values = jnp.where(order == 1, largest, values)
    return values.astype(jnp.int32)


def steps_of(key, shape, cuts, least, high):
    def one(axis_at, parts):
        heights = jax.random.uniform(jax.random.fold_in(jax.random.fold_in(key, 6), axis_at), (parts,), jnp.float32, least / len(cuts), high / len(cuts))
        return jnp.repeat(jnp.exp(heights), shape[axis_at] // parts).reshape((-1,) + (1,) * (len(shape) - axis_at - 1))

    factor_of = one(*cuts[0])
    for cut in cuts[1:]:
        factor_of = factor_of * one(*cut)
    return factor_of


def bell_draw(stream_key, extent, deviation, most, split=(), kind=jnp.bfloat16):
    result = jax.random.normal(stream_key, extent, jnp.float32) * deviation
    if len(split) > 0:
        result = steps_of(stream_key, extent, split, -0.22, 0.18) * result
    return jnp.clip(result, min=-most, max=most).astype(kind)


def setup_inputs(seed: int = 0) -> dict:
    splits = jax.random.split(jax.random.key(seed), 15)
    inputs = bell_draw(splits[0], (ROWS, ROW_LEN, D), 1.0, 6.0, ((0, 8), (1, 16)), jnp.float32)
    query_weight = bell_draw(splits[1], (D, D), D ** -0.5, 0.21875, ((0, 128),), jnp.float32)
    key_weight = bell_draw(splits[2], (D, D), D ** -0.5, 0.21875, ((0, 128),), jnp.float32)
    value_weight = bell_draw(splits[3], (D, D), D ** -0.5, 0.21875, ((0, 128),), jnp.float32)
    out_weight = bell_draw(splits[4], (D, D), (D // 128) ** -0.5, 2.5, ((0, 128),), jnp.float32)
    up_weight = bell_draw(splits[5], (D, FF), D ** -0.5, 0.21875, ((0, 128),), jnp.float32)
    down_weight = bell_draw(splits[6], (FF, D), FF ** -0.5, 0.109375, ((0, 128),), jnp.float32)
    gain_one = jnp.clip(1.0 + 0.18 * jax.random.normal(splits[7], (D,), jnp.float32), 0.1, 1.9)
    offset_one = bell_draw(splits[8], (D,), 0.5, 3.0, ((0, 128),), jnp.float32)
    gain_two = jnp.clip(1.0 + 0.18 * jax.random.normal(splits[9], (D,), jnp.float32), 0.1, 1.9)
    offset_two = bell_draw(splits[10], (D,), 0.5, 3.0, ((0, 128),), jnp.float32)
    pos_bias = bell_draw(splits[11], (WINDOW,), 1.0, 4.0, ((0, 128),), jnp.float32)
    prefix_len = draw_prefix_len(jax.random.fold_in(splits[14], 71), 0)
    cotangent = bell_draw(splits[13], (ROWS, ROW_LEN, D), 1.0, 6.0, ((0, 8), (1, 16)), jnp.float32)
    return dict(inputs=inputs, query_weight=query_weight, key_weight=key_weight, value_weight=value_weight, out_weight=out_weight, up_weight=up_weight, down_weight=down_weight, gain_one=gain_one, offset_one=offset_one, gain_two=gain_two, offset_two=offset_two, pos_bias=pos_bias, prefix_len=prefix_len, cotangent=cotangent)


EPSILON = 1e-05

@jax.custom_vjp
def low(v):
    return lax.optimization_barrier(v.astype(jnp.bfloat16)).astype(jnp.float32)

@jax.custom_vjp
def low_back(v):
    return v

def low_keep(v):
    return (low(v), None)

def low_pass(kept, grad):
    return (grad,)

def back_keep(v):
    return (v, None)

def back_low(kept, grad):
    return (low(grad),)
low.defvjp(low_keep, low_pass)
low_back.defvjp(back_keep, back_low)

def matmul(left, right):
    return jnp.dot(left, right, precision=lax.Precision.HIGHEST, preferred_element_type=jnp.float32)

def layer_norm(values, gain, offset):
    centred = values - lax.optimization_barrier(jnp.mean(values, axis=-1, keepdims=True))
    spread = lax.optimization_barrier(jnp.mean(centred * centred, axis=-1, keepdims=True))
    return centred * lax.rsqrt(spread + EPSILON) * gain + offset

def band_matrix(expbias, row_count):
    span = expbias.shape[0]
    pattern = jnp.concatenate([expbias[::-1], jnp.zeros((row_count,), jnp.float32)])
    repeated = jnp.tile(pattern, row_count)[:row_count * (span + row_count - 1)]
    return repeated.reshape(row_count, span + row_count - 1)

def pre_mix(inputs, gain_one, offset_one, query_weight, key_weight, value_weight):
    normed = layer_norm(inputs, gain_one, offset_one)
    return (matmul(normed, query_weight), matmul(normed, key_weight), matmul(normed, value_weight))

def mix_row(queries, key_part, value_part, pos_bias):
    reach = WINDOW - 1
    padding = jnp.zeros((reach, D), jnp.float32)
    weights_pad = jnp.concatenate([padding, jnp.exp(key_part)], axis=0)
    carried_pad = jnp.concatenate([padding, jnp.exp(key_part) * value_part], axis=0)
    banded = band_matrix(jnp.exp(pos_bias), TOK_DEV)

    def one_block(block_index):
        start = (block_index * TOK_DEV).astype(jnp.int32)
        weights_part = lax.dynamic_slice_in_dim(weights_pad, start, TOK_DEV + reach, 0)
        carried_part = lax.dynamic_slice_in_dim(carried_pad, start, TOK_DEV + reach, 0)
        return (matmul(banded, carried_part), matmul(banded, weights_part))
    numer, denom = lax.map(jax.checkpoint(one_block), jnp.arange(ROW_LEN // TOK_DEV, dtype=jnp.int32))
    numer = numer.reshape(ROW_LEN, D)
    denom = denom.reshape(ROW_LEN, D)
    return jax.nn.sigmoid(queries) * (numer / denom)

def forward(inputs, query_weight, key_weight, value_weight, out_weight, up_weight, down_weight, gain_one, offset_one, gain_two, offset_two, pos_bias):

    def one_row(row_input):
        queries, key_part, value_part = pre_mix(row_input, gain_one, offset_one, query_weight, key_weight, value_weight)
        mixed = mix_row(queries, key_part, value_part, pos_bias)
        middle = row_input + matmul(mixed, out_weight)
        hidden = jax.nn.gelu(matmul(layer_norm(middle, gain_two, offset_two), up_weight), approximate=False)
        return middle + matmul(hidden, down_weight)
    return lax.map(one_row, inputs)

def reference(inputs, query_weight, key_weight, value_weight, out_weight, up_weight, down_weight, gain_one, offset_one, gain_two, offset_two, pos_bias, prefix_len, cotangent):
    positions = jnp.arange(ROW_LEN, dtype=jnp.int32)
    scored = (positions[None, :] >= prefix_len[:, None]).astype(jnp.float32)
    weighted_cot = cotangent * scored[:, :, None]
    output, pull = jax.vjp(forward, inputs, query_weight, key_weight, value_weight, out_weight, up_weight, down_weight, gain_one, offset_one, gain_two, offset_two, pos_bias)
    grads = pull(weighted_cot)
    return (output, grads[0], grads[1], grads[2], grads[3], grads[4], grads[5], grads[6], grads[7], grads[8], grads[9], grads[10], grads[11])
```

```python
import functools

import jax
import jax.numpy as jnp
import numpy as np
from jax import lax
from jax.experimental import pallas as pl
from jax.experimental.pallas import tpu as pltpu
from jax.sharding import Mesh
from jax.sharding import PartitionSpec as P

EPSILON = 1e-05
AXES = ("x", "zh", "core", "y", "zl")
RING = {"x": "x", "y": "y", "z": ("zh", "zl")}
F32, BF16 = jnp.float32, jnp.bfloat16
VMEM_LIMIT = 56 * 1024 * 1024
TOK = 256
NT = (((1,), (1,)), ((), ()))
NN = (((1,), (0,)), ((), ()))
ANY = pl.BlockSpec(memory_space=pl.ANY)
VM = pl.BlockSpec(memory_space=pltpu.VMEM)
SM = pl.BlockSpec(memory_space=pltpu.SMEM)


def shift(array, axis, by):
    return lax.ppermute(array, RING[axis], [(i, (i + by) % 4) for i in range(4)])


def swap_cores(array):
    return lax.ppermute(array, "core", [(0, 1), (1, 0)])


def index_of(x, zh, core, y, zl):
    return (((x * 2 + zh) * 2 + core) * 4 + y) * 2 + zl


def along_row(array, by, from_core, to_core):
    pairs = []
    for chip in range(8):
        if 0 <= chip + by < 8:
            for y in range(4):
                for zl in range(2):
                    for a, b in zip(from_core, to_core):
                        pairs.append(
                            (
                                index_of(chip // 2, chip % 2, a, y, zl),
                                index_of((chip + by) // 2, (chip + by) % 2, b, y, zl),
                            )
                        )
    return lax.ppermute(array, AXES, pairs)


def gather_direct(block, axis):
    return [block] + [shift(block, axis, -k) for k in (1, 2, 3)]


def gather_ring(block, cut, axis):
    after = shift(block, axis, -1)
    before = shift(block, axis, 1)
    return (
        block,
        after,
        before,
        shift(before[:cut], axis, 1),
        shift(after[cut:], axis, -1),
    )


def scatter_direct(parts, axis):
    total = parts[0]
    for k in (1, 2, 3):
        total = total + shift(parts[k], axis, k)
    return total


def scatter_ring(parts, cut, axis):
    own, after, before, far_low, far_high = parts
    low = shift(far_low, axis, 1)
    high = shift(far_high, axis, -1)
    after = jnp.concatenate([after[:cut] + low, after[cut:]], axis=0)
    before = jnp.concatenate([before[:cut], before[cut:] + high], axis=0)
    return own + shift(after, axis, 1) + shift(before, axis, -1)


def split(value):
    high = value.astype(BF16)
    return high, (value - high.astype(F32)).astype(BF16)


def dot3(left, right, dims=NN):
    def one(a, b):
        return lax.dot_general(a, b, dims, preferred_element_type=F32)

    return one(left[0], right[0]) + one(left[0], right[1]) + one(left[1], right[0])


def normal_parts(values):
    centred = values - jnp.mean(values, axis=-1, keepdims=True)
    spread = jnp.mean(centred * centred, axis=-1, keepdims=True)
    scale = lax.rsqrt(spread + EPSILON)
    return centred * scale, scale


def normal_back(grad, xhat, scale, gain):
    e = grad * gain
    return scale * (
        e
        - jnp.mean(e, axis=-1, keepdims=True)
        - xhat * jnp.mean(e * xhat, axis=-1, keepdims=True)
    )


def erf(v):
    v = jnp.clip(v, -4.0, 4.0)
    s = v * v
    top = jnp.float32(-2.72614225801306e-10)
    for c in (
        2.77068142495902e-08,
        -2.10102402082508e-06,
        -5.69250639462346e-05,
        -7.34990630326855e-04,
        -2.95459980854025e-03,
        -1.60960333262415e-02,
    ):
        top = top * s + jnp.float32(c)
    low = jnp.float32(-1.45660718464996e-05)
    for c in (
        -2.13374055278905e-04,
        -1.68282697438203e-03,
        -7.37332916720468e-03,
        -1.42647390514189e-02,
    ):
        low = low * s + jnp.float32(c)
    return v * top / low


def chip_at(x, y, z):
    return (x * 2 + z // 2) * 8 + y * 2 + z % 2


def pieces_map(order, where):
    me = {"x": where[0], "y": where[1], "z": where[2]}
    places = []
    for far in range(4):
        for mid in range(4):
            for near in range(4):
                at = dict(zip(order, (near, mid, far)))
                x, y, z = (lax.rem(me[a] + at[a], 4) for a in "xyz")
                places.append((far, mid * 4 + near, chip_at(x, y, z)))
    return places


def ring_ref(refs, far, block):
    own, after, before, far_low, far_high = refs
    if far == 2:
        return (far_low, block) if block < 8 else (far_high, block - 8)
    return {0: own, 1: after, 3: before}[far], block


def unpack_attn_kernel(
    where, own, after, before, low, high, q_hi, q_lo, kv_hi, kv_lo, o_hi, o_lo, blocks, sems
):
    copies = []
    for i, (far, block, chip) in enumerate(pieces_map(("z", "x", "y"), where)):
        ref, at = ring_ref((own, after, before, low, high), far, block)
        skip = 0 if ref is high else 8
        copies.append(
            pltpu.make_async_copy(ref.at[pl.ds(skip + 48 * at, 48)], blocks.at[chip], sems.at[i])
        )
    for copy in copies:
        copy.start()
    for copy in copies:
        copy.wait()

    def step(group, carry):
        held = [blocks[group * 8 + j] for j in range(8)]

        def rows(first):
            return jnp.concatenate([h[first : first + 6] for h in held], axis=0)

        for c in range(2):
            at = pl.ds(pl.multiple_of(group * 96 + c * 48, 16), 48)
            q_hi[at, :], q_lo[at, :] = split(rows(6 * c))
            kv_hi[at, :384], kv_lo[at, :384] = split(rows(12 + 6 * c))
            kv_hi[at, 384:], kv_lo[at, 384:] = split(rows(24 + 6 * c))
            at = pl.ds(pl.multiple_of(group * 48, 16), 48)
            o_hi[at, pl.ds(384 * c, 384)], o_lo[at, pl.ds(384 * c, 384)] = split(rows(36 + 6 * c))
        return carry

    lax.fori_loop(0, 8, step, 0)


def unpack_up_kernel(where, own, after, before, low, high, up_hi, up_lo, blocks, sems):
    copies = []
    for i, (far, block, chip) in enumerate(pieces_map(("y", "z", "x"), where)):
        ref, at = ring_ref((own, after, before, low, high), far, block)
        copies.append(pltpu.make_async_copy(ref.at[at], blocks.at[chip], sems.at[i]))
    for copy in copies:
        copy.start()
    for copy in copies:
        copy.wait()

    def step(group, carry):
        held = [blocks[group * 8 + j] for j in range(8)]
        for c in range(2):
            at = pl.ds(pl.multiple_of(group * 96 + c * 48, 16), 48)
            for b in range(6):
                first = 12 * b + 6 * c
                rows = jnp.concatenate([h[first : first + 6] for h in held], axis=0)
                lanes = pl.ds(256 * b, 256)
                up_hi[at, lanes], up_lo[at, lanes] = split(rows)
        return carry

    lax.fori_loop(0, 8, step, 0)


def unpack_down_kernel(where, gathered, down_hi, down_lo, rows, sems):
    copies = []
    for i, (far, block, chip) in enumerate(pieces_map(("x", "y", "z"), where)):
        z = lax.rem(where[2] + far, 4)
        at = pl.ds(pl.multiple_of(chip * 24, 8), 24)
        copies.append(pltpu.make_async_copy(gathered.at[z, block], rows.at[at], sems.at[i]))
    for copy in copies:
        copy.start()
    for copy in copies:
        copy.wait()

    def step(i, carry):
        at = pl.ds(pl.multiple_of(i * 192, 16), 192)
        down_hi[at, :], down_lo[at, :] = split(rows[at, :])
        return carry

    lax.fori_loop(0, 8, step, 0)


def toeplitz(base):
    return pltpu.roll(jnp.broadcast_to(base, (TOK, 2 * TOK)), 0, 1, stride=1, stride_axis=0)


def attn_kernel(
    x_ref, vec_ref, base_ref, valid_ref, q_hi, q_lo, kv_hi, kv_lo, o_hi, o_lo,
    part_ref, nt_hi, nt_lo, sig_ref, ratio_ref, inv_ref, w_ref, v_ref,
):
    gain, offset = vec_ref[0:1, :], vec_ref[1:2, :]
    xhat, _ = normal_parts(x_ref[...])
    normed = xhat * gain + offset
    parts = split(normed)
    nt_hi[...], nt_lo[...] = split(normed.T)
    own = tuple(p[TOK:] for p in parts)
    keys = dot3(parts, (kv_hi[...], kv_lo[...]))
    sig_ref[...] = jax.nn.sigmoid(dot3(own, (q_hi[...], q_lo[...])))
    w = jnp.exp(keys[:, :384])
    w_ref[:TOK] = w[:TOK] * valid_ref[0]
    w_ref[TOK:] = w[TOK:]
    v_ref[...] = keys[:, 384:]
    w = w_ref[...]
    sums = split(jnp.concatenate([w * v_ref[...], w], axis=1))
    band = split(toeplitz(base_ref[0:1, :]))
    for i in range(2):
        at = slice(TOK * i, TOK * i + TOK)
        seen = tuple(s[TOK * i : TOK * i + 2 * TOK] for s in sums)
        mixed = dot3(band, seen)
        inverse = 1.0 / mixed[:, 384:]
        inv_ref[at] = inverse
        ratio_ref[at] = mixed[:, :384] * inverse
    mixed = split(sig_ref[...] * ratio_ref[...])
    part_ref[...] = dot3(mixed, (o_hi[...], o_lo[...]))


def ffn_kernel(
    where, x_ref, mine_ref, theirs_ref, cot_ref, vec_ref, up_hi, up_lo, down_hi, down_lo,
    middle_ref, out_ref, back_ref, u_own, u_after, u_before, u_low, u_high, down_grad,
    n_hi, n_lo, nt_hi, nt_lo, g_hi, g_lo, up_blocks, down_rows, up_sems, down_sems,
):
    step = pl.program_id(0)
    up_map = pieces_map(("y", "z", "x"), where)
    down_map = pieces_map(("x", "y", "z"), where)

    @pl.when(step == 0)
    def _():
        middle = x_ref[...] + (mine_ref[...] + theirs_ref[...])
        middle_ref[...] = middle
        xhat, _ = normal_parts(middle)
        normed = xhat * vec_ref[2:3, :] + vec_ref[3:4, :]
        n_hi[...], n_lo[...] = split(normed)
        nt_hi[...], nt_lo[...] = split(normed.T)
        g_hi[...], g_lo[...] = split(cot_ref[...])

    up = (up_hi[...], up_lo[...])
    down = (down_hi[...], down_lo[...])
    cot = (g_hi[...], g_lo[...])
    preact = dot3((n_hi[...], n_lo[...]), up)
    lower = 0.5 + 0.5 * erf(preact * np.float32(np.sqrt(0.5)))
    hidden = preact * lower
    slope = lower + preact * (
        jnp.exp(-0.5 * preact * preact) * np.float32(1.0 / np.sqrt(2.0 * np.pi))
    )
    grad = split(dot3(cot, down, NT) * slope)
    out = dot3(split(hidden), down)
    back = dot3(grad, up, NT)

    @pl.when(step == 0)
    def _():
        out_ref[...] = out
        back_ref[...] = back

    @pl.when(step > 0)
    def _():
        out_ref[...] += out
        back_ref[...] += back

    at = pl.ds(pl.multiple_of(step * 512, 512), 512)
    down_rows[at, :] = dot3(split(hidden.T), cot)
    up_grad = dot3((nt_hi[...], nt_lo[...]), grad)
    rows = pl.ds(pl.multiple_of(step * 24, 8), 24)
    for group in range(8):
        held = up_grad[group * 96 : group * 96 + 96]
        for j in range(8):
            up_blocks[group * 8 + j, rows, :] = jnp.concatenate(
                [
                    held[48 * c + 6 * j : 48 * c + 6 * j + 6, 256 * b : 256 * b + 256]
                    for b in range(2)
                    for c in range(2)
                ],
                axis=0,
            )

    def up_copies():
        copies = []
        for i, (far, block, chip) in enumerate(up_map):
            ref, place = ring_ref((u_own, u_after, u_before, u_low, u_high), far, block)
            copies.append(
                pltpu.make_async_copy(up_blocks.at[chip], ref.at[place], up_sems.at[i])
            )
        return copies

    def down_copies():
        copies = []
        for i, (far, block, chip) in enumerate(down_map):
            z = lax.rem(where[2] + far, 4)
            rows = pl.ds(pl.multiple_of(chip * 24, 8), 24)
            copies.append(
                pltpu.make_async_copy(down_rows.at[rows], down_grad.at[z, block], down_sems.at[i])
            )
        return copies

    @pl.when(step == pl.num_programs(0) - 1)
    def _():
        copies = up_copies() + down_copies()
        for copy in copies:
            copy.start()
        for copy in copies:
            copy.wait()


def attn_back_kernel(
    where, middle_ref, mine_ref, theirs_ref, cot_ref, vec_ref, base_ref, sig_ref, ratio_ref,
    inv_ref, w_ref, v_ref, nt_hi, nt_lo, o_hi, o_lo,
    gmid_ref, gq_ref, gkv_ref, small_ref, bias_ref, b_own, b_after, b_before, b_low, b_high,
    blocks, sems,
):
    xhat, scale = normal_parts(middle_ref[...])
    mine = mine_ref[...]
    small_ref[2:3, :] = jnp.sum(mine * xhat, axis=0, keepdims=True)
    small_ref[3:4, :] = jnp.sum(mine, axis=0, keepdims=True)
    gmid = cot_ref[...] + normal_back(mine + theirs_ref[...], xhat, scale, vec_ref[2:3, :])
    gmid_ref[...] = gmid
    gmid = split(gmid)
    sig, ratio = sig_ref[...], ratio_ref[...]
    out_grad = dot3(split((sig * ratio).T), gmid)
    gmixed = dot3(gmid, (o_hi[...], o_lo[...]), NT)
    gq = gmixed * ratio * sig * (1.0 - sig)
    gq_ref[...] = gq
    gnum = gmixed * sig * inv_ref[...]
    gsums = split(jnp.concatenate([gnum, -gnum * ratio], axis=1))
    band = toeplitz(base_ref[0:1, :])
    band_t = split(band.T)
    w, v = w_ref[...], v_ref[...]
    sums = split(jnp.concatenate([w * v, w], axis=1))
    spread, gband = [], None
    for i in range(2):
        here = tuple(g[TOK * i : TOK * i + TOK] for g in gsums)
        seen = tuple(s[TOK * i : TOK * i + 2 * TOK] for s in sums)
        spread.append(dot3(band_t, here))
        term = dot3(here, seen, NT)
        gband = term if gband is None else gband + term
    count = TOK
    while count > 1:
        count //= 2
        gband = gband[:count] + pltpu.roll(gband[count:], 2 * TOK - count, 1)
    bias_ref[...] = jnp.broadcast_to(gband * base_ref[0:1, :], (8, 2 * TOK))
    gseen = jnp.concatenate(
        [spread[0][:TOK], spread[0][TOK:] + spread[1][:TOK], spread[1][TOK:]], axis=0
    )
    gkv = jnp.concatenate([w * (gseen[:, :384] * v + gseen[:, 384:]), gseen[:, :384] * w], axis=1)
    gkv_ref[...] = gkv
    q_grad = dot3((nt_hi[:, TOK:], nt_lo[:, TOK:]), split(gq))
    kv_grad = dot3((nt_hi[...], nt_lo[...]), split(gkv))
    for group in range(8):
        for j in range(8):

            def both(array, lanes):
                at = [group * 96 + 48 * c + 6 * j for c in range(2)]
                return [array[a : a + 6, lanes] for a in at]

            o_rows = out_grad[group * 48 + 6 * j : group * 48 + 6 * j + 6]
            blocks[group * 8 + j] = jnp.concatenate(
                both(q_grad, slice(None))
                + both(kv_grad, slice(0, 384))
                + both(kv_grad, slice(384, 768))
                + [o_rows[:, :384], o_rows[:, 384:]],
                axis=0,
            )
    copies = []
    for i, (far, block, chip) in enumerate(pieces_map(("z", "x", "y"), where)):
        ref, at = ring_ref((b_own, b_after, b_before, b_low, b_high), far, block)
        copies.append(pltpu.make_async_copy(blocks.at[chip], ref.at[at], sems.at[i]))
    for copy in copies:
        copy.start()
    for copy in copies:
        copy.wait()


def attn_last_kernel(
    x_ref, gq_ref, gkv_ref, q_hi, q_lo, kv_hi, kv_lo, back_ref, small_ref
):
    back_ref[...] = dot3(split(gkv_ref[...]), (kv_hi[...], kv_lo[...]), NT)
    back_ref[TOK:] += dot3(split(gq_ref[...]), (q_hi[...], q_lo[...]), NT)
    xhat, _ = normal_parts(x_ref[...])
    back = back_ref[...]
    small_ref[0:1, :] = jnp.sum(back * xhat, axis=0, keepdims=True)
    small_ref[1:2, :] = jnp.sum(back, axis=0, keepdims=True)


def shaped(*shape, dtype=F32):
    return jax.ShapeDtypeStruct(shape, dtype)


def call(kernel, out_shape, args, specs, scratch=(), flops=0, moved=0, **more):
    return pl.pallas_call(
        kernel,
        out_shape=out_shape,
        in_specs=specs,
        scratch_shapes=list(scratch),
        compiler_params=pltpu.CompilerParams(vmem_limit_bytes=VMEM_LIMIT),
        cost_estimate=pl.CostEstimate(flops=flops, bytes_accessed=moved, transcendentals=0),
        **more,
    )(*args)


def halves(array, run):
    rows, columns = array.shape
    turns = array.reshape(rows, columns // (2 * run), 2, run)
    return tuple(turns[:, :, c].reshape(rows, columns // 2) for c in range(2))


def joined(first, second, run):
    rows, columns = first.shape
    turns = jnp.stack([a.reshape(rows, columns // run, run) for a in (first, second)], axis=2)
    return turns.reshape(rows, 2 * columns)


def ordered(core, mine, theirs, axis=0):
    return lax.cond(
        core == 0,
        lambda a, b: jnp.concatenate([a, b], axis=axis),
        lambda a, b: jnp.concatenate([b, a], axis=axis),
        mine,
        theirs,
    )


def shards(
    inputs, query_weight, key_weight, value_weight, out_weight, up_weight, down_weight,
    gain_one, offset_one, gain_two, offset_two, pos_bias, prefix_len, cotangent,
):
    x, y, core = lax.axis_index("x"), lax.axis_index("y"), lax.axis_index("core")
    zh, zl = lax.axis_index("zh"), lax.axis_index("zl")
    z = zh * 2 + zl
    where = jnp.stack([x, y, z]).astype(jnp.int32)
    first_core = core == 0

    def pick(pair):
        return jnp.where(first_core, pair[0], pair[1]), jnp.where(first_core, pair[1], pair[0])

    with jax.named_scope("pair_weights"):
        vectors = jnp.concatenate([gain_one, offset_one, gain_two, offset_two, pos_bias])
        kept, sent = [], []
        for w in (query_weight, key_weight, value_weight):
            a, b = pick(halves(w, 48))
            kept.append(a)
            sent.append(b)
        a, b = pick(halves(up_weight, 192))
        kept += [a[:, 384 * i : 384 * i + 384] for i in range(4)]
        sent += [b[:, 384 * i : 384 * i + 384] for i in range(4)]
        line = jnp.pad(vectors, (0, 384 * 6 - 26)).reshape(6, 384)
        kept, sent = (jnp.concatenate(a + [line], axis=0) for a in (kept, sent))
        got = swap_cores(sent)
        one, two = jnp.where(first_core, kept, got), jnp.where(first_core, got, kept)
        rows = []
        for m in range(3):
            rows += [one[6 * m : 6 * m + 6], two[6 * m : 6 * m + 6]]
        rows += [out_weight[:, :384], out_weight[:, 384:]]
        line = jnp.concatenate([one[42, :26], two[42, :26]])
        rows.append(jnp.pad(line, (0, 384 * 8 - 52)).reshape(8, 384))
        attn_block = jnp.concatenate(rows, axis=0)
        ups = [
            jnp.concatenate([h[18 + 6 * i : 24 + 6 * i] for i in range(4)], axis=1)
            for h in (one, two)
        ]
        up_block = jnp.concatenate(
            [u[:, 256 * b : 256 * b + 256] for b in range(6) for u in ups], axis=0
        )
        down_block = down_weight

    with jax.named_scope("tokens"):
        tokens = inputs[0]
        seq = (x * 2 + zh) * 2 + core
        positions = seq * TOK + jnp.arange(TOK, dtype=jnp.int32)
        scored = (positions >= prefix_len[0]).astype(F32)
        cot = cotangent[0] * scored[:, None]
        other_tokens = swap_cores(tokens)
        other_cot = swap_cores(cot)
        came = along_row(tokens, 1, (1,), (0,))
        halo = jnp.where(first_core, came, swap_cores(came))
        x_own = ordered(core, tokens, other_tokens)
        cot_own = ordered(core, cot, other_cot)
        x_ext = jnp.concatenate([halo, x_own], axis=0)
        valid = jnp.where(x * 2 + zh > 0, 1.0, 0.0).astype(F32).reshape(1)

    with jax.named_scope("gather"):
        attn = jnp.stack(gather_direct(attn_block, "z"))
        up = jnp.stack(gather_direct(up_block, "y"))
        down = jnp.stack(gather_direct(down_block, "x"))
        attn = jnp.concatenate(gather_direct(attn, "x"), axis=0)
        up = jnp.concatenate(gather_direct(up, "z"), axis=0)
        down = jnp.concatenate(gather_direct(down, "y"), axis=0)
        line = jnp.pad(attn[:, 48, :52].reshape(-1), (0, 8 * 384 - 832)).reshape(8, 384)
        attn = jnp.concatenate([line, attn[:, :48].reshape(768, 384)], axis=0)
        attn = gather_ring(attn, 392, "y")
        up = gather_ring(up, 8, "x")
        down = lax.all_gather(down, RING["z"], axis=0)

    with jax.named_scope("vectors"):
        lines = jnp.stack([attn[0][:8], attn[1][:8], attn[3][:8], attn[2][:8]])
        lines = lines.reshape(4, -1)[:, :832].reshape(64, 52)
        chips = jnp.arange(64, dtype=jnp.int32)
        cx, cz, cy = chips // 16, (chips // 8) % 2 * 2 + chips % 2, chips % 8 // 2
        place = ((cy - y) % 4) * 16 + ((cx - x) % 4) * 4 + (cz - z) % 4
        pick_rows = (place[:, None] == jnp.arange(64, dtype=jnp.int32)).astype(F32)
        lines = jnp.dot(pick_rows, lines, precision=lax.Precision.HIGHEST)
        lines = lines.reshape(8, 8, 2, 26).transpose(0, 2, 1, 3)
        vec = jnp.stack([lines[..., 6 * i : 6 * i + 6].reshape(768) for i in range(4)])
        vec = jnp.pad(vec, ((0, 4), (0, 0)))
        weight = jnp.exp(lines[..., 24:].reshape(256))
        base = jnp.concatenate([jnp.zeros((1,), F32), weight[::-1], jnp.zeros((255,), F32)])
        base = jnp.broadcast_to(base, (8, 512))

    with jax.named_scope("unpack"):
        dma64 = pltpu.SemaphoreType.DMA((64,))
        halves_of = lambda *shape: (shaped(*shape, dtype=BF16),) * 2
        q_w = call(
            unpack_attn_kernel,
            halves_of(768, 384) + halves_of(768, 768) + halves_of(384, 768),
            (where, *attn),
            [SM] + [ANY] * 5,
            (pltpu.VMEM((64, 48, 384), F32), dma64),
            moved=10_000_000,
        )
        q_w, kv_w, o_w = q_w[:2], q_w[2:4], q_w[4:]
        up_w = call(
            unpack_up_kernel,
            halves_of(768, 1536),
            (where, *up),
            [SM] + [ANY] * 5,
            (pltpu.VMEM((64, 72, 256), F32), dma64),
            moved=10_000_000,
        )
        down_w = call(
            unpack_down_kernel,
            halves_of(1536, 768),
            (where, down),
            [SM, ANY],
            (pltpu.VMEM((1536, 768), F32), dma64),
            moved=10_000_000,
        )

    with jax.named_scope("attn"):
        part, nt_hi, nt_lo, sig, ratio, inv, wexp, val = call(
            attn_kernel,
            (shaped(512, 768),)
            + halves_of(768, 768)
            + (shaped(512, 384),) * 3
            + (shaped(768, 384),) * 2,
            (x_ext, vec, base, valid, *q_w, *kv_w, *o_w),
            [VM] * 3 + [SM] + [VM] * 6,
            flops=5_700_000_000,
            moved=20_000_000,
        )
        part_other = swap_cores(part)

    with jax.named_scope("ffn"):
        whole = lambda *shape: pl.BlockSpec(shape, lambda i: (0,) * len(shape))
        once = whole(512, 768)
        (middle, out_part, back_part, *grads) = call(
            ffn_kernel,
            (shaped(512, 768),) * 3
            + (shaped(16, 72, 256),) * 3
            + (shaped(8, 72, 256),) * 2
            + (shaped(4, 16, 24, 768),),
            (where, x_own, part, part_other, cot_own, vec, *up_w, *down_w),
            [SM, once, once, once, once, whole(8, 768)]
            + [pl.BlockSpec((768, 512), lambda i: (0, i))] * 2
            + [pl.BlockSpec((512, 768), lambda i: (i, 0))] * 2,
            [pltpu.VMEM((512, 768), BF16)] * 2
            + [pltpu.VMEM((768, 512), BF16)] * 2
            + [pltpu.VMEM((512, 768), BF16)] * 2
            + [pltpu.VMEM((64, 72, 256), F32), pltpu.VMEM((1536, 768), F32), dma64, dma64],
            flops=21_700_000_000,
            moved=40_000_000,
            grid=(3,),
            out_specs=(once,) * 3 + (ANY,) * 6,
        )
        up_grads, down_grads = grads[:5], grads[5]
        back_other = swap_cores(back_part)

    with jax.named_scope("attn_back"):
        gmid, gq, gkv, small_two, bias, *attn_grads = call(
            attn_back_kernel,
            (shaped(512, 768), shaped(512, 384), shaped(768, 768), shaped(8, 768), shaped(8, 512))
            + (shaped(16, 48, 384),) * 3
            + (shaped(8, 48, 384),) * 2,
            (where, middle, back_part, back_other, cot_own, vec, base, sig, ratio, inv, wexp, val)
            + (nt_hi, nt_lo, *o_w),
            [SM] + [VM] * 15,
            (pltpu.VMEM((64, 48, 384), F32), dma64),
            flops=8_000_000_000,
            moved=30_000_000,
            out_specs=(VM,) * 5 + (ANY,) * 5,
        )
    with jax.named_scope("attn_last"):
        back_one, small_one = call(
            attn_last_kernel,
            (shaped(768, 768), shaped(8, 768)),
            (x_ext, gq, gkv, *q_w, *kv_w),
            [VM] * 7,
            flops=3_600_000_000,
            moved=12_000_000,
        )

    with jax.named_scope("scatter"):
        down = lax.psum_scatter(down_grads, RING["z"], scatter_dimension=0, tiled=True)
        up = scatter_ring(up_grads, 8, "x")
        attn = scatter_ring(attn_grads, 8, "y")
        lines = jnp.concatenate([small_one[:2], small_two[2:4]], axis=0).reshape(4, 8, 2, 8, 6)
        lines = lines.transpose(1, 3, 2, 0, 4).reshape(64, 2, 24)
        bias_line = bias[0, 1:257][::-1].reshape(8, 2, 8, 2).transpose(0, 2, 1, 3)
        lines = jnp.concatenate([lines, bias_line.reshape(64, 2, 2)], axis=2).reshape(64, 52)
        lines = lax.dot_general(
            pick_rows, lines, (((0,), (0,)), ((), ())), precision=lax.Precision.HIGHEST
        ).reshape(4, 16, 52)
        lines = jnp.pad(lines, ((0, 0), (0, 0), (0, 76)))
        lines = scatter_direct([lines[k] for k in range(4)], "y")
        lines = jnp.pad(lines, ((0, 0), (0, 256)))[:, None]
        attn = jnp.concatenate([attn, jnp.pad(lines, ((0, 0), (0, 7), (0, 0)))], axis=1)
        down = down.reshape(4, 4, 24, 768)
        attn = attn.reshape(4, 4, 56, 384)
        up = up.reshape(4, 4, 72, 256)
        for array_axis in range(2):
            down = scatter_direct([down[k] for k in range(4)], ("y", "x")[array_axis])
            up = scatter_direct([up[k] for k in range(4)], ("z", "y")[array_axis])
            attn = scatter_direct([attn[k] for k in range(4)], ("x", "z")[array_axis])

    with jax.named_scope("pair_grads"):
        def of(c):
            rows = [attn[12 * m + 6 * c : 12 * m + 6 * c + 6] for m in range(3)]
            ups = [up[12 * b + 6 * c : 12 * b + 6 * c + 6] for b in range(6)]
            wide = jnp.concatenate(ups, axis=1)
            rows += [wide[:, 384 * i : 384 * i + 384] for i in range(4)]
            line = jnp.pad(attn[48, 26 * c : 26 * c + 26], (0, 384 * 6 - 26)).reshape(6, 384)
            return jnp.concatenate(rows + [line], axis=0)

        mine, theirs = pick((of(0), of(1)))
        got = swap_cores(theirs)
        one, two = jnp.where(first_core, mine, got), jnp.where(first_core, got, mine)
        qkv = [joined(one[6 * m : 6 * m + 6], two[6 * m : 6 * m + 6], 48) for m in range(3)]
        wide = [jnp.concatenate([h[18 + 6 * i : 24 + 6 * i] for i in range(4)], axis=1) for h in (one, two)]
        up_out = joined(wide[0], wide[1], 192)
        line = one[42, :26] + two[42, :26]
        out_out = jnp.concatenate([attn[36:42], attn[42:48]], axis=1)

    with jax.named_scope("token_outputs"):
        start = core * TOK
        other = TOK - start

        def rows_at(array, at, count=TOK):
            return lax.dynamic_slice_in_dim(array, at, count, 0)

        output = (
            rows_at(middle, start)
            + rows_at(out_part, start)
            + swap_cores(rows_at(out_part, other))
        )
        half = TOK // 2
        back_halo = rows_at(back_one, core * half, half) + swap_cores(
            rows_at(back_one, half - core * half, half)
        )
        came = along_row(back_halo, -1, (0, 1), (0, 1))
        came = jnp.concatenate([swap_cores(came), came], axis=0)
        back = rows_at(back_one, TOK + start) + swap_cores(rows_at(back_one, TOK + other))
        back = back + jnp.where(first_core, 0.0, came)
        xhat, scale = normal_parts(tokens)
        input_grad = rows_at(gmid, start) + normal_back(back, xhat, scale, vec[0:1])

    return (
        output[None], input_grad[None], *qkv, out_out, up_out, down,
        line[0:6], line[6:12], line[12:18], line[18:24], line[24:26],
    )


def solution(mesh):
    fine = Mesh(mesh.devices.reshape(4, 2, 2, 4, 2), AXES)
    tokens = P(("y", "zl"), ("x", "zh", "core"), None)
    matrix = P(AXES, None)
    vector = P(AXES)
    return jax.shard_map(
        shards,
        mesh=fine,
        in_specs=(tokens,) + (matrix,) * 6 + (vector,) * 5 + (P(("y", "zl")), tokens),
        out_specs=(tokens, tokens) + (matrix,) * 6 + (vector,) * 5,
        check_vma=False,
    )
```

```python
import functools

import jax
import jax.numpy as jnp
import numpy as np
from jax import lax
from jax.experimental import pallas as pl
from jax.experimental.pallas import tpu as pltpu
from jax.sharding import Mesh
from jax.sharding import PartitionSpec as P

EPSILON = 1e-05
AXES = ("x", "zh", "core", "y", "zl")
RING = {"x": "x", "y": "y", "z": ("zh", "zl")}
F32, BF16 = jnp.float32, jnp.bfloat16
TOK = 256
NT = (((1,), (1,)), ((), ()))
NN = (((1,), (0,)), ((), ()))
ANY = pl.BlockSpec(memory_space=pl.ANY)
HB = pl.BlockSpec(memory_space=pltpu.HBM)
VM = pl.BlockSpec(memory_space=pltpu.VMEM)
SM = pl.BlockSpec(memory_space=pltpu.SMEM)


def shift(array, axis, by):
    return lax.ppermute(array, RING[axis], [(i, (i + by) % 4) for i in range(4)])


def swap_cores(array):
    return lax.ppermute(array, "core", [(0, 1), (1, 0)])


def index_of(x, zh, core, y, zl):
    return (((x * 2 + zh) * 2 + core) * 4 + y) * 2 + zl


def along_row(array, by, from_core, to_core):
    pairs = []
    for chip in range(8):
        if 0 <= chip + by < 8:
            for y in range(4):
                for zl in range(2):
                    for a, b in zip(from_core, to_core):
                        pairs.append(
                            (
                                index_of(chip // 2, chip % 2, a, y, zl),
                                index_of((chip + by) // 2, (chip + by) % 2, b, y, zl),
                            )
                        )
    return lax.ppermute(array, AXES, pairs)


def hop(array, axis, by=1):
    pairs = []
    for at in np.ndindex(4, 4, 2, 4):
        to = dict(zip("xzcy", at))
        to[axis] = (to[axis] + by * (1 - 2 * to["c"])) % 4
        pairs.append(
            tuple(index_of(p[0], p[1] // 2, p[2], p[3], p[1] % 2) for p in (at, tuple(to.values())))
        )
    return lax.ppermute(array, AXES, pairs)


FROM = (0, 3, 1, 2)


def both_ways(block, axis):
    return hop(block, axis), hop(block, axis, -1)


def scatter_start(parts, axis):
    return hop(parts[2], axis), hop(parts[3], axis, -1)


def add_kernel(where, a0, a1, b0, b1, a_sum, b_sum):
    a_sum[...] = a0[...] + a1[...]
    b_sum[...] = b0[...] + b1[...]


def scatter_end(where, one, two, came, axes, parts=None):
    shapes = (one[1].shape, two[1].shape)
    parts = parts or far
    args = (where, parts(one[1]), near(came[0][0]), parts(two[1]), near(came[1][0]))
    sums = glue(add_kernel, shapes, args, given=lambda array: array)
    return [(c[1], hop(a, axis)) for c, a, axis in zip(came, sums, axes)]


def gather_at_once(block, axis):
    return [block] + [shift(block, axis, -k) for k in (1, 2, 3)]


def scatter_at_once(parts, axis):
    return [parts[0]] + [shift(parts[k], axis, k) for k in (1, 2, 3)]


def split(value):
    high = value.astype(BF16)
    return high, (value - high.astype(F32)).astype(BF16)


def dot3(left, right, dims=NN):
    def one(a, b):
        return lax.dot_general(a, b, dims, preferred_element_type=F32)

    return one(left[0], right[0]) + one(left[0], right[1]) + one(left[1], right[0])


def normal_parts(values):
    centred = values - jnp.mean(values, axis=-1, keepdims=True)
    spread = jnp.mean(centred * centred, axis=-1, keepdims=True)
    scale = lax.rsqrt(spread + EPSILON)
    return centred * scale, scale


def normal_back(grad, xhat, scale, gain):
    e = grad * gain
    return scale * (
        e
        - jnp.mean(e, axis=-1, keepdims=True)
        - xhat * jnp.mean(e * xhat, axis=-1, keepdims=True)
    )


def normal_cdf(v):
    density = jnp.exp(-0.5 * v * v)
    d = 1.0 + np.float32(0.3275911 * np.sqrt(0.5)) * jnp.abs(v)
    t = pl.reciprocal(d, approx=True)
    t = t * (2.0 - d * t)
    t = t * (2.0 - d * t)
    total = np.float32(0.5 * 1.061405429)
    for c in (-1.453152027, 1.421413741, -0.284496736, 0.254829592):
        total = total * t + np.float32(0.5 * c)
    total = total * t * density
    return jnp.where(v < 0.0, total, 1.0 - total), density * np.float32(1.0 / np.sqrt(2.0 * np.pi))


HALF_ONE, HALF_TWO = 56, 48


def halved(array, c, run):
    count = array.shape[1] // (2 * run)
    return jnp.concatenate(
        [array[:, (2 * i + c) * run : (2 * i + c + 1) * run] for i in range(count)], axis=1
    )


def joined(first, second, run):
    count = first.shape[1] // run
    return jnp.concatenate(
        [h[:, i * run : (i + 1) * run] for i in range(count) for h in (first, second)], axis=1
    )


def pack_one_kernel(where, q, k, v, up, vec, kept, sent):
    both = []
    for c in range(2):
        wide = halved(up[...], c, 192)
        both.append(
            jnp.concatenate(
                [halved(w[...], c, 48) for w in (q, k, v)]
                + [wide[:, 384 * i : 384 * i + 384] for i in range(4)]
                + [jnp.concatenate([vec[0:6], jnp.zeros((6, 256), F32)], axis=1)],
                axis=0,
            )
        )
    first = where[3] == 0
    kept[...] = jnp.where(first, both[0], both[1])
    sent[...] = jnp.where(first, both[1], both[0])


def pack_two_kernel(where, kept, got, out, block):
    first = where[3] == 0
    one = jnp.where(first, kept[...], got[...])
    two = jnp.where(first, got[...], kept[...])

    def rows(i):
        return [one[6 * i : 6 * i + 6], two[6 * i : 6 * i + 6]]

    line = one[42:43, :128] + pltpu.roll(two[42:43, :128], 64, 1)
    block[0:24] = jnp.concatenate(rows(0) + rows(1), axis=0)
    block[24:32] = jnp.concatenate([jnp.broadcast_to(line, (8, 128)), jnp.zeros((8, 256), F32)], axis=1)
    block[32:56] = jnp.concatenate(rows(3) + rows(4), axis=0)
    block[56:80] = jnp.concatenate(rows(2) + [out[:, :384], out[:, 384:]], axis=0)
    block[80:104] = jnp.concatenate(rows(5) + rows(6), axis=0)


def stack_one_kernel(where, p0, p1, p2, p3, one, two):
    for off, ref in enumerate((p0, p1, p2, p3)):
        at = lax.rem(where[2] + off, 4)
        one[at] = ref[:HALF_ONE]
        two[at] = ref[HALF_ONE:]


def at_hops(where, axis, hops):
    return lax.rem(where[axis] + 4 + hops * (1 - 2 * where[3]), 4)


def stack_down_kernel(where, p0, p1, p2, p3, out):
    for off, ref in enumerate((p0, p1, p2, p3)):
        out[lax.rem(where[0] + off, 4)] = ref[...]


def stack_two_kernel(axis, where, p0, p1, p2, p3, attn, up):
    skip = 8 if axis == 0 else 0
    row = lax.broadcasted_iota(jnp.int32, (8, 128), 0)
    vec = [jnp.zeros((8, 128), F32)] * 3
    for hops, ref in zip(FROM, (p0, p1, p2, p3)):
        at = at_hops(where, axis, hops)
        for z in range(4):
            rows = pl.ds(pl.multiple_of(at * 96 + 24 * z, 8), 24)
            attn[rows] = ref[z, 0:24]
            up[rows] = ref[z, 24 + skip : 48 + skip]
            if skip:
                line = ref[z, 24:32, :128]
                vec[z % 2] = jnp.where(row == at * 2 + z // 2, line, vec[z % 2])
    if skip:
        attn[384:392] = jnp.concatenate(vec, axis=1)


def feature_places():
    x, zh, c, y, zl, r = np.indices((4, 2, 2, 4, 2, 6)).reshape(6, -1)
    return [a.astype(np.int32) for a in (y, zl * 8 + x * 2 + zh, x * 4 + zh * 2 + zl, c * 64 + r)]


def offset_places():
    x, zh, c, y, zl, r = np.indices((4, 2, 2, 4, 2, 2)).reshape(6, -1)
    places = []
    for a in (y, zl * 8 + x * 2 + zh, x * 4 + zh * 2 + zl, c * 64 + 24 + r):
        line = np.full((512,), -1000, np.int32)
        line[1:257] = a[::-1]
        places.append(line)
    return places


def place_tables():
    rows = [np.pad(np.stack(t), ((0, 4), (0, 0))) for t in (feature_places(), offset_places())]
    return rows + [np.ascontiguousarray(np.pad(r.T, ((0, 0), (0, 120)))) for r in rows]


def three_parts(value):
    high, rest = split(value)
    rest = value - high.astype(F32)
    return (high, *split(rest))


def pick_dot(left, right):
    return sum(jnp.dot(a, b, preferred_element_type=F32) for a in left for b in right)


def vectors_kernel(where, p0, p1, p2, p3, features, offsets, vec, base):
    lines = []
    for ref in (p0, p2, p3, p1):
        last = ref[384:392, :256]
        lines += [last[:, :128], last[:, 128:]]
    lines = three_parts(jnp.concatenate(lines, axis=0).T)

    def spread(table):
        hops = jnp.bitwise_and((table[0:1, :] + 4 - where[1]) * (1 - 2 * where[3]), 3)
        place = hops * 16 + table[1:2, :]
        chips = lax.broadcasted_iota(jnp.int32, (64, table.shape[1]), 0) == place
        return pick_dot(lines, (chips.astype(F32).astype(BF16),))

    table = features[...]
    values = spread(table)
    lane = lax.broadcasted_iota(jnp.int32, values.shape, 0)
    picked = [
        jnp.sum(jnp.where(lane == table[3:4, :] + 6 * i, values, 0.0), axis=0, keepdims=True)
        for i in range(4)
    ]
    vec[...] = jnp.concatenate(picked + [jnp.zeros((4, 768), F32)], axis=0)
    table = offsets[...]
    values = spread(table)
    lane = lax.broadcasted_iota(jnp.int32, values.shape, 0)
    picked = jnp.sum(jnp.where(lane == table[3:4, :], values, 0.0), axis=0, keepdims=True)
    base[...] = jnp.broadcast_to(jnp.where(table[3:4, :] >= 0, jnp.exp(picked), 0.0), (8, 512))


def place_lines(where, smalls, bias, features, offsets, feature_columns, offset_columns):
    def gathered(values, table, columns, lane):
        hops = jnp.bitwise_and((table[0:1, :] + 4 - where[1]) * (1 - 2 * where[3]), 3)
        place = hops * 16 + table[1:2, :]
        chips = lax.broadcasted_iota(jnp.int32, (64, table.shape[1]), 0) == place
        lanes = lax.broadcasted_iota(jnp.int32, (table.shape[1], 128), 1) == columns[:, 3:4] + lane
        return pick_dot(
            three_parts(jnp.where(chips, values, 0.0)), (lanes.astype(F32).astype(BF16),)
        )

    total = gathered(bias, offsets[...], offset_columns[...], 0)
    for i, small in enumerate(smalls):
        total += gathered(small, features[...], feature_columns[...], 6 * i)
    return total


def ring_copies(where, axis, places, parts, whole, sems):
    return [
        (p.at[pl.ds(0, whole.shape[1])], whole.at[at_hops(where, axis, hops)], sems.at[i])
        for i, (hops, p) in enumerate(zip(places, parts))
    ]


def bring(where, ones, twos, one, two, sems):
    copies = ring_copies(where, 1, FROM, ones, one, sems.at[0])
    copies += ring_copies(where, 0, FROM, twos, two, sems.at[1])
    copies = [pltpu.make_async_copy(*c) for c in copies]
    for copy in copies:
        copy.start()
    for copy in copies:
        copy.wait()


def send(where, axis, parts, whole, sems):
    copies = ring_copies(where, axis, range(4), parts, whole, sems)
    copies = [pltpu.make_async_copy(place, part, sem) for part, place, sem in copies]
    for copy in copies:
        copy.start()
    return copies


def by_group(one, two, group):
    x, zh = group // 2, lax.rem(group, 2)
    held = ([], [])
    for y in range(4):
        for zl in range(2):
            z = zh * 2 + zl
            held[0].append(one[y, pl.ds(pl.multiple_of((x * 4 + z) * 24, 8), 24)])
            held[1].append(two[x, pl.ds(pl.multiple_of((y * 4 + z) * 24, 8), 24)])
    return held


def unpack_attn(one, two, q_hi, q_lo, kv_hi, kv_lo, o_hi, o_lo):
    def step(group, carry):
        held = by_group(one, two, group)

        def rows(part, first):
            return jnp.concatenate([h[first : first + 6] for h in held[part]], axis=0)

        for c in range(2):
            at = pl.ds(pl.multiple_of(group * 96 + c * 48, 16), 48)
            q_hi[at, :], q_lo[at, :] = split(rows(0, 6 * c))
            kv_hi[at, :384], kv_lo[at, :384] = split(rows(0, 12 + 6 * c))
            kv_hi[at, 384:], kv_lo[at, 384:] = split(rows(1, 6 * c))
            at = pl.ds(pl.multiple_of(group * 48, 16), 48)
            lanes = pl.ds(384 * c, 384)
            o_hi[at, lanes], o_lo[at, lanes] = split(rows(1, 12 + 6 * c))
        return carry

    lax.fori_loop(0, 8, step, 0)


def unpack_up(one, two, up_hi, up_lo):
    def step(group, carry):
        held = by_group(one, two, group)
        for c in range(2):
            at = pl.ds(pl.multiple_of(group * 96 + c * 48, 16), 48)
            for part in range(2):
                for b in range(2):
                    first = 12 * b + 6 * c
                    rows = jnp.concatenate([h[first : first + 6] for h in held[part]], axis=0)
                    lanes = pl.ds(768 * part + 384 * b, 384)
                    up_hi[at, lanes], up_lo[at, lanes] = split(rows)
        return carry

    lax.fori_loop(0, 8, step, 0)


def place_in_blocks(one, two, first, second):
    for group in range(8):
        x, zh = group // 2, group % 2
        for y in range(4):
            for zl in range(2):
                z, j = zh * 2 + zl, y * 2 + zl

                def rows(array):
                    at = [group * 96 + 48 * c + 6 * j for c in range(2)]
                    return [array[a : a + 6] for a in at]

                if first is not None:
                    one[y, (x * 4 + z) * 24 : (x * 4 + z) * 24 + 24] = jnp.concatenate(
                        rows(first[0]) + rows(first[1]), axis=0
                    )
                if second is not None:
                    ends = second[1]
                    if ends.shape[0] == 768:
                        ends = rows(ends)
                    else:
                        ends = ends[group * 48 + 6 * j : group * 48 + 6 * j + 6]
                        ends = [ends[:, :384], ends[:, 384:]]
                    two[x, (y * 4 + z) * 24 : (y * 4 + z) * 24 + 24] = jnp.concatenate(
                        rows(second[0]) + ends, axis=0
                    )


def part_one_kernel(axis, where, a0, a1, a2, b0, b1, b2, *more):
    skip = 8 if axis == 0 else 0
    if skip:
        lines = a0[384:392, :256] + a1[384:392, :256] + a2[384:392, :256]
        row = lax.broadcasted_iota(jnp.int32, (8, 128), 0)
    for hops, out in enumerate(more[-4:]):
        at = at_hops(where, axis, hops)
        for z in range(4):
            rows = pl.ds(pl.multiple_of(at * 96 + 24 * z, 8), 24)
            out[z, 0:24] = a0[rows] + a1[rows] + a2[rows]
            if skip:
                line = lines[:, 128 * (z % 2) : 128 * (z % 2) + 128]
                line = jnp.sum(jnp.where(row == at * 2 + z // 2, line, 0.0), axis=0, keepdims=True)
                out[z, 24:32] = jnp.concatenate(
                    [jnp.broadcast_to(line, (8, 128)), jnp.zeros((8, 256), F32)], axis=1
                )
            out[z, 24 + skip : 48 + skip] = b0[rows] + b1[rows] + b2[rows]


def part_down_kernel(axis, where, down, *outs):
    for hops, out in enumerate(outs):
        out[...] = down[at_hops(where, axis, hops)]


def sum_down_kernel(axis, where, a0, a1, a2, *outs):
    for hops, out in enumerate(outs):
        at = at_hops(where, axis, hops)
        out[...] = a0[at] + a1[at] + a2[at]


def add_one_kernel(where, a0, a1, total):
    total[...] = a0[...] + a1[...]


def part_two_kernel(where, a0, a1, a2, b0, b1, b2, o0, o1, o2, o3):
    for k, out in enumerate((o0, o1, o2, o3)):
        z = lax.rem(where[2] + k, 4)
        out[:HALF_ONE] = a0[z] + a1[z] + a2[z]
        out[HALF_ONE:] = b0[z] + b1[z] + b2[z]


def sum_three_kernel(where, a0, a1, a2, a3, out, kept, sent):
    block = (a0[...] + a1[...]) + (a2[...] + a3[...])
    out[...] = jnp.concatenate([block[68:74], block[74:80]], axis=1)
    line = block[24:25, :128]
    both = []
    for c in range(2):
        rows = [block[at + 6 * c : at + 6 * c + 6] for at in (0, 12, 56, 32, 44, 80, 92)]
        vec = line if c == 0 else pltpu.roll(line, 64, 1)
        vec = jnp.concatenate([jnp.broadcast_to(vec, (6, 128)), jnp.zeros((6, 256), F32)], axis=1)
        both.append(jnp.concatenate(rows + [vec], axis=0))
    first = where[3] == 0
    kept[...] = jnp.where(first, both[0], both[1])
    sent[...] = jnp.where(first, both[1], both[0])


def finish_kernel(where, kept, got, q, k, v, up, vec):
    first = where[3] == 0
    one = jnp.where(first, kept[...], got[...])
    two = jnp.where(first, got[...], kept[...])
    for i, ref in enumerate((q, k, v)):
        ref[...] = joined(one[6 * i : 6 * i + 6], two[6 * i : 6 * i + 6], 48)
    wide = [
        jnp.concatenate([h[18 + 6 * i : 24 + 6 * i] for i in range(4)], axis=1) for h in (one, two)
    ]
    up[...] = joined(wide[0], wide[1], 192)
    vec[...] = jnp.broadcast_to(one[42:43, :128] + two[42:43, :128], (8, 128))


def toeplitz(base):
    return pltpu.roll(jnp.broadcast_to(base, (TOK, 2 * TOK)), 0, 1, stride=1, stride_axis=0)


def fetch_pair(where, mine, other, held, first, sems):
    core = where[3]
    return fetch(
        (mine, other),
        [held.at[pl.ds(pl.multiple_of(first + c * TOK, TOK), TOK)] for c in (core, 1 - core)],
        sems,
    )


def fetch(refs, held, sems):
    copies = [pltpu.make_async_copy(r, h, sems.at[i]) for i, (r, h) in enumerate(zip(refs, held))]
    for copy in copies:
        copy.start()
    return copies


def wait(copies):
    for copy in copies:
        copy.wait()


ATTN_HELD = (
    (((768, 384), BF16),) * 2
    + (((768, 768), BF16),) * 2
    + (((384, 768), BF16),) * 2
    + (((768, 768), BF16),) * 2
    + (((512, 384), F32),) * 3
    + (((768, 384), F32),) * 2
)


def attn_kernel(
    where, halo, tokens, others, vec_ref, base_ref, valid_ref, a0, a1, a2, a3, b0, b1, b2, b3,
    part_ref, *more,
):
    outs, held = more[:13], more[13:26]
    x_ref, one, two, sems, in_sems, out_sems = more[26:]
    q_hi, q_lo, kv_hi, kv_lo, o_hi, o_lo, xt_hi, xt_lo, sig_ref, ratio_ref, inv_ref, w_ref, v_ref = held

    def keep(first, count):
        at = slice(first, first + count)
        return fetch(held[at], outs[at], out_sems.at[pl.ds(first, count)])

    fetched = fetch((halo,), (x_ref.at[pl.ds(0, TOK)],), in_sems)
    fetched += fetch_pair(where, tokens, others, x_ref, TOK, in_sems.at[pl.ds(1, 2)])
    bring(where, (a0, a1, a2, a3), (b0, b1, b2, b3), one, two, sems)
    unpack_attn(one, two, q_hi, q_lo, kv_hi, kv_lo, o_hi, o_lo)
    kept = keep(0, 6)
    gain, offset = vec_ref[0:1, :], vec_ref[1:2, :]
    wait(fetched)
    xhat, _ = normal_parts(x_ref[...])
    normed = xhat * gain + offset
    parts = split(normed)
    xt_hi[...], xt_lo[...] = split(xhat.T)
    kept += keep(6, 2)
    own = tuple(p[TOK:] for p in parts)
    keys = dot3(parts, (kv_hi[...], kv_lo[...]))
    sig_ref[...] = jax.nn.sigmoid(dot3(own, (q_hi[...], q_lo[...])))
    w = jnp.exp(keys[:, :384])
    w_ref[:TOK] = w[:TOK] * valid_ref[0]
    w_ref[TOK:] = w[TOK:]
    v_ref[...] = keys[:, 384:]
    kept += keep(8, 1) + keep(11, 2)
    w = w_ref[...]
    sums = split(jnp.concatenate([w * v_ref[...], w], axis=1))
    band = split(toeplitz(base_ref[0:1, :]))
    for i in range(2):
        at = slice(TOK * i, TOK * i + TOK)
        seen = tuple(s[TOK * i : TOK * i + 2 * TOK] for s in sums)
        mixed = dot3(band, seen)
        inverse = 1.0 / mixed[:, 384:]
        inv_ref[at] = inverse
        ratio_ref[at] = mixed[:, :384] * inverse
    kept += keep(9, 2)
    mixed = split(sig_ref[...] * ratio_ref[...])
    part_ref[...] = dot3(mixed, (o_hi[...], o_lo[...]))
    wait(kept)


def ffn_early_kernel(
    where, down_far, mine, other, down_hi_far, down_lo_far, gh_ref,
    down, down_hi, down_lo, cot_ref, cot_sems, in_sems, out_sems,
):
    kept = fetch([down_far.at[z] for z in range(4)], [down.at[z] for z in range(4)], in_sems)
    fetched = fetch_pair(where, mine, other, cot_ref, 0, cot_sems)
    sent = []
    for zh in range(2):
        wait(kept[2 * zh : 2 * zh + 2])
        for x in range(4):
            for y in range(4):
                rows = jnp.concatenate([down[2 * zh + zl, y, x] for zl in range(2)], axis=0)
                at = pl.ds(((x * 2 + zh) * 4 + y) * 48, 48)
                down_hi[at, :], down_lo[at, :] = split(rows)
    sent += fetch((down_hi, down_lo), (down_hi_far, down_lo_far), out_sems)
    wait(fetched)
    cot = split(cot_ref[...])
    for i in range(2):
        at = slice(768 * i, 768 * i + 768)
        gh_ref[:, at] = dot3(cot, (down_hi[at], down_lo[at]), NT)
    wait(sent)


def ffn_kernel(
    where, tokens, others, mine_far, theirs_far, vec_ref, gh_ref, a0, a1, a2, a3, b0, b1, b2, b3,
    middle_far, nt_hi, nt_lo, h_hi, h_lo, g_hi, g_lo, back_ref,
    x_ref, mine_ref, theirs_ref, middle_ref, one, two, up_hi, up_lo, sems, in_sems, out_sems,
):
    fetched = fetch((mine_far, theirs_far), (mine_ref, theirs_ref), in_sems)
    fetched += fetch_pair(where, tokens, others, x_ref, 0, in_sems.at[pl.ds(2, 2)])
    bring(where, (a0, a1, a2, a3), (b0, b1, b2, b3), one, two, sems)
    unpack_up(one, two, up_hi, up_lo)
    wait(fetched)
    middle_ref[...] = x_ref[...] + (mine_ref[...] + theirs_ref[...])
    sent = fetch((middle_ref,), (middle_far,), out_sems)
    xhat, _ = normal_parts(middle_ref[...])
    normed = xhat * vec_ref[2:3, :] + vec_ref[3:4, :]
    parts = split(normed)
    nt_hi[...], nt_lo[...] = split(normed.T)
    for i in range(6):
        at = slice(256 * i, 256 * i + 256)
        up = (up_hi[:, at], up_lo[:, at])
        preact = dot3(parts, up)
        lower, density = normal_cdf(preact)
        slope = lower + preact * density
        h_hi[:, at], h_lo[:, at] = split(preact * lower)
        grad = split(gh_ref[:, at] * slope)
        g_hi[:, at], g_lo[:, at] = grad
        back = dot3(grad, up, NT)
        if i == 0:
            back_ref[...] = back
        else:
            back_ref[...] += back
    wait(sent)


def ffn_late_kernel(
    where, cot_mine, cot_other, nt_hi, nt_lo, h_hi, h_lo, g_hi, g_lo,
    down_grad_far, a0, a1, a2, a3, b0, b1, b2, b3, one, two, sems, cot_ref, down_grad,
    in_sems, out_sems,
):
    fetched = fetch_pair(where, cot_mine, cot_other, cot_ref, 0, in_sems)
    nt = (nt_hi[...], nt_lo[...])
    sent = []
    for i in range(2):
        at = slice(768 * i, 768 * i + 768)
        grad = dot3(nt, (g_hi[:, at], g_lo[:, at]))
        pair = (grad[:, :384], grad[:, 384:])
        place_in_blocks(one, two, *((pair, None) if i == 0 else (None, pair)))
        sent += send(where, 1 - i, ((a0, a1, a2, a3), (b0, b1, b2, b3))[i], (one, two)[i], sems.at[i])
        if i == 0:
            wait(fetched)
            cot = split(cot_ref[...])
        rows = dot3((h_hi[:, at].T, h_lo[:, at].T), cot)
        for chip in range(32):
            x, zh, y, zl = (2 * i + chip // 16), chip // 8 % 2, chip // 2 % 4, chip % 2
            down_grad[2 * zh + zl, y, x] = rows[chip * 24 : chip * 24 + 24]
        for z in range(4):
            for y in range(4):
                part = (z, y, pl.ds(2 * i, 2))
                sem = out_sems.at[i * 16 + z * 4 + y]
                sent.append(pltpu.make_async_copy(down_grad.at[part], down_grad_far.at[part], sem))
                sent[-1].start()
    wait(sent)


def out_kernel(f0, f1, f2, f3, out_ref, h_hi, h_lo, down_hi, down_lo, sems):
    wait(fetch((f0, f1, f2, f3), (h_hi, h_lo, down_hi, down_lo), sems))
    for i in range(2):
        at = slice(768 * i, 768 * i + 768)
        out = dot3((h_hi[:, at], h_lo[:, at]), (down_hi[at], down_lo[at]))
        if i == 0:
            out_ref[...] = out
        else:
            out_ref[...] += out


def attn_back_kernel(
    where, vec_ref, base_ref, middle_far, mine_far, theirs_far, cot_mine, cot_other,
    f0, f1, f2, f3, f4, f5, f6, gmid_far, gq_ref, gkv_ref, out_grad, small_ref, bias_ref,
    middle_ref, mine_ref, theirs_ref, cot_ref, gmid_ref,
    o_hi, o_lo, sig_ref, ratio_ref, inv_ref, w_ref, v_ref, sems, out_sems,
):
    copies = fetch(
        (middle_far, mine_far, theirs_far), (middle_ref, mine_ref, theirs_ref), sems
    )
    copies += fetch_pair(where, cot_mine, cot_other, cot_ref, 0, sems.at[pl.ds(3, 2)])
    kept = fetch(
        (f0, f1, f2, f3, f4, f5, f6),
        (o_hi, o_lo, sig_ref, ratio_ref, inv_ref, w_ref, v_ref),
        sems.at[pl.ds(5, 7)],
    )
    wait(copies)
    xhat, scale = normal_parts(middle_ref[...])
    mine = mine_ref[...]
    small_ref[2:3, :] = jnp.sum(mine * xhat, axis=0, keepdims=True)
    small_ref[3:4, :] = jnp.sum(mine, axis=0, keepdims=True)
    gmid = cot_ref[...] + normal_back(mine + theirs_ref[...], xhat, scale, vec_ref[2:3, :])
    gmid_ref[...] = gmid
    gmid = split(gmid)
    sent = fetch((gmid_ref,), (gmid_far,), out_sems)
    wait(kept)
    sig, ratio = sig_ref[...], ratio_ref[...]
    out_grad[...] = dot3(split((sig * ratio).T), gmid)
    gmixed = dot3(gmid, (o_hi[...], o_lo[...]), NT)
    gq = gmixed * ratio * sig * (1.0 - sig)
    gq_ref[...] = gq
    gnum = gmixed * sig * inv_ref[...]
    gsums = split(jnp.concatenate([gnum, -gnum * ratio], axis=1))
    band = toeplitz(base_ref[0:1, :])
    band_t = split(band.T)
    w, v = w_ref[...], v_ref[...]
    sums = split(jnp.concatenate([w * v, w], axis=1))
    spread, gband = [], None
    for i in range(2):
        here = tuple(g[TOK * i : TOK * i + TOK] for g in gsums)
        seen = tuple(s[TOK * i : TOK * i + 2 * TOK] for s in sums)
        spread.append(dot3(band_t, here))
        term = dot3(here, seen, NT)
        gband = term if gband is None else gband + term
    count = TOK
    while count > 1:
        count //= 2
        gband = gband[:count] + pltpu.roll(gband[count:], 2 * TOK - count, 1)
    bias_ref[...] = jnp.broadcast_to(gband * base_ref[0:1, :], (8, 2 * TOK))
    gseen = jnp.concatenate(
        [spread[0][:TOK], spread[0][TOK:] + spread[1][:TOK], spread[1][TOK:]], axis=0
    )
    gkv = jnp.concatenate([w * (gseen[:, :384] * v + gseen[:, 384:]), gseen[:, :384] * w], axis=1)
    gkv_ref[...] = gkv
    wait(sent)


def attn_grads_kernel(
    where, vec_ref, gq_ref, gkv_ref, out_grad, small_two, bias, features, offsets, feature_columns,
    offset_columns, f0, f1, f2, f3, f4, f5, a0, a1, a2, a3, b0, b1, b2, b3,
    one, two, sems, q_hi, q_lo, kv_hi, kv_lo, xt_hi, xt_lo, in_sems,
):
    kept = fetch((f4, f5, f0, f1, f2, f3), (xt_hi, xt_lo, q_hi, q_lo, kv_hi, kv_lo), in_sems)
    gq, gkv = gq_ref[...], gkv_ref[...]
    vec = vec_ref[...].T
    wait(kept[:2])
    kv_dot = dot3((xt_hi[...], xt_lo[...]), split(gkv))
    q_dot = dot3((xt_hi[:, TOK:], xt_lo[:, TOK:]), split(gq))
    wait(kept[2:])
    grads, small = [], [0.0, 0.0]
    for dots, g, high, low in ((q_dot, gq, q_hi, q_lo), (kv_dot, gkv, kv_hi, kv_lo)):
        total = jnp.sum(g, axis=0, keepdims=True)
        weight = high[...].astype(F32) + low[...].astype(F32)
        small[0] += jnp.sum(dots * weight, axis=1, keepdims=True)
        small[1] += jnp.sum(total * weight, axis=1, keepdims=True)
        grads.append(vec[:, 0:1] * dots + vec[:, 1:2] * total)
    place_in_blocks(one, two, (grads[0], grads[1][:, :384]), (grads[1][:, 384:], out_grad[...]))
    sent = send(where, 0, (b0, b1, b2, b3), two, sems.at[1])
    small = jnp.concatenate(small + [jnp.zeros((768, 126), F32)], axis=1).T
    smalls = (small[0:1], small[1:2], small_two[2:3, :], small_two[3:4, :])
    lines = place_lines(
        where, smalls, bias[0:1, :], features, offsets, feature_columns, offset_columns
    )
    for k in range(4):
        line = lines[16 * k : 16 * k + 16]
        one[at_hops(where, 1, k), 384:392] = jnp.concatenate(
            [line[:8], line[8:], jnp.zeros((8, 128), F32)], axis=1
        )
    wait(sent + send(where, 1, (a0, a1, a2, a3), one, sems.at[0]))


def attn_last_kernel(gq_ref, gkv_ref, f0, f1, f2, f3, back_ref, q_hi, q_lo, kv_hi, kv_lo, sems):
    kept = fetch((f2, f3, f0, f1), (kv_hi, kv_lo, q_hi, q_lo), sems)
    gq, gkv = split(gq_ref[...]), split(gkv_ref[...])
    wait(kept)
    back_ref[...] = dot3(gkv, (kv_hi[...], kv_lo[...]), NT)
    back_ref[TOK:] += dot3(gq, (q_hi[...], q_lo[...]), NT)


def shaped(*shape, dtype=F32):
    return jax.ShapeDtypeStruct(shape, dtype)


def kept_near(*shape, dtype=F32):
    return pltpu.VMEM(shape, dtype)


def kept_far(*shape, dtype=F32):
    return pltpu.HBM(shape, dtype)


def near(array):
    return pltpu.with_memory_space_constraint(array, pltpu.VMEM)


def far(array):
    return pltpu.with_memory_space_constraint(array, pltpu.HBM)


def call(kernel, out_shape, args, specs, scratch=(), flops=0, moved=0, vmem=24, **more):
    return pl.pallas_call(
        kernel,
        out_shape=out_shape,
        in_specs=specs,
        scratch_shapes=list(scratch),
        compiler_params=pltpu.CompilerParams(vmem_limit_bytes=vmem * 1024 * 1024),
        cost_estimate=pl.CostEstimate(flops=flops, bytes_accessed=moved, transcendentals=0),
        **more,
    )(*args)


def glue(kernel, shapes, args, axis=None, given=near, gives=kept_near):
    if axis is not None:
        kernel = functools.partial(kernel, axis)
    return call(
        kernel,
        tuple(gives(*shape) for shape in shapes),
        (args[0], *map(given, args[1:])),
        [SM] + [VM] * (len(args) - 1),
        vmem=10,
    )


def after(arrays, *others):
    return lax.optimization_barrier((arrays, others))[0]


def phase(*arrays):
    return lax.optimization_barrier(arrays)


def shards(
    inputs, query_weight, key_weight, value_weight, out_weight, up_weight, down_weight,
    gain_one, offset_one, gain_two, offset_two, pos_bias, prefix_len, cotangent,
):
    x, y, core = lax.axis_index("x"), lax.axis_index("y"), lax.axis_index("core")
    zh, zl = lax.axis_index("zh"), lax.axis_index("zl")
    z = zh * 2 + zl
    where = jnp.stack([x, y, z, core]).astype(jnp.int32)
    first_core = core == 0
    dma = lambda *shape: pltpu.SemaphoreType.DMA(shape)
    places = (pltpu.VMEM((4, 384, 384), F32),) * 2 + (dma(2, 4),)
    pair16 = lambda *shape: (kept_near(*shape, dtype=BF16),) * 2
    grad_blocks = (kept_far(384, 384),) * 8
    tables = place_tables()

    with jax.named_scope("pack"):
        vectors = jnp.concatenate([gain_one, offset_one, gain_two, offset_two, pos_bias])
        vectors = jnp.broadcast_to(jnp.pad(vectors, (0, 102)), (8, 128))
        kept, sent = glue(
            pack_one_kernel,
            ((48, 384),) * 2,
            (where, query_weight, key_weight, value_weight, up_weight, vectors),
            given=far,
        )
        tokens, cot, down, sent = phase(inputs[0], cotangent[0], down_weight, sent)
        got = swap_cores(sent)
        down = gather_at_once(down, "x")
        (block,) = glue(
            pack_two_kernel,
            ((104, 384),),
            (where, near(kept), near(got), far(out_weight)),
            given=lambda array: array,
        )
        (down,) = glue(stack_down_kernel, ((4, 24, 768),), (where, *down), gives=kept_far)

    with jax.named_scope("gather_z"):
        block, tokens, cot, down = phase(block, tokens, cot, down)
        down = lax.all_gather(down, "y", axis=0)
        seq = (x * 2 + zh) * 2 + core
        positions = seq * TOK + jnp.arange(TOK, dtype=jnp.int32)
        cot = cot * (positions >= prefix_len[0]).astype(F32)[:, None]
        others = swap_cores(tokens)
        block, others, cot = phase(gather_at_once(block, "z"), others, cot)
        one, two = glue(
            stack_one_kernel, ((4, HALF_ONE, 384), (4, HALF_TWO, 384)), (where, *block)
        )

    with jax.named_scope("gather_mid"):
        one, two, cot, tokens = phase(one, two, cot, tokens)
        halo = along_row(tokens, 1, (1,), (0,))
        near_one, near_two = phase(both_ways(one, "x"), both_ways(two, "y"))
        cot_other = swap_cores(after(cot, near_one))
        down = lax.all_gather(after(down, near_one), RING["z"], axis=0)
        far_one, far_two, cot_other = phase(hop(near_one[0], "x"), hop(near_two[0], "y"), cot_other)
        attn_one, up_one = glue(
            stack_two_kernel,
            ((392, 384), (384, 384)),
            (where, one, *near_one, far_one),
            0,
            gives=kept_far,
        )
        attn_two, up_two = glue(
            stack_two_kernel,
            ((384, 384), (384, 384)),
            (where, two, *near_two, far_two),
            1,
            gives=kept_far,
        )

    with jax.named_scope("gather_attn"):
        attn_one, attn_two, up_one, up_two, halo = phase(attn_one, attn_two, up_one, up_two, halo)
        halo = jnp.where(first_core, halo, swap_cores(halo))
        near_one, near_two, halo = phase(
            both_ways(attn_one, "y"), both_ways(attn_two, "x"), halo
        )
        far_one, far_two = phase(hop(near_one[0], "y"), hop(near_two[0], "x"))
        attn_one = (attn_one, *near_one, far_one)
        attn_two = (attn_two, *near_two, far_two)
        valid = jnp.where(x * 2 + zh > 0, 1.0, 0.0).astype(F32).reshape(1)
        all_tokens = (halo, tokens, others)

    with jax.named_scope("attn"):
        attn_one, attn_two, up_one, up_two = phase(attn_one, attn_two, up_one, up_two)
        near_one, near_two = both_ways(up_one, "y"), both_ways(up_two, "x")
        vec, base = call(
            vectors_kernel,
            (shaped(8, 768), shaped(8, 512)),
            (where, *map(far, attn_one), *tables[:2]),
            [SM] + [VM] * 6,
        )
        part, *held = call(
            attn_kernel,
            (shaped(512, 768),) + tuple(kept_far(*h, dtype=t) for h, t in ATTN_HELD),
            (where, *map(far, all_tokens), vec, base, valid, *map(far, attn_one + attn_two)),
            [SM] + [HB] * 3 + [VM, VM, SM] + [HB] * 8,
            [pltpu.VMEM(h, t) for h, t in ATTN_HELD]
            + [pltpu.VMEM((768, 768), F32), *places, dma(3), dma(13)],
            flops=5_700_000_000,
            moved=1_000_000,
            vmem=40,
            out_specs=(VM,) + (HB,) * 13,
        )
        near_one, near_two, part, held = phase(near_one, near_two, part, held)

    with jax.named_scope("ffn_early"):
        part_other = swap_cores(part)
        far_one, far_two = hop(near_one[0], "y"), hop(near_two[0], "x")
        *down_w, gh = call(
            ffn_early_kernel,
            (kept_far(1536, 768, dtype=BF16),) * 2 + (kept_near(512, 1536),),
            (where, *map(far, (down, cot, cot_other))),
            [SM] + [HB] * 3,
            [pltpu.VMEM((4, 4, 4, 24, 768), F32)]
            + [pltpu.VMEM((1536, 768), BF16)] * 2
            + [pltpu.VMEM((512, 768), F32), dma(2), dma(4), dma(2)],
            flops=3_600_000_000,
            moved=1_000_000,
            vmem=24,
            out_specs=(HB, HB, VM),
        )
        part_other, far_one, far_two, down_w, gh = phase(part_other, far_one, far_two, down_w, gh)
        up_all = (up_one, *near_one, far_one, up_two, *near_two, far_two)

    with jax.named_scope("ffn"):
        middle, *ffn_held, back_part = call(
            ffn_kernel,
            (kept_far(512, 768),) + pair16(768, 512) + pair16(512, 1536) * 2 + (kept_far(512, 768),),
            (where, *map(far, (tokens, others, part, part_other)), vec, near(gh), *map(far, up_all)),
            [SM] + [HB] * 4 + [VM] * 2 + [HB] * 8,
            (pltpu.VMEM((512, 768), F32),) * 4
            + places[:2]
            + (pltpu.VMEM((768, 1536), BF16),) * 2
            + (places[2], dma(4), dma(1)),
            flops=7_200_000_000,
            moved=1_000_000,
            vmem=28,
            out_specs=(HB,) + (VM,) * 7,
        )
        back_other = swap_cores(back_part)
        down_grads, *up_grads = call(
            ffn_late_kernel,
            (kept_far(4, 4, 4, 24, 768),) + grad_blocks,
            (where, far(cot), far(cot_other), *map(near, ffn_held)),
            [SM] + [HB] * 2 + [VM] * 6,
            places
            + (pltpu.VMEM((512, 768), F32), pltpu.VMEM((4, 4, 4, 24, 768), F32), dma(2), dma(32)),
            flops=7_300_000_000,
            moved=1_000_000,
            vmem=24,
            out_specs=(HB,) * 9,
        )
        back_other, up_grads, down_grads = phase(back_other, up_grads, down_grads)

    with jax.named_scope("attn_back"):
        up_one, up_two = up_grads[:4], up_grads[4:]
        came = scatter_start(up_one, "y"), scatter_start(up_two, "x")
        q_w, kv_w, o_w, xt, saved = held[:2], held[2:4], held[4:6], held[6:8], held[8:]
        gmid, gq, gkv, out_grad, small_two, bias = call(
            attn_back_kernel,
            (kept_far(512, 768), kept_near(512, 384), kept_near(768, 768), kept_near(384, 768))
            + (shaped(8, 768), shaped(8, 512)),
            (where, vec, base)
            + tuple(map(far, (middle, back_part, back_other, cot, cot_other, *o_w, *saved))),
            [SM] + [VM] * 2 + [HB] * 12,
            [pltpu.VMEM((512, 768), F32)] * 5
            + [pltpu.VMEM(h, t) for h, t in ATTN_HELD[4:6] + ATTN_HELD[8:]]
            + [dma(12), dma(1)],
            flops=5_000_000_000,
            moved=1_000_000,
            vmem=36,
            out_specs=(HB,) + (VM,) * 5,
        )
        down = lax.psum_scatter(down_grads, RING["z"], scatter_dimension=0, tiled=True)[0]
        came, gq, gkv, out_grad = phase(came, gq, gkv, out_grad)

    with jax.named_scope("attn_grads"):
        gq, gkv, out_grad = map(near, (gq, gkv, out_grad))
        up_one_came, up_two_came = scatter_end(where, up_one, up_two, came, "yx")
        attn_grads = call(
            attn_grads_kernel,
            (kept_far(392, 384),) * 4 + (kept_far(384, 384),) * 4,
            (where, vec, gq, gkv, out_grad, small_two, bias, *tables)
            + tuple(map(far, (*q_w, *kv_w, *xt))),
            [SM] + [VM] * 10 + [HB] * 6,
            [pltpu.VMEM((4, 392, 384), F32), *places[1:]]
            + [pltpu.VMEM(h, t) for h, t in ATTN_HELD[:4] + ATTN_HELD[6:8]]
            + [dma(6)],
            flops=3_600_000_000,
            moved=1_000_000,
            vmem=32,
            out_specs=(HB,) * 8,
        )
        up_one_came, up_two_came, attn_grads = phase(up_one_came, up_two_came, attn_grads)

    with jax.named_scope("attn_last"):
        attn_one, attn_two = attn_grads[:4], attn_grads[4:]
        came = scatter_start(attn_one, "y"), scatter_start(attn_two, "x")
        back_one = call(
            attn_last_kernel,
            kept_far(768, 768),
            (gq, gkv, *map(far, (*q_w, *kv_w))),
            [VM] * 2 + [HB] * 4,
            [pltpu.VMEM(h, t) for h, t in ATTN_HELD[:4]] + [dma(4)],
            flops=3_600_000_000,
            moved=1_000_000,
            vmem=20,
        )
        came, back_one = phase(came, back_one)

    start = core * TOK
    other = TOK - start
    half = TOK // 2

    def rows_at(array, at, count=TOK):
        return lax.dynamic_slice_in_dim(array, at, count, 0)

    with jax.named_scope("scatter_attn"):
        attn_one_came, attn_two_came = scatter_end(where, attn_one, attn_two, came, "yx")
        out_part = call(
            out_kernel,
            kept_far(512, 768),
            tuple(map(far, (*ffn_held[2:4], *down_w))),
            [HB] * 4,
            [pltpu.VMEM((512, 1536), BF16)] * 2 + [pltpu.VMEM((1536, 768), BF16)] * 2 + [dma(4)],
            flops=3_600_000_000,
            moved=1_000_000,
            vmem=16,
        )
        down = glue(part_down_kernel, ((4, 24, 768),) * 4, (where, down), 1, given=far)
        down_came = scatter_start(down, "y")
        halo_back = rows_at(back_one, core * half, half) + swap_cores(
            rows_at(back_one, half - core * half, half)
        )
        attn_one_came, attn_two_came, out_part, down_came, halo_back = phase(
            attn_one_came, attn_two_came, out_part, down_came, halo_back
        )

    def tail(own, came):
        return far(own), *map(near, came)

    as_is = lambda array: array

    with jax.named_scope("scatter_mid"):
        halo_back = along_row(halo_back, -1, (0, 1), (0, 1))
        one = glue(
            part_one_kernel,
            ((4, HALF_ONE, 384),) * 4,
            (where, *tail(attn_one[0], attn_one_came), *tail(up_one[0], up_one_came)),
            0,
            given=as_is,
        )
        two = glue(
            part_one_kernel,
            ((4, HALF_TWO, 384),) * 4,
            (where, *tail(attn_two[0], attn_two_came), *tail(up_two[0], up_two_came)),
            1,
            given=as_is,
        )
        came = scatter_start(one, "x"), scatter_start(two, "y")
        came, one, two = phase(came, one, two)

        (next_down,) = glue(add_one_kernel, ((4, 24, 768),), (where, down[1], down_came[0]))
        back_other = swap_cores(rows_at(back_one, TOK + other))
        one_came, two_came = scatter_end(where, one, two, came, "xy", near)
        one_came, two_came, next_down, back_other, halo_back = phase(
            one_came, two_came, hop(next_down, "y"), back_other, halo_back
        )

    with jax.named_scope("scatter_z"):
        block = glue(
            part_two_kernel, ((104, 384),) * 4, (where, one[0], *one_came, two[0], *two_came)
        )
        down = glue(sum_down_kernel, ((24, 768),) * 4, (where, down[0], down_came[1], next_down), 0)
        block, down = phase(block, down)
        block = scatter_at_once(block, "z")
        down_came = scatter_start(down, "x")
        output_other = swap_cores(rows_at(out_part, other))
        halo_back = jnp.concatenate([swap_cores(halo_back), halo_back], axis=0)
        back = rows_at(back_one, TOK + start) + back_other
        back = back + jnp.where(first_core, 0.0, halo_back)
        xhat, scale = normal_parts(inputs[0])
        input_grad = rows_at(gmid, start) + normal_back(back, xhat, scale, vec[0:1])
        block, down_came, output_other, input_grad = phase(block, down_came, output_other, input_grad)

    with jax.named_scope("finish"):
        out_grad, kept, sent = glue(
            sum_three_kernel, ((6, 768), (48, 384), (48, 384)), (where, *block)
        )
        (next_down,) = glue(add_one_kernel, ((24, 768),), (where, down[1], down_came[0]))
        got, next_down = phase(swap_cores(sent), hop(next_down, "x"))
        output = rows_at(middle, start) + rows_at(out_part, start) + output_other
        down = down[0] + down_came[1] + next_down
        *qkv, up_out, line = glue(
            finish_kernel, ((6, 768),) * 3 + ((6, 3072), (8, 128)), (where, kept, got), gives=shaped
        )
        line = line[0]

    return (
        output[None], input_grad[None], *qkv, out_grad, up_out, down,
        line[0:6], line[6:12], line[12:18], line[18:24], line[24:26],
    )


def solution(mesh):
    fine = Mesh(mesh.devices.reshape(4, 2, 2, 4, 2), AXES)
    tokens = P(("y", "zl"), ("x", "zh", "core"), None)
    matrix = P(AXES, None)
    vector = P(AXES)
    return jax.shard_map(
        shards,
        mesh=fine,
        in_specs=(tokens,) + (matrix,) * 6 + (vector,) * 5 + (P(("y", "zl")), tokens),
        out_specs=(tokens, tokens) + (matrix,) * 6 + (vector,) * 5,
        check_vma=False,
    )
```

```python
import functools

import jax
import jax.numpy as jnp
import numpy as np
from jax import lax
from jax.experimental import pallas as pl
from jax.experimental.pallas import tpu as pltpu
from jax.sharding import Mesh
from jax.sharding import PartitionSpec as P

EPSILON = 1e-05
AXES = ("x", "zh", "core", "y", "zl")
RING = {"x": "x", "y": "y", "z": ("zh", "zl")}
F32, BF16 = jnp.float32, jnp.bfloat16
TOK = 256
NT = (((1,), (1,)), ((), ()))
NN = (((1,), (0,)), ((), ()))
ANY = pl.BlockSpec(memory_space=pl.ANY)
HB = pl.BlockSpec(memory_space=pltpu.HBM)
VM = pl.BlockSpec(memory_space=pltpu.VMEM)
SM = pl.BlockSpec(memory_space=pltpu.SMEM)


def shift(array, axis, by):
    return lax.ppermute(array, RING[axis], [(i, (i + by) % 4) for i in range(4)])


def swap_cores(array):
    return lax.ppermute(array, "core", [(0, 1), (1, 0)])


def index_of(x, zh, core, y, zl):
    return (((x * 2 + zh) * 2 + core) * 4 + y) * 2 + zl


def along_row(array, by, from_core, to_core):
    pairs = []
    for chip in range(8):
        if 0 <= chip + by < 8:
            for y in range(4):
                for zl in range(2):
                    for a, b in zip(from_core, to_core):
                        pairs.append(
                            (
                                index_of(chip // 2, chip % 2, a, y, zl),
                                index_of((chip + by) // 2, (chip + by) % 2, b, y, zl),
                            )
                        )
    return lax.ppermute(array, AXES, pairs)


def hop(array, axis, by=1):
    pairs = []
    for at in np.ndindex(4, 4, 2, 4):
        to = dict(zip("xzcy", at))
        to[axis] = (to[axis] + by * (1 - 2 * to["c"])) % 4
        pairs.append(
            tuple(index_of(p[0], p[1] // 2, p[2], p[3], p[1] % 2) for p in (at, tuple(to.values())))
        )
    return lax.ppermute(array, AXES, pairs)


FROM = (0, 3, 1, 2)


def both_ways(block, axis):
    return hop(block, axis), hop(block, axis, -1)


def scatter_start(parts, axis):
    return hop(parts[2], axis), hop(parts[3], axis, -1)


def add_kernel(where, a0, a1, b0, b1, a_sum, b_sum):
    a_sum[...] = a0[...] + a1[...]
    b_sum[...] = b0[...] + b1[...]


def scatter_end(where, one, two, came, axes, parts=None):
    shapes = (one[1].shape, two[1].shape)
    parts = parts or far
    args = (where, parts(one[1]), came[0][0], parts(two[1]), came[1][0])
    sums = glue(add_kernel, shapes, args, given=lambda array: array, gives=shaped)
    return [(c[1], hop(a, axis)) for c, a, axis in zip(came, sums, axes)]


def gather_at_once(block, axis):
    return [block] + [shift(block, axis, -k) for k in (1, 2, 3)]


def scatter_at_once(parts, axis):
    return [parts[0]] + [shift(parts[k], axis, k) for k in (1, 2, 3)]


def split(value):
    high = value.astype(BF16)
    return high, (value - high.astype(F32)).astype(BF16)


def dot3(left, right, dims=NN):
    def one(a, b):
        return lax.dot_general(a, b, dims, preferred_element_type=F32)

    return one(left[0], right[0]) + one(left[0], right[1]) + one(left[1], right[0])


def normal_parts(values):
    centred = values - jnp.mean(values, axis=-1, keepdims=True)
    spread = jnp.mean(centred * centred, axis=-1, keepdims=True)
    scale = lax.rsqrt(spread + EPSILON)
    return centred * scale, scale


def normal_back(grad, xhat, scale, gain):
    e = grad * gain
    return scale * (
        e
        - jnp.mean(e, axis=-1, keepdims=True)
        - xhat * jnp.mean(e * xhat, axis=-1, keepdims=True)
    )


def normal_cdf(v):
    density = jnp.exp(-0.5 * v * v)
    d = 1.0 + np.float32(0.3275911 * np.sqrt(0.5)) * jnp.abs(v)
    t = pl.reciprocal(d, approx=True)
    t = t * (2.0 - d * t)
    t = t * (2.0 - d * t)
    total = np.float32(0.5 * 1.061405429)
    for c in (-1.453152027, 1.421413741, -0.284496736, 0.254829592):
        total = total * t + np.float32(0.5 * c)
    total = total * t * density
    return jnp.where(v < 0.0, total, 1.0 - total), density * np.float32(1.0 / np.sqrt(2.0 * np.pi))


HALF_ONE, HALF_TWO = 56, 48


def halved(array, c, run):
    count = array.shape[1] // (2 * run)
    return jnp.concatenate(
        [array[:, (2 * i + c) * run : (2 * i + c + 1) * run] for i in range(count)], axis=1
    )


def joined(first, second, run):
    count = first.shape[1] // run
    return jnp.concatenate(
        [h[:, i * run : (i + 1) * run] for i in range(count) for h in (first, second)], axis=1
    )


def pack_one_kernel(where, q, k, v, up, g_one, o_one, g_two, o_two, bias, kept, sent):
    vec = [ref[...] for ref in (g_one, o_one, g_two, o_two, bias)]
    vec = jnp.concatenate(vec + [jnp.zeros((1, 384 - 26), F32)], axis=1)
    both = []
    for c in range(2):
        wide = halved(up[...], c, 192)
        both.append(
            jnp.concatenate(
                [halved(w[...], c, 48) for w in (q, k, v)]
                + [wide[:, 384 * i : 384 * i + 384] for i in range(4)]
                + [jnp.broadcast_to(vec, (6, 384))],
                axis=0,
            )
        )
    first = where[3] == 0
    kept[...] = jnp.where(first, both[0], both[1])
    sent[...] = jnp.where(first, both[1], both[0])


def pack_two_kernel(where, kept, got, out, block):
    first = where[3] == 0
    one = jnp.where(first, kept[...], got[...])
    two = jnp.where(first, got[...], kept[...])

    def rows(i):
        return [one[6 * i : 6 * i + 6], two[6 * i : 6 * i + 6]]

    line = one[42:43, :128] + pltpu.roll(two[42:43, :128], 64, 1)
    block[0:24] = jnp.concatenate(rows(0) + rows(1), axis=0)
    block[24:32] = jnp.concatenate([jnp.broadcast_to(line, (8, 128)), jnp.zeros((8, 256), F32)], axis=1)
    block[32:56] = jnp.concatenate(rows(3) + rows(4), axis=0)
    block[56:80] = jnp.concatenate(rows(2) + [out[:, :384], out[:, 384:]], axis=0)
    block[80:104] = jnp.concatenate(rows(5) + rows(6), axis=0)


def stack_one_kernel(where, p0, p1, p2, p3, one, two):
    for off, ref in enumerate((p0, p1, p2, p3)):
        at = lax.rem(where[2] + off, 4)
        one[at] = ref[:HALF_ONE]
        two[at] = ref[HALF_ONE:]


def at_hops(where, axis, hops):
    return lax.rem(where[axis] + 4 + hops * (1 - 2 * where[3]), 4)


def stack_down_kernel(where, p0, p1, p2, p3, out):
    for hops, ref in zip(FROM, (p0, p1, p2, p3)):
        out[at_hops(where, 0, hops)] = ref[...]


def stack_two_kernel(axis, where, p0, p1, p2, p3, attn, up):
    skip = 8 if axis == 0 else 0
    row = lax.broadcasted_iota(jnp.int32, (8, 128), 0)
    vec = [jnp.zeros((8, 128), F32)] * 3
    for hops, ref in zip(FROM, (p0, p1, p2, p3)):
        at = at_hops(where, axis, hops)
        for z in range(4):
            rows = pl.ds(pl.multiple_of(at * 96 + 24 * z, 8), 24)
            attn[rows] = ref[z, 0:24]
            up[rows] = ref[z, 24 + skip : 48 + skip]
            if skip:
                line = ref[z, 24:32, :128]
                vec[z % 2] = jnp.where(row == at * 2 + z // 2, line, vec[z % 2])
    if skip:
        attn[384:392] = jnp.concatenate(vec, axis=1)


def stack_both_kernel(where, *refs):
    stack_two_kernel(0, where, *refs[:4], *refs[8:10])
    stack_two_kernel(1, where, *refs[4:8], *refs[10:])


def feature_places():
    x, zh, c, y, zl, r = np.indices((4, 2, 2, 4, 2, 6)).reshape(6, -1)
    return [a.astype(np.int32) for a in (y, zl * 8 + x * 2 + zh, x * 4 + zh * 2 + zl, c * 64 + r)]


def offset_places():
    x, zh, c, y, zl, r = np.indices((4, 2, 2, 4, 2, 2)).reshape(6, -1)
    places = []
    for a in (y, zl * 8 + x * 2 + zh, x * 4 + zh * 2 + zl, c * 64 + 24 + r):
        line = np.full((512,), -1000, np.int32)
        line[1:257] = a[::-1]
        places.append(line)
    return places


def place_tables():
    rows = [np.pad(np.stack(t), ((0, 4), (0, 0))) for t in (feature_places(), offset_places())]
    return rows + [np.ascontiguousarray(np.pad(r.T, ((0, 0), (0, 120)))) for r in rows]


def three_parts(value):
    high, rest = split(value)
    rest = value - high.astype(F32)
    return (high, *split(rest))


def pick_dot(left, right):
    return sum(jnp.dot(a, b, preferred_element_type=F32) for a in left for b in right)


def spread_vectors(where, pieces, features, offsets):
    lines = []
    for k in (0, 2, 3, 1):
        last = pieces[k][:, :256]
        lines += [last[:, :128], last[:, 128:]]
    lines = three_parts(jnp.concatenate(lines, axis=0).T)

    def spread(table):
        hops = jnp.bitwise_and((table[0:1, :] + 4 - where[1]) * (1 - 2 * where[3]), 3)
        place = hops * 16 + table[1:2, :]
        chips = lax.broadcasted_iota(jnp.int32, (64, table.shape[1]), 0) == place
        return pick_dot(lines, (chips.astype(F32).astype(BF16),))

    values = spread(features)
    lane = lax.broadcasted_iota(jnp.int32, values.shape, 0)
    picked = [
        jnp.sum(jnp.where(lane == features[3:4, :] + 6 * i, values, 0.0), axis=0, keepdims=True)
        for i in range(4)
    ]
    values = spread(offsets)
    lane = lax.broadcasted_iota(jnp.int32, values.shape, 0)
    base = jnp.sum(jnp.where(lane == offsets[3:4, :], values, 0.0), axis=0, keepdims=True)
    base = jnp.where(offsets[3:4, :] >= 0, jnp.exp(base), 0.0)
    return picked, base


def place_lines(where, smalls, bias, features, offsets, feature_columns, offset_columns):
    def gathered(values, table, columns, lane):
        hops = jnp.bitwise_and((table[0:1, :] + 4 - where[1]) * (1 - 2 * where[3]), 3)
        place = hops * 16 + table[1:2, :]
        chips = lax.broadcasted_iota(jnp.int32, (64, table.shape[1]), 0) == place
        lanes = lax.broadcasted_iota(jnp.int32, (table.shape[1], 128), 1) == columns[:, 3:4] + lane
        return pick_dot(
            three_parts(jnp.where(chips, values, 0.0)), (lanes.astype(F32).astype(BF16),)
        )

    total = gathered(bias, offsets[...], offset_columns[...], 0)
    for i, small in enumerate(smalls):
        total += gathered(small, features[...], feature_columns[...], 6 * i)
    return total


def ring_copies(where, axis, places, parts, whole, sems, rows=384):
    return [
        (p.at[pl.ds(0, rows)], whole.at[at_hops(where, axis, hops), pl.ds(0, rows)], sems.at[i])
        for i, (hops, p) in enumerate(zip(places, parts))
    ]


def bring(where, ones, twos, one, two, sems):
    copies = ring_copies(where, 1, FROM, ones, one, sems.at[0])
    copies += ring_copies(where, 0, FROM, twos, two, sems.at[1])
    copies = [pltpu.make_async_copy(*c) for c in copies]
    for copy in copies:
        copy.start()
    return copies


def send(where, axis, parts, whole, sems, rows=384):
    copies = ring_copies(where, axis, range(4), parts, whole, sems, rows)
    copies = [pltpu.make_async_copy(place, part, sem) for part, place, sem in copies]
    for copy in copies:
        copy.start()
    return copies


def by_group(one, two, group):
    x, zh = group // 2, lax.rem(group, 2)
    held = ([], [])
    for y in range(4):
        for zl in range(2):
            z = zh * 2 + zl
            held[0].append(one[y, pl.ds(pl.multiple_of((x * 4 + z) * 24, 8), 24)])
            held[1].append(two[x, pl.ds(pl.multiple_of((y * 4 + z) * 24, 8), 24)])
    return held


def unpack_attn(one, two, q_hi, q_lo, kv_hi, kv_lo, o_hi, o_lo):
    def step(group, carry):
        held = by_group(one, two, group)

        def rows(part, first):
            return jnp.concatenate([h[first : first + 6] for h in held[part]], axis=0)

        for c in range(2):
            at = pl.ds(pl.multiple_of(group * 96 + c * 48, 16), 48)
            q_hi[at, :], q_lo[at, :] = split(rows(0, 6 * c))
            kv_hi[at, :384], kv_lo[at, :384] = split(rows(0, 12 + 6 * c))
            kv_hi[at, 384:], kv_lo[at, 384:] = split(rows(1, 6 * c))
            at = pl.ds(pl.multiple_of(group * 48, 16), 48)
            lanes = pl.ds(384 * c, 384)
            o_hi[at, lanes], o_lo[at, lanes] = split(rows(1, 12 + 6 * c))
        return carry

    lax.fori_loop(0, 8, step, 0)


def unpack_up(one, two, up_hi, up_lo):
    def step(group, carry):
        held = by_group(one, two, group)
        for c in range(2):
            at = pl.ds(pl.multiple_of(group * 96 + c * 48, 16), 48)
            for part in range(2):
                for b in range(2):
                    first = 12 * b + 6 * c
                    rows = jnp.concatenate([h[first : first + 6] for h in held[part]], axis=0)
                    lanes = pl.ds(768 * part + 384 * b, 384)
                    up_hi[at, lanes], up_lo[at, lanes] = split(rows)
        return carry

    lax.fori_loop(0, 8, step, 0)


def place_in_blocks(one, two, first, second):
    for group in range(8):
        x, zh = group // 2, group % 2
        for y in range(4):
            for zl in range(2):
                z, j = zh * 2 + zl, y * 2 + zl

                def rows(array):
                    at = [group * 96 + 48 * c + 6 * j for c in range(2)]
                    return [array[a : a + 6] for a in at]

                if first is not None:
                    one[y, (x * 4 + z) * 24 : (x * 4 + z) * 24 + 24] = jnp.concatenate(
                        rows(first[0]) + rows(first[1]), axis=0
                    )
                if second is not None:
                    ends = second[1]
                    if ends.shape[0] == 768:
                        ends = rows(ends)
                    else:
                        ends = ends[group * 48 + 6 * j : group * 48 + 6 * j + 6]
                        ends = [ends[:, :384], ends[:, 384:]]
                    two[x, (y * 4 + z) * 24 : (y * 4 + z) * 24 + 24] = jnp.concatenate(
                        rows(second[0]) + ends, axis=0
                    )


def part_one_kernel(axis, where, a0, a1, a2, b0, b1, b2, *more):
    skip = 8 if axis == 0 else 0
    if skip:
        lines = a0[384:392, :256] + a1[384:392, :256] + a2[384:392, :256]
        row = lax.broadcasted_iota(jnp.int32, (8, 128), 0)
    for hops, out in enumerate(more[-4:]):
        at = at_hops(where, axis, hops)
        for z in range(4):
            rows = pl.ds(pl.multiple_of(at * 96 + 24 * z, 8), 24)
            out[z, 0:24] = a0[rows] + a1[rows] + a2[rows]
            if skip:
                line = lines[:, 128 * (z % 2) : 128 * (z % 2) + 128]
                line = jnp.sum(jnp.where(row == at * 2 + z // 2, line, 0.0), axis=0, keepdims=True)
                out[z, 24:32] = jnp.concatenate(
                    [jnp.broadcast_to(line, (8, 128)), jnp.zeros((8, 256), F32)], axis=1
                )
            out[z, 24 + skip : 48 + skip] = b0[rows] + b1[rows] + b2[rows]


def part_down_kernel(axis, where, down, *outs):
    for hops, out in enumerate(outs):
        out[...] = down[at_hops(where, axis, hops)]


def add_one_kernel(where, a0, a1, total):
    total[...] = a0[...] + a1[...]


def part_two_kernel(where, a0, a1, a2, b0, b1, b2, o0, o1, o2, o3):
    for k, out in enumerate((o0, o1, o2, o3)):
        z = lax.rem(where[2] + k, 4)
        out[:HALF_ONE] = a0[z] + a1[z] + a2[z]
        out[HALF_ONE:] = b0[z] + b1[z] + b2[z]


def sum_three_kernel(where, a0, a1, a2, a3, out, kept, sent):
    block = (a0[...] + a1[...]) + (a2[...] + a3[...])
    out[...] = jnp.concatenate([block[68:74], block[74:80]], axis=1)
    line = block[24:25, :128]
    both = []
    for c in range(2):
        rows = [block[at + 6 * c : at + 6 * c + 6] for at in (0, 12, 56, 32, 44, 80, 92)]
        vec = line if c == 0 else pltpu.roll(line, 64, 1)
        vec = jnp.concatenate([jnp.broadcast_to(vec, (6, 128)), jnp.zeros((6, 256), F32)], axis=1)
        both.append(jnp.concatenate(rows + [vec], axis=0))
    first = where[3] == 0
    kept[...] = jnp.where(first, both[0], both[1])
    sent[...] = jnp.where(first, both[1], both[0])


def finish_kernel(where, kept, got, q, k, v, up, *vectors):
    first = where[3] == 0
    one = jnp.where(first, kept[...], got[...])
    two = jnp.where(first, got[...], kept[...])
    for i, ref in enumerate((q, k, v)):
        ref[...] = joined(one[6 * i : 6 * i + 6], two[6 * i : 6 * i + 6], 48)
    wide = [
        jnp.concatenate([h[18 + 6 * i : 24 + 6 * i] for i in range(4)], axis=1) for h in (one, two)
    ]
    up[...] = joined(wide[0], wide[1], 192)
    line = one[42:43, :128] + two[42:43, :128]
    for i, ref in enumerate(vectors):
        ref[...] = line[:, 6 * i : 6 * i + ref.shape[1]]


def toeplitz(base):
    return pltpu.roll(jnp.broadcast_to(base, (TOK, 2 * TOK)), 0, 1, stride=1, stride_axis=0)


def fetch_pair(where, mine, other, held, first, sems):
    core = where[3]
    return fetch(
        (mine, other),
        [held.at[pl.ds(pl.multiple_of(first + c * TOK, TOK), TOK)] for c in (core, 1 - core)],
        sems,
    )


def fetch(refs, held, sems):
    copies = [pltpu.make_async_copy(r, h, sems.at[i]) for i, (r, h) in enumerate(zip(refs, held))]
    for copy in copies:
        copy.start()
    return copies


def wait(copies):
    for copy in copies:
        copy.wait()


ATTN_HELD = (
    (((768, 384), BF16),) * 2
    + (((768, 768), BF16),) * 2
    + (((384, 768), BF16),) * 2
    + (((512, 384), F32),) * 3
    + (((768, 384), F32),) * 2
)


def norm_kernel(where, halo, tokens, others, xhat_ref, xt_hi_far, xt_lo_far, x_ref, xt_hi, xt_lo, sems):
    fetched = fetch((halo,), (x_ref.at[pl.ds(0, TOK)],), sems)
    fetched += fetch_pair(where, tokens, others, x_ref, TOK, sems.at[pl.ds(1, 2)])
    wait(fetched)
    xhat, _ = normal_parts(x_ref[...])
    xhat_ref[...] = xhat
    xt_hi[...], xt_lo[...] = split(xhat.T)
    wait(fetch((xt_hi, xt_lo), (xt_hi_far, xt_lo_far), sems.at[pl.ds(3, 2)]))


def attn_kernel(
    where, xhat_ref, valid_ref, features, offsets, a0, a1, a2, a3, b0, b1, b2, b3,
    part_far, vec_ref, base_ref, *more,
):
    outs, held = more[:11], more[11:22]
    part_ref, one, two, lines, sems, out_sems, part_sems, line_sems = more[22:]
    q_hi, q_lo, kv_hi, kv_lo, o_hi, o_lo, sig_ref, ratio_ref, inv_ref, w_ref, v_ref = held

    def keep(first, count):
        at = slice(first, first + count)
        return fetch(held[at], outs[at], out_sems.at[pl.ds(first, count)])

    fetched = fetch(
        [a.at[pl.ds(384, 8)] for a in (a0, a1, a2, a3)], [lines.at[k] for k in range(4)], line_sems
    )
    copies = bring(where, (a0, a1, a2, a3), (b0, b1, b2, b3), one, two, sems)
    wait(fetched)
    picked, base = spread_vectors(where, [lines[k] for k in range(4)], features[...], offsets[...])
    vec_ref[...] = jnp.concatenate(picked + [jnp.zeros((4, 768), F32)], axis=0)
    base_ref[...] = jnp.broadcast_to(base, (8, 512))
    wait(copies)
    unpack_attn(one, two, q_hi, q_lo, kv_hi, kv_lo, o_hi, o_lo)
    kept = keep(0, 6)
    gain, offset = picked[:2]
    parts = split(xhat_ref[...] * gain + offset)
    own = tuple(p[TOK:] for p in parts)
    keys = dot3(parts, (kv_hi[...], kv_lo[...]))
    sig_ref[...] = jax.nn.sigmoid(dot3(own, (q_hi[...], q_lo[...])))
    w = jnp.exp(keys[:, :384])
    w_ref[:TOK] = w[:TOK] * valid_ref[0]
    w_ref[TOK:] = w[TOK:]
    v_ref[...] = keys[:, 384:]
    kept += keep(6, 1) + keep(9, 2)
    w = w_ref[...]
    sums = split(jnp.concatenate([w * v_ref[...], w], axis=1))
    band = split(toeplitz(base))
    for i in range(2):
        at = slice(TOK * i, TOK * i + TOK)
        seen = tuple(s[TOK * i : TOK * i + 2 * TOK] for s in sums)
        mixed = dot3(band, seen)
        inverse = 1.0 / mixed[:, 384:]
        inv_ref[at] = inverse
        ratio_ref[at] = mixed[:, :384] * inverse
    kept += keep(7, 2)
    mixed = split(sig_ref[...] * ratio_ref[...])
    part_ref[...] = dot3(mixed, (o_hi[...], o_lo[...]))
    halves = [pl.ds(TOK * c, TOK) for c in range(2)]
    wait(kept + fetch([part_ref.at[p] for p in halves], [part_far.at[p] for p in halves], part_sems))


def fetch_down(down_far, down, sems):
    return fetch([down_far.at[z] for z in range(4)], [down.at[z] for z in range(4)], sems)


def unpack_down(fetched, down, down_hi, down_lo):
    for zh in range(2):
        wait(fetched[2 * zh : 2 * zh + 2])
        for x in range(4):
            for y in range(4):
                rows = jnp.concatenate([down[2 * zh + zl, y, x] for zl in range(2)], axis=0)
                at = pl.ds(((x * 2 + zh) * 4 + y) * 48, 48)
                down_hi[at, :], down_lo[at, :] = split(rows)


def ffn_early_kernel(
    where, down_far, mine, other, gh_ref, down, down_hi, down_lo, cot_ref, cot_sems, in_sems
):
    kept = fetch_down(down_far, down, in_sems)
    fetched = fetch_pair(where, mine, other, cot_ref, 0, cot_sems)
    unpack_down(kept, down, down_hi, down_lo)
    wait(fetched)
    cot = split(cot_ref[...])
    for i in range(2):
        at = slice(768 * i, 768 * i + 768)
        gh_ref[:, at] = dot3(cot, (down_hi[at], down_lo[at]), NT)


def ffn_kernel(
    where, tokens, others, mine_far, theirs_ref, vec_ref, gh_ref, a0, a1, a2, a3, b0, b1, b2, b3,
    middle_far, middle_own, nt_hi, nt_lo, h_hi, h_lo, g_hi, g_lo, back_far,
    middle_ref, back_ref, x_ref, mine_ref, one, two, up_hi, up_lo, sems, in_sems, out_sems,
):
    fetched = fetch((mine_far,), (mine_ref,), in_sems)
    fetched += fetch_pair(where, tokens, others, x_ref, 0, in_sems.at[pl.ds(2, 2)])
    wait(bring(where, (a0, a1, a2, a3), (b0, b1, b2, b3), one, two, sems))
    unpack_up(one, two, up_hi, up_lo)
    wait(fetched)
    middle_ref[...] = x_ref[...] + (mine_ref[...] + theirs_ref[...])
    own = pl.ds(pl.multiple_of(where[3] * TOK, TOK), TOK)
    sent = fetch((middle_ref, middle_ref.at[own]), (middle_far, middle_own), out_sems)
    xhat, _ = normal_parts(middle_ref[...])
    normed = xhat * vec_ref[2:3, :] + vec_ref[3:4, :]
    parts = split(normed)
    nt_hi[...], nt_lo[...] = split(normed.T)
    halves = [pl.ds(TOK * c, TOK) for c in range(2)]
    for c, rows in enumerate((slice(0, TOK), slice(TOK, 2 * TOK))):
        for i in range(6):
            at = slice(256 * i, 256 * i + 256)
            preact = dot3(tuple(p[rows] for p in parts), (up_hi[:, at], up_lo[:, at]))
            lower, density = normal_cdf(preact)
            slope = lower + preact * density
            h_hi[rows, at], h_lo[rows, at] = split(preact * lower)
            g_hi[rows, at], g_lo[rows, at] = split(gh_ref[rows, at] * slope)
        back_ref[rows] = dot3((g_hi[rows], g_lo[rows]), (up_hi[...], up_lo[...]), NT)
        sent += fetch((back_ref.at[halves[c]],), (back_far.at[halves[c]],), out_sems.at[pl.ds(2 + c, 1)])
    wait(sent)


def ffn_late_kernel(
    where, cot_mine, cot_other, nt_hi, nt_lo, h_hi, h_lo, g_hi, g_lo,
    down_grad_far, a0, a1, a2, a3, b0, b1, b2, b3, one, two, sems, cot_ref, down_grad,
    in_sems, out_sems,
):
    fetched = fetch_pair(where, cot_mine, cot_other, cot_ref, 0, in_sems)
    nt = (nt_hi[...], nt_lo[...])
    sent = []
    wait(fetched)
    cot = split(cot_ref[...])
    for i in range(2):
        at = slice(768 * i, 768 * i + 768)
        rows = dot3((h_hi[:, at].T, h_lo[:, at].T), cot)
        for chip in range(32):
            x, zh, y, zl = (2 * i + chip // 16), chip // 8 % 2, chip // 2 % 4, chip % 2
            down_grad[2 * zh + zl, y, x] = rows[chip * 24 : chip * 24 + 24]
        for place in range(16):
            part = (place // 4, place % 4, pl.ds(2 * i, 2))
            sem = out_sems.at[i * 16 + place]
            sent.append(pltpu.make_async_copy(down_grad.at[part], down_grad_far.at[part], sem))
            sent[-1].start()
    for i in range(2):
        at = slice(768 * i, 768 * i + 768)
        grad = dot3(nt, (g_hi[:, at], g_lo[:, at]))
        pair = (grad[:, :384], grad[:, 384:])
        place_in_blocks(one, two, *((pair, None) if i == 0 else (None, pair)))
        sent += send(where, 1 - i, ((a0, a1, a2, a3), (b0, b1, b2, b3))[i], (one, two)[i], sems.at[i])
    wait(sent)


def out_kernel(
    where, h_hi_far, h_lo_far, down_far, own, other,
    h_hi, h_lo, down, down_hi, down_lo, out_ref, sems, in_sems, out_sems,
):
    kept = fetch_down(down_far, down, in_sems)
    fetched = fetch((h_hi_far, h_lo_far), (h_hi, h_lo), sems)
    unpack_down(kept, down, down_hi, down_lo)
    wait(fetched)
    for i in range(2):
        at = slice(768 * i, 768 * i + 768)
        out = dot3((h_hi[:, at], h_lo[:, at]), (down_hi[at], down_lo[at]))
        if i == 0:
            out_ref[...] = out
        else:
            out_ref[...] += out
    places = [pl.ds(pl.multiple_of(TOK * c, TOK), TOK) for c in (where[3], 1 - where[3])]
    wait(fetch([out_ref.at[p] for p in places], (own, other), out_sems))


def attn_back_kernel(
    where, vec_ref, base_ref, middle_far, mine_far, theirs_ref, cot_mine, cot_other,
    f0, f1, f2, f3, f4, f5, f6, gmid_own, gq_ref, gkv_ref, out_grad, small_ref, bias_ref,
    middle_ref, mine_ref, cot_ref, gmid_ref,
    o_hi, o_lo, sig_ref, ratio_ref, inv_ref, w_ref, v_ref, sems, out_sems,
):
    halves = [pl.ds(TOK * c, TOK) for c in range(2)]
    first = [
        fetch([far.at[p] for p in halves], [ref.at[p] for p in halves], sems.at[pl.ds(9 + 2 * i, 2)])
        for i, (far, ref) in enumerate(((middle_far, middle_ref), (mine_far, mine_ref)))
    ]
    copies = fetch_pair(where, cot_mine, cot_other, cot_ref, 0, sems)
    copies += fetch((f0, f1), (o_hi, o_lo), sems.at[pl.ds(2, 2)])
    wait(first[0])
    xhat, scale = normal_parts(middle_ref[...])
    wait(first[1])
    kept = fetch(
        (f2, f3, f4, f5, f6), (sig_ref, ratio_ref, inv_ref, w_ref, v_ref), sems.at[pl.ds(4, 5)]
    )
    mine = mine_ref[...]
    small_ref[2:3, :] = jnp.sum(mine * xhat, axis=0, keepdims=True)
    small_ref[3:4, :] = jnp.sum(mine, axis=0, keepdims=True)
    gmid = normal_back(mine + theirs_ref[...], xhat, scale, vec_ref[2:3, :])
    wait(copies)
    gmid = cot_ref[...] + gmid
    gmid_ref[...] = gmid
    gmid = split(gmid)
    own = pl.ds(pl.multiple_of(where[3] * TOK, TOK), TOK)
    sent = fetch((gmid_ref.at[own],), (gmid_own,), out_sems)
    gmixed = dot3(gmid, (o_hi[...], o_lo[...]), NT)
    wait(kept)
    sig, ratio = sig_ref[...], ratio_ref[...]
    out_grad[...] = dot3(split((sig * ratio).T), gmid)
    gq = gmixed * ratio * sig * (1.0 - sig)
    gq_ref[...] = gq
    gnum = gmixed * sig * inv_ref[...]
    gsums = split(jnp.concatenate([gnum, -gnum * ratio], axis=1))
    band = toeplitz(base_ref[0:1, :])
    band_t = split(band.T)
    w, v = w_ref[...], v_ref[...]
    sums = split(jnp.concatenate([w * v, w], axis=1))
    spread, gband = [], None
    for i in range(2):
        here = tuple(g[TOK * i : TOK * i + TOK] for g in gsums)
        seen = tuple(s[TOK * i : TOK * i + 2 * TOK] for s in sums)
        spread.append(dot3(band_t, here))
        term = dot3(here, seen, NT)
        gband = term if gband is None else gband + term
    count = TOK
    while count > 1:
        count //= 2
        gband = gband[:count] + pltpu.roll(gband[count:], 2 * TOK - count, 1)
    bias_ref[...] = jnp.broadcast_to(gband * base_ref[0:1, :], (8, 2 * TOK))
    gseen = jnp.concatenate(
        [spread[0][:TOK], spread[0][TOK:] + spread[1][:TOK], spread[1][TOK:]], axis=0
    )
    gkv = jnp.concatenate([w * (gseen[:, :384] * v + gseen[:, 384:]), gseen[:, :384] * w], axis=1)
    gkv_ref[...] = gkv
    wait(sent)


def attn_grads_kernel(
    where, vec_ref, gq_ref, gkv_ref, out_grad, small_two, bias, features, offsets, feature_columns,
    offset_columns, f0, f1, f2, f3, f4, f5, a0, a1, a2, a3, b0, b1, b2, b3,
    one, two, sems, q_hi, q_lo, kv_hi, kv_lo, xt_hi, xt_lo, in_sems, line_sems,
):
    kept = fetch((f4, f5, f0, f1, f2, f3), (xt_hi, xt_lo, q_hi, q_lo, kv_hi, kv_lo), in_sems)
    gq, gkv = gq_ref[...], gkv_ref[...]
    vec = vec_ref[...].T
    wait(kept[:2])
    small = [0.0, 0.0]

    def grad_of(dots, g):
        total = jnp.sum(g, axis=0, keepdims=True)
        return vec[:, 0:1] * dots + vec[:, 1:2] * total

    def add_small(dots, g, high, low):
        weight = high[...].astype(F32) + low[...].astype(F32)
        total = jnp.sum(g, axis=0, keepdims=True)
        small[0] += jnp.sum(dots * weight, axis=1, keepdims=True)
        small[1] += jnp.sum(total * weight, axis=1, keepdims=True)

    kv_dot = dot3((xt_hi[...], xt_lo[...]), split(gkv))
    kv_grad = grad_of(kv_dot, gkv)
    place_in_blocks(one, two, None, (kv_grad[:, 384:], out_grad[...]))
    sent = send(where, 0, (b0, b1, b2, b3), two, sems.at[1])
    q_dot = dot3((xt_hi[:, TOK:], xt_lo[:, TOK:]), split(gq))
    place_in_blocks(one, two, (grad_of(q_dot, gq), kv_grad[:, :384]), None)
    sent += send(where, 1, (a0, a1, a2, a3), one, sems.at[0], 384)
    wait(kept[2:])
    add_small(kv_dot, gkv, kv_hi, kv_lo)
    add_small(q_dot, gq, q_hi, q_lo)
    small = jnp.concatenate(small + [jnp.zeros((768, 126), F32)], axis=1).T
    smalls = (small[0:1], small[1:2], small_two[2:3, :], small_two[3:4, :])
    lines = place_lines(
        where, smalls, bias[0:1, :], features, offsets, feature_columns, offset_columns
    )
    for k, part in enumerate((a0, a1, a2, a3)):
        line = lines[16 * k : 16 * k + 16]
        place = one.at[at_hops(where, 1, k), pl.ds(384, 8)]
        place[...] = jnp.concatenate([line[:8], line[8:], jnp.zeros((8, 128), F32)], axis=1)
        sent.append(pltpu.make_async_copy(place, part.at[pl.ds(384, 8)], line_sems.at[k]))
        sent[-1].start()
    wait(sent)


def attn_last_kernel(
    where, gq_ref, gkv_ref, f0, f1, f2, f3, own, other, halo_own, halo_other,
    q_hi, q_lo, kv_hi, kv_lo, back_ref, sems, out_sems,
):
    kept = fetch((f2, f3, f0, f1), (kv_hi, kv_lo, q_hi, q_lo), sems)
    gq, gkv = split(gq_ref[...]), split(gkv_ref[...])
    wait(kept)
    back_ref[...] = dot3(gkv, (kv_hi[...], kv_lo[...]), NT)
    back_ref[TOK:] += dot3(gq, (q_hi[...], q_lo[...]), NT)
    core, half = where[3], TOK // 2
    places = [(TOK * (1 + c), TOK) for c in (core, 1 - core)] + [
        (half * c, half) for c in (core, 1 - core)
    ]
    places = [back_ref.at[pl.ds(pl.multiple_of(at, half), n)] for at, n in places]
    wait(fetch(places, (own, other, halo_own, halo_other), out_sems))


def tokens_kernel(
    where, tokens, gmid, back, back_other, halo_low, halo_high, vec_ref, middle, out, out_other,
    out_ref, output_ref,
):
    output_ref[...] = middle[...] + (out[...] + out_other[...])
    back = back[...] + back_other[...]
    halo = jnp.concatenate([halo_low[...], halo_high[...]], axis=0)
    back = back + jnp.where(where[3] == 0, 0.0, halo)
    xhat, scale = normal_parts(tokens[...])
    out_ref[...] = gmid[...] + normal_back(back, xhat, scale, vec_ref[0:1, :])


def shaped(*shape, dtype=F32):
    return jax.ShapeDtypeStruct(shape, dtype)


def kept_near(*shape, dtype=F32):
    return pltpu.VMEM(shape, dtype)


def kept_far(*shape, dtype=F32):
    return pltpu.HBM(shape, dtype)


def near(array):
    return pltpu.with_memory_space_constraint(array, pltpu.VMEM)


def far(array):
    return pltpu.with_memory_space_constraint(array, pltpu.HBM)


def call(kernel, out_shape, args, specs, scratch=(), flops=0, moved=0, vmem=24, **more):
    return pl.pallas_call(
        kernel,
        out_shape=out_shape,
        in_specs=specs,
        scratch_shapes=list(scratch),
        compiler_params=pltpu.CompilerParams(vmem_limit_bytes=vmem * 1024 * 1024),
        cost_estimate=pl.CostEstimate(flops=flops, bytes_accessed=moved, transcendentals=0),
        **more,
    )(*args)


def glue(kernel, shapes, args, axis=None, given=near, gives=kept_near):
    if axis is not None:
        kernel = functools.partial(kernel, axis)
    return call(
        kernel,
        tuple((gives[i] if isinstance(gives, tuple) else gives)(*s) for i, s in enumerate(shapes)),
        (args[0], *map(given, args[1:])),
        [SM] + [VM] * (len(args) - 1),
        vmem=10,
    )


def after(arrays, *others):
    return lax.optimization_barrier((arrays, others))[0]


def phase(*arrays):
    return lax.optimization_barrier(arrays)


def shards(
    inputs, query_weight, key_weight, value_weight, out_weight, up_weight, down_weight,
    gain_one, offset_one, gain_two, offset_two, pos_bias, prefix_len, cotangent,
):
    x, y, core = lax.axis_index("x"), lax.axis_index("y"), lax.axis_index("core")
    zh, zl = lax.axis_index("zh"), lax.axis_index("zl")
    z = zh * 2 + zl
    where = jnp.stack([x, y, z, core]).astype(jnp.int32)
    first_core = core == 0
    dma = lambda *shape: pltpu.SemaphoreType.DMA(shape)
    places = (pltpu.VMEM((4, 384, 384), F32),) * 2 + (dma(2, 4),)
    pair16 = lambda *shape: (kept_near(*shape, dtype=BF16),) * 2
    grad_blocks = (kept_far(384, 384),) * 8
    tables = place_tables()

    with jax.named_scope("pack"):
        near_down = both_ways(down_weight, "x")
        vectors = [a[None] for a in (gain_one, offset_one, gain_two, offset_two, pos_bias)]
        kept, sent = glue(
            pack_one_kernel,
            ((48, 384),) * 2,
            (where, query_weight, key_weight, value_weight, up_weight, *vectors),
            given=far,
        )
        tokens, cot, near_down, sent = phase(inputs[0], cotangent[0], near_down, sent)
        got, far_down = swap_cores(sent), hop(near_down[0], "x")
        (block,) = glue(
            pack_two_kernel,
            ((104, 384),),
            (where, near(kept), near(got), far(out_weight)),
            given=lambda array: array,
        )
    with jax.named_scope("gather_z"):
        block, tokens, cot = phase(block, tokens, cot)
        seq = (x * 2 + zh) * 2 + core
        positions = seq * TOK + jnp.arange(TOK, dtype=jnp.int32)
        cot = cot * (positions >= prefix_len[0]).astype(F32)[:, None]
        block, cot, far_down = phase(gather_at_once(block, "z"), cot, far_down)
        one, two = glue(
            stack_one_kernel,
            ((4, HALF_ONE, 384), (4, HALF_TWO, 384)),
            (where, *block),
            given=lambda array: array,
            gives=shaped,
        )

    with jax.named_scope("gather_mid"):
        one, two, cot, tokens, far_down = phase(one, two, cot, tokens, far_down)
        (down,) = glue(
            stack_down_kernel,
            ((4, 24, 768),),
            (where, down_weight, *near_down, far_down),
            given=lambda array: array,
            gives=kept_far,
        )
        down = lax.all_gather(down, "y", axis=0)
        near_one, near_two = phase(both_ways(one, "x"), both_ways(two, "y"))
        cot_other, others = swap_cores(after(cot, near_one)), swap_cores(after(tokens, near_one))
        halo = along_row(after(tokens, near_one), 1, (1,), (0,))
        far_one, far_two, cot_other, others, halo = phase(
            hop(near_one[0], "x"), hop(near_two[0], "y"), cot_other, others, halo
        )
        down = lax.all_gather(after(down, far_one), RING["z"], axis=0)
        attn_one, up_one, attn_two, up_two = glue(
            stack_both_kernel,
            ((392, 384), (384, 384), (384, 384), (384, 384)),
            (where, one, *near_one, far_one, two, *near_two, far_two),
            given=lambda array: array,
            gives=kept_far,
        )

    with jax.named_scope("gather_attn"):
        attn_one, attn_two, up_one, up_two = phase(attn_one, attn_two, up_one, up_two)
        near_one, near_two = phase(both_ways(attn_one, "y"), both_ways(attn_two, "x"))
        halo = after(halo, near_one)
        far_one, far_two = hop(near_one[0], "y"), hop(near_two[0], "x")
        halo = jnp.where(first_core, halo, swap_cores(halo))
        xhat, *xt = call(
            norm_kernel,
            (kept_near(768, 768),) + (kept_far(768, 768, dtype=BF16),) * 2,
            (where, *map(far, (halo, tokens, others))),
            [SM] + [HB] * 3,
            [pltpu.VMEM((768, 768), F32)] + [pltpu.VMEM((768, 768), BF16)] * 2 + [dma(5)],
            vmem=16,
            out_specs=(VM, HB, HB),
        )
        far_one, far_two, xhat, xt = phase(far_one, far_two, xhat, xt)
        attn_one = (attn_one, *near_one, far_one)
        attn_two = (attn_two, *near_two, far_two)
        valid = jnp.where(x * 2 + zh > 0, 1.0, 0.0).astype(F32).reshape(1)

    with jax.named_scope("attn"):
        attn_one, attn_two, up_one, up_two = phase(attn_one, attn_two, up_one, up_two)
        near_one, near_two = both_ways(up_one, "y"), both_ways(up_two, "x")
        part, vec, base, *held = call(
            attn_kernel,
            (kept_far(512, 768), shaped(8, 768), shaped(8, 512)) + tuple(kept_far(*h, dtype=t) for h, t in ATTN_HELD),
            (where, near(xhat), valid, *tables[:2], *map(far, attn_one + attn_two)),
            [SM, VM, SM, VM, VM] + [HB] * 8,
            [pltpu.VMEM(h, t) for h, t in ATTN_HELD]
            + [pltpu.VMEM((512, 768), F32), *places[:2], pltpu.VMEM((4, 8, 384), F32), places[2]]
            + [dma(11), dma(2), dma(4)],
            flops=5_700_000_000,
            moved=1_000_000,
            vmem=36,
            out_specs=(HB, VM, VM) + (HB,) * 11,
        )
        near_one, near_two, part, held = phase(near_one, near_two, part, held)

    with jax.named_scope("ffn_early"):
        part_other = swap_cores(part)
        far_one, far_two = hop(near_one[0], "y"), hop(near_two[0], "x")
        gh = call(
            ffn_early_kernel,
            kept_near(512, 1536),
            (where, *map(far, (down, cot, cot_other))),
            [SM] + [HB] * 3,
            [pltpu.VMEM((4, 4, 4, 24, 768), F32)]
            + [pltpu.VMEM((1536, 768), BF16)] * 2
            + [pltpu.VMEM((512, 768), F32), dma(2), dma(4)],
            flops=3_600_000_000,
            moved=1_000_000,
            vmem=20,
        )
        down_full = down
        part_other, far_one, far_two, gh = phase(part_other, far_one, far_two, gh)
        up_all = (up_one, *near_one, far_one, up_two, *near_two, far_two)

    with jax.named_scope("ffn"):
        middle, middle_own, *ffn_held, back_part = call(
            ffn_kernel,
            (kept_far(512, 768), kept_far(256, 768))
            + pair16(768, 512)
            + pair16(512, 1536) * 2
            + (kept_far(512, 768),),
            (where, *map(far, (tokens, others, part)), part_other, vec, near(gh))
            + (*map(far, up_all[:3]), up_all[3], *map(far, up_all[4:7]), up_all[7]),
            [SM] + [HB] * 3 + [VM] * 3 + ([HB] * 3 + [ANY]) * 2,
            (pltpu.VMEM((512, 768), F32),) * 4
            + places[:2]
            + (pltpu.VMEM((768, 1536), BF16),) * 2
            + (places[2], dma(4), dma(4)),
            flops=7_200_000_000,
            moved=1_000_000,
            vmem=30,
            out_specs=(HB, HB) + (VM,) * 6 + (HB,),
        )
        back_other = swap_cores(back_part)
        down_grads, *up_grads = call(
            ffn_late_kernel,
            (kept_far(4, 4, 4, 24, 768),) + grad_blocks,
            (where, far(cot), far(cot_other), *map(near, ffn_held)),
            [SM] + [HB] * 2 + [VM] * 6,
            places
            + (pltpu.VMEM((512, 768), F32), pltpu.VMEM((4, 4, 4, 24, 768), F32), dma(2), dma(32)),
            flops=7_300_000_000,
            moved=1_000_000,
            vmem=24,
            out_specs=(HB,) * 9,
        )
        back_other, up_grads, down_grads = phase(back_other, up_grads, down_grads)

    with jax.named_scope("attn_back"):
        up_one, up_two = up_grads[:4], up_grads[4:]
        came = scatter_start(up_one, "y"), scatter_start(up_two, "x")
        q_w, kv_w, o_w, saved = held[:2], held[2:4], held[4:6], held[6:]
        gmid, gq, gkv, out_grad, small_two, bias = call(
            attn_back_kernel,
            (kept_far(256, 768), kept_near(512, 384), kept_near(768, 768), kept_near(384, 768))
            + (shaped(8, 768), shaped(8, 512)),
            (where, vec, base)
            + (far(middle), far(back_part), back_other)
            + tuple(map(far, (cot, cot_other, *o_w, *saved))),
            [SM] + [VM] * 2 + [HB] * 2 + [VM] + [HB] * 9,
            [pltpu.VMEM((512, 768), F32)] * 4
            + [pltpu.VMEM(h, t) for h, t in ATTN_HELD[4:]]
            + [dma(15), dma(1)],
            flops=5_000_000_000,
            moved=1_000_000,
            vmem=32,
            out_specs=(HB,) + (VM,) * 5,
        )
        down = lax.psum_scatter(down_grads, RING["z"], scatter_dimension=0, tiled=True)[0]
        came, gq, gkv, out_grad = phase(came, gq, gkv, out_grad)

    with jax.named_scope("attn_grads"):
        gq, gkv, out_grad = map(near, (gq, gkv, out_grad))
        up_one_came, up_two_came = scatter_end(where, up_one, up_two, came, "yx")
        attn_grads = call(
            attn_grads_kernel,
            (kept_far(392, 384),) * 4 + (kept_far(384, 384),) * 4,
            (where, vec, gq, gkv, out_grad, small_two, bias, *tables)
            + tuple(map(far, (*q_w, *kv_w, *xt))),
            [SM] + [VM] * 10 + [HB] * 6,
            [pltpu.VMEM((4, 392, 384), F32), *places[1:]]
            + [pltpu.VMEM(h, t) for h, t in ATTN_HELD[:4]]
            + [pltpu.VMEM((768, 768), BF16)] * 2
            + [dma(6), dma(4)],
            flops=3_600_000_000,
            moved=1_000_000,
            vmem=32,
            out_specs=(HB,) * 8,
        )
        up_one_came, up_two_came, attn_grads = phase(up_one_came, up_two_came, attn_grads)

    with jax.named_scope("attn_last"):
        attn_one, attn_two = attn_grads[:4], attn_grads[4:]
        came = scatter_start(attn_one, "y"), scatter_start(attn_two, "x")
        back_own, back_other, halo_own, halo_other = call(
            attn_last_kernel,
            (kept_far(256, 768),) * 2 + (kept_far(128, 768),) * 2,
            (where, gq, gkv, *map(far, (*q_w, *kv_w))),
            [SM] + [VM] * 2 + [HB] * 4,
            [pltpu.VMEM(h, t) for h, t in ATTN_HELD[:4]]
            + [pltpu.VMEM((768, 768), F32), dma(4), dma(4)],
            flops=3_600_000_000,
            moved=1_000_000,
            vmem=20,
            out_specs=(HB,) * 4,
        )
        halo_other = swap_cores(halo_other)
        came, back_own, back_other, halo_own, halo_other, down = phase(
            came, back_own, back_other, halo_own, halo_other, down
        )
        down = lax.psum_scatter(down, "y", scatter_dimension=0, tiled=True)[0]

    with jax.named_scope("scatter_attn"):
        attn_one_came, attn_two_came = scatter_end(where, attn_one, attn_two, came, "yx")
        out_own, out_other = call(
            out_kernel,
            (kept_far(256, 768),) * 2,
            (where, *map(far, (*ffn_held[2:4], down_full))),
            [SM] + [HB] * 3,
            [pltpu.VMEM((512, 1536), BF16)] * 2
            + [pltpu.VMEM((4, 4, 4, 24, 768), F32)]
            + [pltpu.VMEM((1536, 768), BF16)] * 2
            + [pltpu.VMEM((512, 768), F32), dma(2), dma(4), dma(2)],
            flops=3_600_000_000,
            moved=1_000_000,
            vmem=24,
            out_specs=(HB,) * 2,
        )
        back_other = swap_cores(back_other)
        halo_high = along_row(halo_own + halo_other, -1, (0, 1), (0, 1))
        attn_one_came, attn_two_came, out_own, out_other, halo_high, back_other = phase(
            attn_one_came, attn_two_came, out_own, out_other, halo_high, back_other
        )

    def attn_tail(own, came):
        return far(own), far(came[0]), came[1]

    def up_tail(own, came):
        return far(own), far(came[0]), far(came[1])

    now_and_later = (kept_far,) * 2 + (shaped,) * 2

    as_is = lambda array: array

    with jax.named_scope("scatter_mid"):
        one = glue(
            part_one_kernel,
            ((4, HALF_ONE, 384),) * 4,
            (where, *attn_tail(attn_one[0], attn_one_came), *up_tail(up_one[0], up_one_came)),
            0,
            given=as_is,
            gives=now_and_later,
        )
        two = glue(
            part_one_kernel,
            ((4, HALF_TWO, 384),) * 4,
            (where, *attn_tail(attn_two[0], attn_two_came), *up_tail(up_two[0], up_two_came)),
            1,
            given=as_is,
            gives=now_and_later,
        )
        came = scatter_start(one, "x"), scatter_start(two, "y")
        out_other = swap_cores(out_other)
        came, one, two, down, out_other = phase(came, one, two, down, out_other)

        one_came, two_came = scatter_end(where, one, two, came, "xy")
        down = glue(part_down_kernel, ((24, 768),) * 4, (where, down), 0, given=far)
        down_came = scatter_start(down, "x")
        one_came, two_came, down_came, down = phase(one_came, two_came, down_came, down)

    with jax.named_scope("scatter_z"):
        block = glue(
            part_two_kernel,
            ((104, 384),) * 4,
            (where, *attn_tail(one[0], one_came), *attn_tail(two[0], two_came)),
            given=as_is,
            gives=shaped,
        )
        (next_down,) = glue(add_one_kernel, ((24, 768),), (where, down[1], down_came[0]))
        block, next_down = phase(block, next_down)
        block = scatter_at_once(block, "z")
        next_down = hop(next_down, "x")
        halo_low = swap_cores(halo_high)
        gmid = after(gmid, next_down)
        input_grad, output = glue(
            tokens_kernel,
            ((256, 768),) * 2,
            (where, inputs[0], gmid, back_own, back_other, halo_low, halo_high, vec)
            + (middle_own, out_own, out_other),
            given=as_is,
            gives=shaped,
        )
        down = down[0] + down_came[1] + next_down
        block, down, input_grad, output = phase(block, down, input_grad, output)

    with jax.named_scope("finish"):
        out_grad, kept, sent = glue(
            sum_three_kernel,
            ((6, 768), (48, 384), (48, 384)),
            (where, *block),
            given=as_is,
            gives=(shaped,) * 3,
        )
        got = swap_cores(sent)
        *qkv, up_out = glue(
            finish_kernel,
            ((6, 768),) * 3 + ((6, 3072),) + ((1, 6),) * 4 + ((1, 2),),
            (where, kept, got),
            gives=shaped,
        )
        qkv, up_out, vectors = qkv[:3], qkv[3], [v[0] for v in (*qkv[4:], up_out)]

    return (
        output[None], input_grad[None], *qkv, out_grad, up_out, down,
        *vectors,
    )


def solution(mesh):
    fine = Mesh(mesh.devices.reshape(4, 2, 2, 4, 2), AXES)
    tokens = P(("y", "zl"), ("x", "zh", "core"), None)
    matrix = P(AXES, None)
    vector = P(AXES)
    return jax.shard_map(
        shards,
        mesh=fine,
        in_specs=(tokens,) + (matrix,) * 6 + (vector,) * 5 + (P(("y", "zl")), tokens),
        out_specs=(tokens, tokens) + (matrix,) * 6 + (vector,) * 5,
        check_vma=False,
    )
```

```python
import functools

import jax
import jax.numpy as jnp
import numpy as np
from jax import lax
from jax.experimental import pallas as pl
from jax.experimental.pallas import tpu as pltpu
from jax.sharding import Mesh
from jax.sharding import PartitionSpec as P

EPSILON = 1e-05
AXES = ("x", "zh", "core", "y", "zl")
RING = {"x": "x", "y": "y", "z": ("zh", "zl")}
F32, BF16 = jnp.float32, jnp.bfloat16
TOK = 256
NT = (((1,), (1,)), ((), ()))
NN = (((1,), (0,)), ((), ()))
ANY = pl.BlockSpec(memory_space=pl.ANY)
HB = pl.BlockSpec(memory_space=pltpu.HBM)
VM = pl.BlockSpec(memory_space=pltpu.VMEM)
SM = pl.BlockSpec(memory_space=pltpu.SMEM)


def shift(array, axis, by):
    return lax.ppermute(array, RING[axis], [(i, (i + by) % 4) for i in range(4)])


def swap_cores(array):
    return lax.ppermute(array, "core", [(0, 1), (1, 0)])


def index_of(x, zh, core, y, zl):
    return (((x * 2 + zh) * 2 + core) * 4 + y) * 2 + zl


def along_row(array, by, from_core, to_core):
    pairs = []
    for chip in range(8):
        if 0 <= chip + by < 8:
            for y in range(4):
                for zl in range(2):
                    for a, b in zip(from_core, to_core):
                        pairs.append(
                            (
                                index_of(chip // 2, chip % 2, a, y, zl),
                                index_of((chip + by) // 2, (chip + by) % 2, b, y, zl),
                            )
                        )
    return lax.ppermute(array, AXES, pairs)


def hop(array, axis, by=1):
    pairs = []
    for at in np.ndindex(4, 4, 2, 4):
        to = dict(zip("xzcy", at))
        to[axis] = (to[axis] + by * (1 - 2 * to["c"])) % 4
        pairs.append(
            tuple(index_of(p[0], p[1] // 2, p[2], p[3], p[1] % 2) for p in (at, tuple(to.values())))
        )
    return lax.ppermute(array, AXES, pairs)


FROM = (0, 3, 1, 2)


def both_ways(block, axis):
    return hop(block, axis), hop(block, axis, -1)


def scatter_start(parts, axis):
    return hop(parts[2], axis), hop(parts[3], axis, -1)


def add_kernel(where, a0, a1, b0, b1, a_sum, b_sum):
    a_sum[...] = a0[...] + a1[...]
    b_sum[...] = b0[...] + b1[...]


def scatter_end(where, one, two, came, axes, parts=None):
    shapes = (one[1].shape, two[1].shape)
    parts = parts or far
    args = (where, parts(one[1]), came[0][0], parts(two[1]), came[1][0])
    sums = glue(add_kernel, shapes, args, given=lambda array: array, gives=shaped)
    return [(c[1], hop(a, axis)) for c, a, axis in zip(came, sums, axes)]


def gather_at_once(block, axis):
    return [block] + [shift(block, axis, -k) for k in (1, 2, 3)]


def scatter_at_once(parts, axis):
    return [parts[0]] + [shift(parts[k], axis, k) for k in (1, 2, 3)]


def split(value):
    high = value.astype(BF16)
    return high, (value - high.astype(F32)).astype(BF16)


def dot3(left, right, dims=NN):
    def one(a, b):
        return lax.dot_general(a, b, dims, preferred_element_type=F32)

    return one(left[0], right[0]) + one(left[0], right[1]) + one(left[1], right[0])


def normal_parts(values):
    centred = values - jnp.mean(values, axis=-1, keepdims=True)
    spread = jnp.mean(centred * centred, axis=-1, keepdims=True)
    scale = lax.rsqrt(spread + EPSILON)
    return centred * scale, scale


def normal_back(grad, xhat, scale, gain):
    e = grad * gain
    return scale * (
        e
        - jnp.mean(e, axis=-1, keepdims=True)
        - xhat * jnp.mean(e * xhat, axis=-1, keepdims=True)
    )


def normal_cdf(v):
    density = jnp.exp(-0.5 * v * v)
    d = 1.0 + np.float32(0.3275911 * np.sqrt(0.5)) * jnp.abs(v)
    t = pl.reciprocal(d, approx=True)
    t = t * (2.0 - d * t)
    t = t * (2.0 - d * t)
    total = np.float32(0.5 * 1.061405429)
    for c in (-1.453152027, 1.421413741, -0.284496736, 0.254829592):
        total = total * t + np.float32(0.5 * c)
    total = total * t * density
    return jnp.where(v < 0.0, total, 1.0 - total), density * np.float32(1.0 / np.sqrt(2.0 * np.pi))


HALF_ONE, HALF_TWO = 56, 48


def halved(array, c, run):
    count = array.shape[1] // (2 * run)
    return jnp.concatenate(
        [array[:, (2 * i + c) * run : (2 * i + c + 1) * run] for i in range(count)], axis=1
    )


def joined(first, second, run):
    count = first.shape[1] // run
    return jnp.concatenate(
        [h[:, i * run : (i + 1) * run] for i in range(count) for h in (first, second)], axis=1
    )


def pack_one_kernel(where, q, k, v, up, g_one, o_one, g_two, o_two, bias, kept, sent):
    vec = [ref[...] for ref in (g_one, o_one, g_two, o_two, bias)]
    vec = jnp.concatenate(vec + [jnp.zeros((1, 384 - 26), F32)], axis=1)
    both = []
    for c in range(2):
        wide = halved(up[...], c, 192)
        both.append(
            jnp.concatenate(
                [halved(w[...], c, 48) for w in (q, k, v)]
                + [wide[:, 384 * i : 384 * i + 384] for i in range(4)]
                + [jnp.broadcast_to(vec, (6, 384))],
                axis=0,
            )
        )
    first = where[3] == 0
    kept[...] = jnp.where(first, both[0], both[1])
    sent[...] = jnp.where(first, both[1], both[0])


def pack_two_kernel(where, kept, got, out, block):
    first = where[3] == 0
    one = jnp.where(first, kept[...], got[...])
    two = jnp.where(first, got[...], kept[...])

    def rows(i):
        return [one[6 * i : 6 * i + 6], two[6 * i : 6 * i + 6]]

    line = one[42:43, :128] + pltpu.roll(two[42:43, :128], 64, 1)
    block[0:24] = jnp.concatenate(rows(0) + rows(1), axis=0)
    block[24:32] = jnp.concatenate([jnp.broadcast_to(line, (8, 128)), jnp.zeros((8, 256), F32)], axis=1)
    block[32:56] = jnp.concatenate(rows(3) + rows(4), axis=0)
    block[56:80] = jnp.concatenate(rows(2) + [out[:, :384], out[:, 384:]], axis=0)
    block[80:104] = jnp.concatenate(rows(5) + rows(6), axis=0)


def stack_one_kernel(where, p0, p1, p2, p3, one, two):
    for off, ref in enumerate((p0, p1, p2, p3)):
        at = lax.rem(where[2] + off, 4)
        one[at] = ref[:HALF_ONE]
        two[at] = ref[HALF_ONE:]


def at_hops(where, axis, hops):
    return lax.rem(where[axis] + 4 + hops * (1 - 2 * where[3]), 4)


def stack_down_kernel(where, p0, p1, p2, p3, out):
    for hops, ref in zip(FROM, (p0, p1, p2, p3)):
        out[at_hops(where, 0, hops)] = ref[...]


def stack_two_kernel(axis, where, p0, p1, p2, p3, attn, up):
    skip = 8 if axis == 0 else 0
    row = lax.broadcasted_iota(jnp.int32, (8, 128), 0)
    vec = [jnp.zeros((8, 128), F32)] * 3
    for hops, ref in zip(FROM, (p0, p1, p2, p3)):
        at = at_hops(where, axis, hops)
        for z in range(4):
            rows = pl.ds(pl.multiple_of(at * 96 + 24 * z, 8), 24)
            attn[rows] = ref[z, 0:24]
            up[rows] = ref[z, 24 + skip : 48 + skip]
            if skip:
                line = ref[z, 24:32, :128]
                vec[z % 2] = jnp.where(row == at * 2 + z // 2, line, vec[z % 2])
    if skip:
        attn[384:392] = jnp.concatenate(vec, axis=1)


def stack_both_kernel(where, *refs):
    stack_two_kernel(0, where, *refs[:4], *refs[8:10])
    stack_two_kernel(1, where, *refs[4:8], *refs[10:])


def feature_places():
    x, zh, c, y, zl, r = np.indices((4, 2, 2, 4, 2, 6)).reshape(6, -1)
    return [a.astype(np.int32) for a in (y, zl * 8 + x * 2 + zh, x * 4 + zh * 2 + zl, c * 64 + r)]


def offset_places():
    x, zh, c, y, zl, r = np.indices((4, 2, 2, 4, 2, 2)).reshape(6, -1)
    places = []
    for a in (y, zl * 8 + x * 2 + zh, x * 4 + zh * 2 + zl, c * 64 + 24 + r):
        line = np.full((512,), -1000, np.int32)
        line[1:257] = a[::-1]
        places.append(line)
    return places


def place_tables():
    rows = [np.pad(np.stack(t), ((0, 4), (0, 0))) for t in (feature_places(), offset_places())]
    return rows + [np.ascontiguousarray(np.pad(r.T, ((0, 0), (0, 120)))) for r in rows]


def three_parts(value):
    high, rest = split(value)
    rest = value - high.astype(F32)
    return (high, *split(rest))


def pick_dot(left, right):
    return sum(jnp.dot(a, b, preferred_element_type=F32) for a in left for b in right)


def spread_vectors(where, pieces, features, offsets):
    lines = []
    for k in (0, 2, 3, 1):
        last = pieces[k][:, :256]
        lines += [last[:, :128], last[:, 128:]]
    lines = three_parts(jnp.concatenate(lines, axis=0).T)

    def spread(table):
        hops = jnp.bitwise_and((table[0:1, :] + 4 - where[1]) * (1 - 2 * where[3]), 3)
        place = hops * 16 + table[1:2, :]
        chips = lax.broadcasted_iota(jnp.int32, (64, table.shape[1]), 0) == place
        return pick_dot(lines, (chips.astype(F32).astype(BF16),))

    values = spread(features)
    lane = lax.broadcasted_iota(jnp.int32, values.shape, 0)
    picked = [
        jnp.sum(jnp.where(lane == features[3:4, :] + 6 * i, values, 0.0), axis=0, keepdims=True)
        for i in range(4)
    ]
    values = spread(offsets)
    lane = lax.broadcasted_iota(jnp.int32, values.shape, 0)
    base = jnp.sum(jnp.where(lane == offsets[3:4, :], values, 0.0), axis=0, keepdims=True)
    base = jnp.where(offsets[3:4, :] >= 0, jnp.exp(base), 0.0)
    return picked, base


def place_lines(where, smalls, bias, features, offsets, feature_columns, offset_columns):
    def gathered(values, table, columns, lane):
        hops = jnp.bitwise_and((table[0:1, :] + 4 - where[1]) * (1 - 2 * where[3]), 3)
        place = hops * 16 + table[1:2, :]
        chips = lax.broadcasted_iota(jnp.int32, (64, table.shape[1]), 0) == place
        lanes = lax.broadcasted_iota(jnp.int32, (table.shape[1], 128), 1) == columns[:, 3:4] + lane
        return pick_dot(
            three_parts(jnp.where(chips, values, 0.0)), (lanes.astype(F32).astype(BF16),)
        )

    total = gathered(bias, offsets[...], offset_columns[...], 0)
    for i, small in enumerate(smalls):
        total += gathered(small, features[...], feature_columns[...], 6 * i)
    return total


def ring_copies(where, axis, places, parts, whole, sems, rows=384):
    return [
        (p.at[pl.ds(0, rows)], whole.at[at_hops(where, axis, hops), pl.ds(0, rows)], sems.at[i])
        for i, (hops, p) in enumerate(zip(places, parts))
    ]


def bring(where, ones, twos, one, two, sems):
    copies = ring_copies(where, 1, FROM, ones, one, sems.at[0])
    copies += ring_copies(where, 0, FROM, twos, two, sems.at[1])
    copies = [pltpu.make_async_copy(*c) for c in copies]
    for copy in copies:
        copy.start()
    return copies


def send(where, axis, parts, whole, sems, rows=384):
    copies = ring_copies(where, axis, range(4), parts, whole, sems, rows)
    copies = [pltpu.make_async_copy(place, part, sem) for part, place, sem in copies]
    for copy in copies:
        copy.start()
    return copies


def by_group(one, two, group):
    x, zh = group // 2, lax.rem(group, 2)
    held = ([], [])
    for y in range(4):
        for zl in range(2):
            z = zh * 2 + zl
            held[0].append(one[y, pl.ds(pl.multiple_of((x * 4 + z) * 24, 8), 24)])
            held[1].append(two[x, pl.ds(pl.multiple_of((y * 4 + z) * 24, 8), 24)])
    return held


def unpack_attn(one, two, q_hi, q_lo, kv_hi, kv_lo, o_hi, o_lo):
    def step(group, carry):
        held = by_group(one, two, group)

        def rows(part, first):
            return jnp.concatenate([h[first : first + 6] for h in held[part]], axis=0)

        for c in range(2):
            at = pl.ds(pl.multiple_of(group * 96 + c * 48, 16), 48)
            q_hi[at, :], q_lo[at, :] = split(rows(0, 6 * c))
            kv_hi[at, :384], kv_lo[at, :384] = split(rows(0, 12 + 6 * c))
            kv_hi[at, 384:], kv_lo[at, 384:] = split(rows(1, 6 * c))
            at = pl.ds(pl.multiple_of(group * 48, 16), 48)
            lanes = pl.ds(384 * c, 384)
            o_hi[at, lanes], o_lo[at, lanes] = split(rows(1, 12 + 6 * c))
        return carry

    lax.fori_loop(0, 8, step, 0)


def unpack_up(one, two, up_hi, up_lo):
    def step(group, carry):
        held = by_group(one, two, group)
        for c in range(2):
            at = pl.ds(pl.multiple_of(group * 96 + c * 48, 16), 48)
            for part in range(2):
                for b in range(2):
                    first = 12 * b + 6 * c
                    rows = jnp.concatenate([h[first : first + 6] for h in held[part]], axis=0)
                    lanes = pl.ds(768 * part + 384 * b, 384)
                    up_hi[at, lanes], up_lo[at, lanes] = split(rows)
        return carry

    lax.fori_loop(0, 8, step, 0)


def place_in_blocks(one, two, first, second):
    for group in range(8):
        x, zh = group // 2, group % 2
        for y in range(4):
            for zl in range(2):
                z, j = zh * 2 + zl, y * 2 + zl

                def rows(array):
                    at = [group * 96 + 48 * c + 6 * j for c in range(2)]
                    return [array[a : a + 6] for a in at]

                if first is not None:
                    one[y, (x * 4 + z) * 24 : (x * 4 + z) * 24 + 24] = jnp.concatenate(
                        rows(first[0]) + rows(first[1]), axis=0
                    )
                if second is not None:
                    ends = second[1]
                    if ends.shape[0] == 768:
                        ends = rows(ends)
                    else:
                        ends = ends[group * 48 + 6 * j : group * 48 + 6 * j + 6]
                        ends = [ends[:, :384], ends[:, 384:]]
                    two[x, (y * 4 + z) * 24 : (y * 4 + z) * 24 + 24] = jnp.concatenate(
                        rows(second[0]) + ends, axis=0
                    )


def sum_kernel(where, a0, a1, b0, b1, b2, a_sum, b_sum):
    a_sum[...] = a0[...] + a1[...]
    b_sum[...] = b0[...] + b1[...] + b2[...]


def part_one_kernel(axis, where, a0, a1, b0, *more):
    skip = 8 if axis == 0 else 0
    if skip:
        lines = a0[384:392, :256] + a1[384:392, :256]
        row = lax.broadcasted_iota(jnp.int32, (8, 128), 0)
    for hops, out in enumerate(more[-4:]):
        at = at_hops(where, axis, hops)
        for z in range(4):
            rows = pl.ds(pl.multiple_of(at * 96 + 24 * z, 8), 24)
            out[z, 0:24] = a0[rows] + a1[rows]
            if skip:
                line = lines[:, 128 * (z % 2) : 128 * (z % 2) + 128]
                line = jnp.sum(jnp.where(row == at * 2 + z // 2, line, 0.0), axis=0, keepdims=True)
                out[z, 24:32] = jnp.concatenate(
                    [jnp.broadcast_to(line, (8, 128)), jnp.zeros((8, 256), F32)], axis=1
                )
            out[z, 24 + skip : 48 + skip] = b0[rows]


def part_down_kernel(axis, where, down, *outs):
    for hops, out in enumerate(outs):
        out[...] = down[at_hops(where, axis, hops)]


def add_one_kernel(where, a0, a1, total):
    total[...] = a0[...] + a1[...]


def part_two_kernel(where, a0, a1, a2, b0, b1, b2, o0, o1, o2, o3):
    for k, out in enumerate((o0, o1, o2, o3)):
        z = lax.rem(where[2] + k, 4)
        out[:HALF_ONE] = a0[z] + a1[z] + a2[z]
        out[HALF_ONE:] = b0[z] + b1[z] + b2[z]


def sum_three_kernel(where, a0, a1, a2, a3, out, kept, sent):
    block = (a0[...] + a1[...]) + (a2[...] + a3[...])
    out[...] = jnp.concatenate([block[68:74], block[74:80]], axis=1)
    line = block[24:25, :128]
    both = []
    for c in range(2):
        rows = [block[at + 6 * c : at + 6 * c + 6] for at in (0, 12, 56, 32, 44, 80, 92)]
        vec = line if c == 0 else pltpu.roll(line, 64, 1)
        vec = jnp.concatenate([jnp.broadcast_to(vec, (6, 128)), jnp.zeros((6, 256), F32)], axis=1)
        both.append(jnp.concatenate(rows + [vec], axis=0))
    first = where[3] == 0
    kept[...] = jnp.where(first, both[0], both[1])
    sent[...] = jnp.where(first, both[1], both[0])


def finish_kernel(where, kept, got, q, k, v, up, *vectors):
    first = where[3] == 0
    one = jnp.where(first, kept[...], got[...])
    two = jnp.where(first, got[...], kept[...])
    for i, ref in enumerate((q, k, v)):
        ref[...] = joined(one[6 * i : 6 * i + 6], two[6 * i : 6 * i + 6], 48)
    wide = [
        jnp.concatenate([h[18 + 6 * i : 24 + 6 * i] for i in range(4)], axis=1) for h in (one, two)
    ]
    up[...] = joined(wide[0], wide[1], 192)
    line = one[42:43, :128] + two[42:43, :128]
    for i, ref in enumerate(vectors):
        ref[...] = line[:, 6 * i : 6 * i + ref.shape[1]]


def toeplitz(base):
    return pltpu.roll(jnp.broadcast_to(base, (TOK, 2 * TOK)), 0, 1, stride=1, stride_axis=0)


def fetch_pair(where, mine, other, held, first, sems):
    core = where[3]
    return fetch(
        (mine, other),
        [held.at[pl.ds(pl.multiple_of(first + c * TOK, TOK), TOK)] for c in (core, 1 - core)],
        sems,
    )


def fetch(refs, held, sems):
    copies = [pltpu.make_async_copy(r, h, sems.at[i]) for i, (r, h) in enumerate(zip(refs, held))]
    for copy in copies:
        copy.start()
    return copies


def wait(copies):
    for copy in copies:
        copy.wait()


ATTN_HELD = (
    (((768, 384), BF16),) * 2
    + (((768, 768), BF16),) * 2
    + (((384, 768), BF16),) * 2
    + (((512, 384), F32),) * 3
    + (((768, 384), F32),) * 2
)


def norm_kernel(where, halo, tokens, others, xhat_ref, xt_hi_far, xt_lo_far, x_ref, xt_hi, xt_lo, sems):
    fetched = fetch((halo,), (x_ref.at[pl.ds(0, TOK)],), sems)
    fetched += fetch_pair(where, tokens, others, x_ref, TOK, sems.at[pl.ds(1, 2)])
    wait(fetched)
    xhat, _ = normal_parts(x_ref[...])
    xhat_ref[...] = xhat
    xt_hi[...], xt_lo[...] = split(xhat.T)
    wait(fetch((xt_hi, xt_lo), (xt_hi_far, xt_lo_far), sems.at[pl.ds(3, 2)]))


def attn_kernel(
    where, xhat_ref, valid_ref, features, offsets, a0, a1, a2, a3, b0, b1, b2, b3,
    part_far, vec_ref, base_ref, *more,
):
    outs, held = more[:11], more[11:22]
    part_ref, one, two, lines, sems, out_sems, half_sems, line_sems = more[22:]
    q_hi, q_lo, kv_hi, kv_lo, o_hi, o_lo, sig_ref, ratio_ref, inv_ref, w_ref, v_ref = held

    def keep(first, count):
        at = slice(first, first + count)
        return fetch(held[at], outs[at], out_sems.at[pl.ds(first, count)])

    fetched = fetch(
        [a.at[pl.ds(384, 8)] for a in (a0, a1, a2, a3)], [lines.at[k] for k in range(4)], line_sems
    )
    copies = bring(where, (a0, a1, a2, a3), (b0, b1, b2, b3), one, two, sems)
    wait(fetched)
    picked, base = spread_vectors(where, [lines[k] for k in range(4)], features[...], offsets[...])
    vec_ref[...] = jnp.concatenate(picked + [jnp.zeros((4, 768), F32)], axis=0)
    base_ref[...] = jnp.broadcast_to(base, (8, 512))
    wait(copies)
    unpack_attn(one, two, q_hi, q_lo, kv_hi, kv_lo, o_hi, o_lo)
    kept = keep(0, 6)
    gain, offset = picked[:2]
    parts = split(xhat_ref[...] * gain + offset)
    own = tuple(p[TOK:] for p in parts)
    keys = dot3(parts, (kv_hi[...], kv_lo[...]))
    sig_ref[...] = jax.nn.sigmoid(dot3(own, (q_hi[...], q_lo[...])))
    w = jnp.exp(keys[:, :384])
    w_ref[:TOK] = w[:TOK] * valid_ref[0]
    w_ref[TOK:] = w[TOK:]
    v_ref[...] = keys[:, 384:]
    kept += keep(6, 1) + keep(9, 2)
    w = w_ref[...]
    sums = split(jnp.concatenate([w * v_ref[...], w], axis=1))
    band = split(toeplitz(base))
    for i in range(2):
        at, half = slice(TOK * i, TOK * i + TOK), pl.ds(TOK * i, TOK)
        seen = tuple(s[TOK * i : TOK * i + 2 * TOK] for s in sums)
        mixed = dot3(band, seen)
        inverse = 1.0 / mixed[:, 384:]
        inv_ref[at] = inverse
        ratio_ref[at] = mixed[:, :384] * inverse
        for j in (7, 8):
            kept += fetch((held[j].at[half],), (outs[j].at[half],), half_sems.at[i, pl.ds(j - 7, 1)])
        mixed = split(sig_ref[at] * ratio_ref[at])
        part_ref[at] = dot3(mixed, (o_hi[...], o_lo[...]))
        kept += fetch((part_ref.at[half],), (part_far.at[half],), half_sems.at[i, pl.ds(2, 1)])
    wait(kept)


def fetch_down(down_far, down, sems):
    return fetch([down_far.at[z] for z in range(4)], [down.at[z] for z in range(4)], sems)


def unpack_down(fetched, down, down_hi, down_lo):
    for zh in range(2):
        wait(fetched[2 * zh : 2 * zh + 2])
        for x in range(4):
            for y in range(4):
                rows = jnp.concatenate([down[2 * zh + zl, y, x] for zl in range(2)], axis=0)
                at = pl.ds(((x * 2 + zh) * 4 + y) * 48, 48)
                down_hi[at, :], down_lo[at, :] = split(rows)


def ffn_early_kernel(
    where, down_far, mine, other, gh_ref, down, down_hi, down_lo, cot_ref, cot_sems, in_sems
):
    kept = fetch_down(down_far, down, in_sems)
    fetched = fetch_pair(where, mine, other, cot_ref, 0, cot_sems)
    unpack_down(kept, down, down_hi, down_lo)
    wait(fetched)
    cot = split(cot_ref[...])
    for i in range(2):
        at = slice(768 * i, 768 * i + 768)
        gh_ref[:, at] = dot3(cot, (down_hi[at], down_lo[at]), NT)


def ffn_kernel(
    where, tokens, others, mine_far, theirs_ref, vec_ref, gh_ref, a0, a1, a2, a3, b0, b1, b2, b3,
    middle_far, middle_own, nt_hi, nt_lo, h_hi, h_lo, g_hi, g_lo, back_far,
    middle_ref, back_ref, x_ref, mine_ref, one, two, up_hi, up_lo, sems, in_sems, out_sems,
):
    fetched = fetch((mine_far,), (mine_ref,), in_sems)
    fetched += fetch_pair(where, tokens, others, x_ref, 0, in_sems.at[pl.ds(2, 2)])
    wait(bring(where, (a0, a1, a2, a3), (b0, b1, b2, b3), one, two, sems))
    unpack_up(one, two, up_hi, up_lo)
    wait(fetched)
    middle_ref[...] = x_ref[...] + (mine_ref[...] + theirs_ref[...])
    own = pl.ds(pl.multiple_of(where[3] * TOK, TOK), TOK)
    sent = fetch((middle_ref, middle_ref.at[own]), (middle_far, middle_own), out_sems)
    xhat, _ = normal_parts(middle_ref[...])
    normed = xhat * vec_ref[2:3, :] + vec_ref[3:4, :]
    parts = split(normed)
    nt_hi[...], nt_lo[...] = split(normed.T)
    halves = [pl.ds(TOK * c, TOK) for c in range(2)]
    for c, rows in enumerate((slice(0, TOK), slice(TOK, 2 * TOK))):
        for i in range(6):
            at = slice(256 * i, 256 * i + 256)
            preact = dot3(tuple(p[rows] for p in parts), (up_hi[:, at], up_lo[:, at]))
            lower, density = normal_cdf(preact)
            slope = lower + preact * density
            h_hi[rows, at], h_lo[rows, at] = split(preact * lower)
            g_hi[rows, at], g_lo[rows, at] = split(gh_ref[rows, at] * slope)
        back_ref[rows] = dot3((g_hi[rows], g_lo[rows]), (up_hi[...], up_lo[...]), NT)
        sent += fetch((back_ref.at[halves[c]],), (back_far.at[halves[c]],), out_sems.at[pl.ds(2 + c, 1)])
    wait(sent)


def ffn_late_kernel(
    where, cot_mine, cot_other, nt_hi, nt_lo, h_hi, h_lo, g_hi, g_lo,
    down_grad_far, a0, a1, a2, a3, b0, b1, b2, b3, one, two, sems, cot_ref, down_grad,
    in_sems, out_sems,
):
    fetched = fetch_pair(where, cot_mine, cot_other, cot_ref, 0, in_sems)
    nt = (nt_hi[...], nt_lo[...])
    sent = []
    wait(fetched)
    cot = split(cot_ref[...])
    for i in range(2):
        at = slice(768 * i, 768 * i + 768)
        rows = dot3((h_hi[:, at].T, h_lo[:, at].T), cot)
        for chip in range(32):
            x, zh, y, zl = (2 * i + chip // 16), chip // 8 % 2, chip // 2 % 4, chip % 2
            down_grad[2 * zh + zl, y, x] = rows[chip * 24 : chip * 24 + 24]
        for place in range(16):
            part = (place // 4, place % 4, pl.ds(2 * i, 2))
            sem = out_sems.at[i * 16 + place]
            sent.append(pltpu.make_async_copy(down_grad.at[part], down_grad_far.at[part], sem))
            sent[-1].start()
    for i in range(2):
        at = slice(768 * i, 768 * i + 768)
        grad = dot3(nt, (g_hi[:, at], g_lo[:, at]))
        pair = (grad[:, :384], grad[:, 384:])
        place_in_blocks(one, two, *((pair, None) if i == 0 else (None, pair)))
        sent += send(where, 1 - i, ((a0, a1, a2, a3), (b0, b1, b2, b3))[i], (one, two)[i], sems.at[i])
    wait(sent)


def out_kernel(
    where, h_hi_far, h_lo_far, down_far, own, other,
    h_hi, h_lo, down, down_hi, down_lo, out_ref, sems, in_sems, out_sems,
):
    kept = fetch_down(down_far, down, in_sems)
    fetched = fetch((h_hi_far, h_lo_far), (h_hi, h_lo), sems)
    unpack_down(kept, down, down_hi, down_lo)
    wait(fetched)
    for i in range(2):
        at = slice(768 * i, 768 * i + 768)
        out = dot3((h_hi[:, at], h_lo[:, at]), (down_hi[at], down_lo[at]))
        if i == 0:
            out_ref[...] = out
        else:
            out_ref[...] += out
    places = [pl.ds(pl.multiple_of(TOK * c, TOK), TOK) for c in (where[3], 1 - where[3])]
    wait(fetch([out_ref.at[p] for p in places], (own, other), out_sems))


def attn_back_kernel(
    where, vec_ref, base_ref, middle_far, mine_far, theirs_ref, cot_mine, cot_other,
    f0, f1, f2, f3, f4, f5, f6, gmid_own, gq_ref, gkv_ref, out_grad, small_ref, bias_ref,
    middle_ref, mine_ref, cot_ref, gmid_ref,
    o_hi, o_lo, sig_ref, ratio_ref, inv_ref, w_ref, v_ref, sems, out_sems,
):
    halves = [pl.ds(TOK * c, TOK) for c in range(2)]
    first = [
        fetch([far.at[p] for p in halves], [ref.at[p] for p in halves], sems.at[pl.ds(9 + 2 * i, 2)])
        for i, (far, ref) in enumerate(((middle_far, middle_ref), (mine_far, mine_ref)))
    ]
    copies = fetch_pair(where, cot_mine, cot_other, cot_ref, 0, sems)
    copies += fetch((f0, f1), (o_hi, o_lo), sems.at[pl.ds(2, 2)])
    wait(first[0])
    xhat, scale = normal_parts(middle_ref[...])
    wait(first[1])
    kept = fetch(
        (f2, f3, f4, f5, f6), (sig_ref, ratio_ref, inv_ref, w_ref, v_ref), sems.at[pl.ds(4, 5)]
    )
    mine = mine_ref[...]
    small_ref[2:3, :] = jnp.sum(mine * xhat, axis=0, keepdims=True)
    small_ref[3:4, :] = jnp.sum(mine, axis=0, keepdims=True)
    gmid = normal_back(mine + theirs_ref[...], xhat, scale, vec_ref[2:3, :])
    wait(copies)
    gmid = cot_ref[...] + gmid
    gmid_ref[...] = gmid
    gmid = split(gmid)
    own = pl.ds(pl.multiple_of(where[3] * TOK, TOK), TOK)
    sent = fetch((gmid_ref.at[own],), (gmid_own,), out_sems)
    gmixed = dot3(gmid, (o_hi[...], o_lo[...]), NT)
    wait(kept)
    sig, ratio = sig_ref[...], ratio_ref[...]
    out_grad[...] = dot3(split((sig * ratio).T), gmid)
    gq = gmixed * ratio * sig * (1.0 - sig)
    gq_ref[...] = gq
    gnum = gmixed * sig * inv_ref[...]
    gsums = split(jnp.concatenate([gnum, -gnum * ratio], axis=1))
    band = toeplitz(base_ref[0:1, :])
    band_t = split(band.T)
    w, v = w_ref[...], v_ref[...]
    sums = split(jnp.concatenate([w * v, w], axis=1))
    spread, gband = [], None
    for i in range(2):
        here = tuple(g[TOK * i : TOK * i + TOK] for g in gsums)
        seen = tuple(s[TOK * i : TOK * i + 2 * TOK] for s in sums)
        spread.append(dot3(band_t, here))
        term = dot3(here, seen, NT)
        gband = term if gband is None else gband + term
    count = TOK
    while count > 1:
        count //= 2
        gband = gband[:count] + pltpu.roll(gband[count:], 2 * TOK - count, 1)
    bias_ref[...] = jnp.broadcast_to(gband * base_ref[0:1, :], (8, 2 * TOK))
    gseen = jnp.concatenate(
        [spread[0][:TOK], spread[0][TOK:] + spread[1][:TOK], spread[1][TOK:]], axis=0
    )
    gkv = jnp.concatenate([w * (gseen[:, :384] * v + gseen[:, 384:]), gseen[:, :384] * w], axis=1)
    gkv_ref[...] = gkv
    wait(sent)


def attn_grads_kernel(
    where, vec_ref, gq_ref, gkv_ref, out_grad, small_two, bias, features, offsets, feature_columns,
    offset_columns, f0, f1, f2, f3, f4, f5, a0, a1, a2, a3, b0, b1, b2, b3,
    one, two, sems, q_hi, q_lo, kv_hi, kv_lo, xt_hi, xt_lo, in_sems, line_sems,
):
    kept = fetch((f4, f5, f0, f1, f2, f3), (xt_hi, xt_lo, q_hi, q_lo, kv_hi, kv_lo), in_sems)
    gq, gkv = gq_ref[...], gkv_ref[...]
    vec = vec_ref[...].T
    wait(kept[:2])
    small = [0.0, 0.0]

    def grad_of(dots, g):
        total = jnp.sum(g, axis=0, keepdims=True)
        return vec[:, 0:1] * dots + vec[:, 1:2] * total

    def add_small(dots, g, high, low):
        weight = high[...].astype(F32) + low[...].astype(F32)
        total = jnp.sum(g, axis=0, keepdims=True)
        small[0] += jnp.sum(dots * weight, axis=1, keepdims=True)
        small[1] += jnp.sum(total * weight, axis=1, keepdims=True)

    kv_dot = dot3((xt_hi[...], xt_lo[...]), split(gkv))
    kv_grad = grad_of(kv_dot, gkv)
    place_in_blocks(one, two, None, (kv_grad[:, 384:], out_grad[...]))
    sent = send(where, 0, (b0, b1, b2, b3), two, sems.at[1])
    q_dot = dot3((xt_hi[:, TOK:], xt_lo[:, TOK:]), split(gq))
    place_in_blocks(one, two, (grad_of(q_dot, gq), kv_grad[:, :384]), None)
    sent += send(where, 1, (a0, a1, a2, a3), one, sems.at[0], 384)
    wait(kept[2:])
    add_small(kv_dot, gkv, kv_hi, kv_lo)
    add_small(q_dot, gq, q_hi, q_lo)
    small = jnp.concatenate(small + [jnp.zeros((768, 126), F32)], axis=1).T
    smalls = (small[0:1], small[1:2], small_two[2:3, :], small_two[3:4, :])
    lines = place_lines(
        where, smalls, bias[0:1, :], features, offsets, feature_columns, offset_columns
    )
    for k, part in enumerate((a0, a1, a2, a3)):
        line = lines[16 * k : 16 * k + 16]
        place = one.at[at_hops(where, 1, k), pl.ds(384, 8)]
        place[...] = jnp.concatenate([line[:8], line[8:], jnp.zeros((8, 128), F32)], axis=1)
        sent.append(pltpu.make_async_copy(place, part.at[pl.ds(384, 8)], line_sems.at[k]))
        sent[-1].start()
    wait(sent)


def attn_last_kernel(
    where, gq_ref, gkv_ref, f0, f1, f2, f3, own, other, halo_own, halo_other,
    q_hi, q_lo, kv_hi, kv_lo, back_ref, sems, out_sems,
):
    kept = fetch((f2, f3, f0, f1), (kv_hi, kv_lo, q_hi, q_lo), sems)
    gq, gkv = split(gq_ref[...]), split(gkv_ref[...])
    wait(kept)
    back_ref[...] = dot3(gkv, (kv_hi[...], kv_lo[...]), NT)
    back_ref[TOK:] += dot3(gq, (q_hi[...], q_lo[...]), NT)
    core, half = where[3], TOK // 2
    places = [(TOK * (1 + c), TOK) for c in (core, 1 - core)] + [
        (half * c, half) for c in (core, 1 - core)
    ]
    places = [back_ref.at[pl.ds(pl.multiple_of(at, half), n)] for at, n in places]
    wait(fetch(places, (own, other, halo_own, halo_other), out_sems))


def tokens_kernel(
    where, tokens, gmid, back, back_other, halo_low, halo_high, vec_ref, middle, out, out_other,
    out_ref, output_ref,
):
    output_ref[...] = middle[...] + (out[...] + out_other[...])
    back = back[...] + back_other[...]
    halo = jnp.concatenate([halo_low[...], halo_high[...]], axis=0)
    back = back + jnp.where(where[3] == 0, 0.0, halo)
    xhat, scale = normal_parts(tokens[...])
    out_ref[...] = gmid[...] + normal_back(back, xhat, scale, vec_ref[0:1, :])


def shaped(*shape, dtype=F32):
    return jax.ShapeDtypeStruct(shape, dtype)


def kept_near(*shape, dtype=F32):
    return pltpu.VMEM(shape, dtype)


def kept_far(*shape, dtype=F32):
    return pltpu.HBM(shape, dtype)


def near(array):
    return pltpu.with_memory_space_constraint(array, pltpu.VMEM)


def far(array):
    return pltpu.with_memory_space_constraint(array, pltpu.HBM)


def call(kernel, out_shape, args, specs, scratch=(), flops=0, moved=0, vmem=24, **more):
    return pl.pallas_call(
        kernel,
        out_shape=out_shape,
        in_specs=specs,
        scratch_shapes=list(scratch),
        compiler_params=pltpu.CompilerParams(vmem_limit_bytes=vmem * 1024 * 1024),
        cost_estimate=pl.CostEstimate(flops=flops, bytes_accessed=moved, transcendentals=0),
        **more,
    )(*args)


def glue(kernel, shapes, args, axis=None, given=near, gives=kept_near):
    if axis is not None:
        kernel = functools.partial(kernel, axis)
    return call(
        kernel,
        tuple((gives[i] if isinstance(gives, tuple) else gives)(*s) for i, s in enumerate(shapes)),
        (args[0], *map(given, args[1:])),
        [SM] + [VM] * (len(args) - 1),
        vmem=10,
    )


def after(arrays, *others):
    return lax.optimization_barrier((arrays, others))[0]


def phase(*arrays):
    return lax.optimization_barrier(arrays)


def shards(
    inputs, query_weight, key_weight, value_weight, out_weight, up_weight, down_weight,
    gain_one, offset_one, gain_two, offset_two, pos_bias, prefix_len, cotangent,
):
    x, y, core = lax.axis_index("x"), lax.axis_index("y"), lax.axis_index("core")
    zh, zl = lax.axis_index("zh"), lax.axis_index("zl")
    z = zh * 2 + zl
    where = jnp.stack([x, y, z, core]).astype(jnp.int32)
    first_core = core == 0
    dma = lambda *shape: pltpu.SemaphoreType.DMA(shape)
    places = (pltpu.VMEM((4, 384, 384), F32),) * 2 + (dma(2, 4),)
    pair16 = lambda *shape: (kept_near(*shape, dtype=BF16),) * 2
    grad_blocks = (kept_far(384, 384),) * 8
    tables = place_tables()

    with jax.named_scope("pack"):
        near_down = both_ways(down_weight, "x")
        vectors = [a[None] for a in (gain_one, offset_one, gain_two, offset_two, pos_bias)]
        kept, sent = glue(
            pack_one_kernel,
            ((48, 384),) * 2,
            (where, query_weight, key_weight, value_weight, up_weight, *vectors),
            given=far,
        )
        tokens, cot, near_down, sent = phase(inputs[0], cotangent[0], near_down, sent)
        got, far_down = swap_cores(sent), hop(near_down[0], "x")
        (block,) = glue(
            pack_two_kernel,
            ((104, 384),),
            (where, near(kept), near(got), far(out_weight)),
            given=lambda array: array,
        )
    with jax.named_scope("gather_z"):
        block, tokens, cot = phase(block, tokens, cot)
        seq = (x * 2 + zh) * 2 + core
        positions = seq * TOK + jnp.arange(TOK, dtype=jnp.int32)
        cot = cot * (positions >= prefix_len[0]).astype(F32)[:, None]
        block, cot, far_down = phase(gather_at_once(block, "z"), cot, far_down)
        one, two = glue(
            stack_one_kernel,
            ((4, HALF_ONE, 384), (4, HALF_TWO, 384)),
            (where, *block),
            given=lambda array: array,
            gives=shaped,
        )

    with jax.named_scope("gather_mid"):
        one, two, cot, tokens, far_down = phase(one, two, cot, tokens, far_down)
        (down,) = glue(
            stack_down_kernel,
            ((4, 24, 768),),
            (where, down_weight, *near_down, far_down),
            given=lambda array: array,
            gives=kept_far,
        )
        down = lax.all_gather(down, "y", axis=0)
        others = swap_cores(tokens)
        near_one, near_two, others = phase(both_ways(one, "x"), both_ways(two, "y"), others)
        halo = along_row(after(tokens, near_one), 1, (1,), (0,))
        far_one, far_two, halo = phase(hop(near_one[0], "x"), hop(near_two[0], "y"), halo)
        down = lax.all_gather(after(down, far_one), RING["z"], axis=0)
        attn_one, up_one, attn_two, up_two = glue(
            stack_both_kernel,
            ((392, 384), (384, 384), (384, 384), (384, 384)),
            (where, one, *near_one, far_one, two, *near_two, far_two),
            given=lambda array: array,
            gives=kept_far,
        )

    with jax.named_scope("gather_attn"):
        attn_one, attn_two, up_one, up_two = phase(attn_one, attn_two, up_one, up_two)
        near_one, near_two = phase(both_ways(attn_one, "y"), both_ways(attn_two, "x"))
        halo, cot = after((halo, cot), near_one)
        far_one, far_two = hop(near_one[0], "y"), hop(near_two[0], "x")
        cot_other = swap_cores(cot)
        halo = jnp.where(first_core, halo, swap_cores(halo))
        xhat, *xt = call(
            norm_kernel,
            (kept_near(768, 768),) + (kept_far(768, 768, dtype=BF16),) * 2,
            (where, *map(far, (halo, tokens, others))),
            [SM] + [HB] * 3,
            [pltpu.VMEM((768, 768), F32)] + [pltpu.VMEM((768, 768), BF16)] * 2 + [dma(5)],
            vmem=16,
            out_specs=(VM, HB, HB),
        )
        far_one, far_two, xhat, xt, cot_other = phase(far_one, far_two, xhat, xt, cot_other)
        attn_one = (attn_one, *near_one, far_one)
        attn_two = (attn_two, *near_two, far_two)
        valid = jnp.where(x * 2 + zh > 0, 1.0, 0.0).astype(F32).reshape(1)

    with jax.named_scope("attn"):
        attn_one, attn_two, up_one, up_two = phase(attn_one, attn_two, up_one, up_two)
        near_one, near_two = both_ways(up_one, "y"), both_ways(up_two, "x")
        part, vec, base, *held = call(
            attn_kernel,
            (kept_far(512, 768), shaped(8, 768), shaped(8, 512)) + tuple(kept_far(*h, dtype=t) for h, t in ATTN_HELD),
            (where, near(xhat), valid, *tables[:2], *map(far, attn_one + attn_two)),
            [SM, VM, SM, VM, VM] + [HB] * 8,
            [pltpu.VMEM(h, t) for h, t in ATTN_HELD]
            + [pltpu.VMEM((512, 768), F32), *places[:2], pltpu.VMEM((4, 8, 384), F32), places[2]]
            + [dma(11), dma(2, 3), dma(4)],
            flops=5_700_000_000,
            moved=1_000_000,
            vmem=36,
            out_specs=(HB, VM, VM) + (HB,) * 11,
        )
        near_one, near_two, part, held = phase(near_one, near_two, part, held)

    with jax.named_scope("ffn_early"):
        part_other = swap_cores(part)
        far_one, far_two = hop(near_one[0], "y"), hop(near_two[0], "x")
        gh = call(
            ffn_early_kernel,
            kept_near(512, 1536),
            (where, *map(far, (down, cot, cot_other))),
            [SM] + [HB] * 3,
            [pltpu.VMEM((4, 4, 4, 24, 768), F32)]
            + [pltpu.VMEM((1536, 768), BF16)] * 2
            + [pltpu.VMEM((512, 768), F32), dma(2), dma(4)],
            flops=3_600_000_000,
            moved=1_000_000,
            vmem=20,
        )
        down_full = down
        part_other, far_one, far_two, gh = phase(part_other, far_one, far_two, gh)
        up_all = (up_one, *near_one, far_one, up_two, *near_two, far_two)

    with jax.named_scope("ffn"):
        middle, middle_own, *ffn_held, back_part = call(
            ffn_kernel,
            (kept_far(512, 768), kept_far(256, 768))
            + pair16(768, 512)
            + pair16(512, 1536) * 2
            + (kept_far(512, 768),),
            (where, *map(far, (tokens, others, part)), part_other, vec, near(gh))
            + (*map(far, up_all[:3]), up_all[3], *map(far, up_all[4:7]), up_all[7]),
            [SM] + [HB] * 3 + [VM] * 3 + ([HB] * 3 + [ANY]) * 2,
            (pltpu.VMEM((512, 768), F32),) * 4
            + places[:2]
            + (pltpu.VMEM((768, 1536), BF16),) * 2
            + (places[2], dma(4), dma(4)),
            flops=7_200_000_000,
            moved=1_000_000,
            vmem=30,
            out_specs=(HB, HB) + (VM,) * 6 + (HB,),
        )
        back_other = swap_cores(back_part)
        down_grads, *up_grads = call(
            ffn_late_kernel,
            (kept_far(4, 4, 4, 24, 768),) + grad_blocks,
            (where, far(cot), far(cot_other), *map(near, ffn_held)),
            [SM] + [HB] * 2 + [VM] * 6,
            places
            + (pltpu.VMEM((512, 768), F32), pltpu.VMEM((4, 4, 4, 24, 768), F32), dma(2), dma(32)),
            flops=7_300_000_000,
            moved=1_000_000,
            vmem=24,
            out_specs=(HB,) * 9,
        )
        back_other, up_grads, down_grads = phase(back_other, up_grads, down_grads)

    with jax.named_scope("attn_back"):
        up_one, up_two = up_grads[:4], up_grads[4:]
        came = scatter_start(up_one, "y"), scatter_start(up_two, "x")
        q_w, kv_w, o_w, saved = held[:2], held[2:4], held[4:6], held[6:]
        gmid, gq, gkv, out_grad, small_two, bias = call(
            attn_back_kernel,
            (kept_far(256, 768), kept_near(512, 384), kept_near(768, 768), kept_near(384, 768))
            + (shaped(8, 768), shaped(8, 512)),
            (where, vec, base)
            + (far(middle), far(back_part), back_other)
            + tuple(map(far, (cot, cot_other, *o_w, *saved))),
            [SM] + [VM] * 2 + [HB] * 2 + [VM] + [HB] * 9,
            [pltpu.VMEM((512, 768), F32)] * 4
            + [pltpu.VMEM(h, t) for h, t in ATTN_HELD[4:]]
            + [dma(15), dma(1)],
            flops=5_000_000_000,
            moved=1_000_000,
            vmem=32,
            out_specs=(HB,) + (VM,) * 5,
        )
        down = lax.psum_scatter(down_grads, RING["z"], scatter_dimension=0, tiled=True)[0]
        came, gq, gkv, out_grad = phase(came, gq, gkv, out_grad)

    with jax.named_scope("attn_grads"):
        gq, gkv, out_grad = map(near, (gq, gkv, out_grad))
        up_one_came, up_two_came = scatter_end(where, up_one, up_two, came, "yx")
        attn_grads = call(
            attn_grads_kernel,
            (kept_far(392, 384),) * 4 + (kept_far(384, 384),) * 4,
            (where, vec, gq, gkv, out_grad, small_two, bias, *tables)
            + tuple(map(far, (*q_w, *kv_w, *xt))),
            [SM] + [VM] * 10 + [HB] * 6,
            [pltpu.VMEM((4, 392, 384), F32), *places[1:]]
            + [pltpu.VMEM(h, t) for h, t in ATTN_HELD[:4]]
            + [pltpu.VMEM((768, 768), BF16)] * 2
            + [dma(6), dma(4)],
            flops=3_600_000_000,
            moved=1_000_000,
            vmem=32,
            out_specs=(HB,) * 8,
        )
        up_one_came, up_two_came, attn_grads = phase(up_one_came, up_two_came, attn_grads)

    with jax.named_scope("attn_last"):
        attn_one, attn_two = attn_grads[:4], attn_grads[4:]
        came = scatter_start(attn_one, "y"), scatter_start(attn_two, "x")
        back_own, back_other, halo_own, halo_other = call(
            attn_last_kernel,
            (kept_far(256, 768),) * 2 + (kept_far(128, 768),) * 2,
            (where, gq, gkv, *map(far, (*q_w, *kv_w))),
            [SM] + [VM] * 2 + [HB] * 4,
            [pltpu.VMEM(h, t) for h, t in ATTN_HELD[:4]]
            + [pltpu.VMEM((768, 768), F32), dma(4), dma(4)],
            flops=3_600_000_000,
            moved=1_000_000,
            vmem=20,
            out_specs=(HB,) * 4,
        )
        halo_other = swap_cores(halo_other)
        came, back_own, back_other, halo_own, halo_other, down = phase(
            came, back_own, back_other, halo_own, halo_other, down
        )
        down = lax.psum_scatter(down, "y", scatter_dimension=0, tiled=True)[0]

    with jax.named_scope("scatter_attn"):
        attn_one_came, attn_two_came = scatter_end(where, attn_one, attn_two, came, "yx")
        out_own, out_other = call(
            out_kernel,
            (kept_far(256, 768),) * 2,
            (where, *map(far, (*ffn_held[2:4], down_full))),
            [SM] + [HB] * 3,
            [pltpu.VMEM((512, 1536), BF16)] * 2
            + [pltpu.VMEM((4, 4, 4, 24, 768), F32)]
            + [pltpu.VMEM((1536, 768), BF16)] * 2
            + [pltpu.VMEM((512, 768), F32), dma(2), dma(4), dma(2)],
            flops=3_600_000_000,
            moved=1_000_000,
            vmem=24,
            out_specs=(HB,) * 2,
        )
        back_other = swap_cores(back_other)
        halo_high = along_row(halo_own + halo_other, -1, (0, 1), (0, 1))
        sums = [
            glue(
                sum_kernel,
                (attn[0].shape, up[0].shape),
                (where, attn[0], attn_came[0], up[0], *up_came),
                given=far,
                gives=kept_far,
            )
            for attn, attn_came, up, up_came in (
                (attn_one, attn_one_came, up_one, up_one_came),
                (attn_two, attn_two_came, up_two, up_two_came),
            )
        ]
        attn_one_came, attn_two_came, out_own, out_other, halo_high, back_other, sums = phase(
            attn_one_came, attn_two_came, out_own, out_other, halo_high, back_other, sums
        )

    def attn_tail(own, came):
        return far(own), far(came[0]), came[1]

    now_and_later = (kept_far,) * 2 + (shaped,) * 2

    as_is = lambda array: array

    with jax.named_scope("scatter_mid"):
        one = glue(
            part_one_kernel,
            ((4, HALF_ONE, 384),) * 4,
            (where, far(sums[0][0]), attn_one_came[1], far(sums[0][1])),
            0,
            given=as_is,
            gives=now_and_later,
        )
        two = glue(
            part_one_kernel,
            ((4, HALF_TWO, 384),) * 4,
            (where, far(sums[1][0]), attn_two_came[1], far(sums[1][1])),
            1,
            given=as_is,
            gives=now_and_later,
        )
        came = scatter_start(one, "x"), scatter_start(two, "y")
        out_other = swap_cores(out_other)
        came, one, two, down, out_other = phase(came, one, two, down, out_other)

        one_came, two_came = scatter_end(where, one, two, came, "xy")
        down = glue(part_down_kernel, ((24, 768),) * 4, (where, down), 0, given=far)
        down_came = scatter_start(down, "x")
        one_came, two_came, down_came, down = phase(one_came, two_came, down_came, down)

    with jax.named_scope("scatter_z"):
        block = glue(
            part_two_kernel,
            ((104, 384),) * 4,
            (where, *attn_tail(one[0], one_came), *attn_tail(two[0], two_came)),
            given=as_is,
            gives=shaped,
        )
        (next_down,) = glue(add_one_kernel, ((24, 768),), (where, down[1], down_came[0]))
        block, next_down = phase(block, next_down)
        block = scatter_at_once(block, "z")
        next_down = hop(next_down, "x")
        halo_low = swap_cores(halo_high)
        gmid = after(gmid, next_down)
        input_grad, output = glue(
            tokens_kernel,
            ((256, 768),) * 2,
            (where, inputs[0], gmid, back_own, back_other, halo_low, halo_high, vec)
            + (middle_own, out_own, out_other),
            given=as_is,
            gives=shaped,
        )
        down = down[0] + down_came[1] + next_down
        block, down, input_grad, output = phase(block, down, input_grad, output)

    with jax.named_scope("finish"):
        out_grad, kept, sent = glue(
            sum_three_kernel,
            ((6, 768), (48, 384), (48, 384)),
            (where, *block),
            given=as_is,
            gives=(shaped,) * 3,
        )
        got = swap_cores(sent)
        *qkv, up_out = glue(
            finish_kernel,
            ((6, 768),) * 3 + ((6, 3072),) + ((1, 6),) * 4 + ((1, 2),),
            (where, kept, got),
            gives=shaped,
        )
        qkv, up_out, vectors = qkv[:3], qkv[3], [v[0] for v in (*qkv[4:], up_out)]

    return (
        output[None], input_grad[None], *qkv, out_grad, up_out, down,
        *vectors,
    )


def solution(mesh):
    fine = Mesh(mesh.devices.reshape(4, 2, 2, 4, 2), AXES)
    tokens = P(("y", "zl"), ("x", "zh", "core"), None)
    matrix = P(AXES, None)
    vector = P(AXES)
    return jax.shard_map(
        shards,
        mesh=fine,
        in_specs=(tokens,) + (matrix,) * 6 + (vector,) * 5 + (P(("y", "zl")), tokens),
        out_specs=(tokens, tokens) + (matrix,) * 6 + (vector,) * 5,
        check_vma=False,
    )
```

```python
import functools

import jax
import jax.numpy as jnp
import numpy as np
from jax import lax
from jax.experimental import pallas as pl
from jax.experimental.pallas import tpu as pltpu
from jax.sharding import Mesh
from jax.sharding import PartitionSpec as P

EPSILON = 1e-05
AXES = ("x", "zh", "core", "y", "zl")
RING = {"x": "x", "y": "y", "z": ("zh", "zl")}
F32, BF16 = jnp.float32, jnp.bfloat16
TOK = 256
NT = (((1,), (1,)), ((), ()))
NN = (((1,), (0,)), ((), ()))
ANY = pl.BlockSpec(memory_space=pl.ANY)
HB = pl.BlockSpec(memory_space=pltpu.HBM)
VM = pl.BlockSpec(memory_space=pltpu.VMEM)
SM = pl.BlockSpec(memory_space=pltpu.SMEM)


def shift(array, axis, by):
    return lax.ppermute(array, RING[axis], [(i, (i + by) % 4) for i in range(4)])


def swap_cores(array):
    return lax.ppermute(array, "core", [(0, 1), (1, 0)])


def index_of(x, zh, core, y, zl):
    return (((x * 2 + zh) * 2 + core) * 4 + y) * 2 + zl


def along_row(array, by, from_core, to_core):
    pairs = []
    for chip in range(8):
        if 0 <= chip + by < 8:
            for y in range(4):
                for zl in range(2):
                    for a, b in zip(from_core, to_core):
                        pairs.append(
                            (
                                index_of(chip // 2, chip % 2, a, y, zl),
                                index_of((chip + by) // 2, (chip + by) % 2, b, y, zl),
                            )
                        )
    return lax.ppermute(array, AXES, pairs)


def hop(array, axis, by=1):
    pairs = []
    for at in np.ndindex(4, 4, 2, 4):
        to = dict(zip("xzcy", at))
        to[axis] = (to[axis] + by * (1 - 2 * to["c"])) % 4
        pairs.append(
            tuple(index_of(p[0], p[1] // 2, p[2], p[3], p[1] % 2) for p in (at, tuple(to.values())))
        )
    return lax.ppermute(array, AXES, pairs)


FROM = (0, 3, 1, 2)


def both_ways(block, axis):
    return hop(block, axis), hop(block, axis, -1)


def scatter_start(parts, axis):
    return hop(parts[2], axis), hop(parts[3], axis, -1)


def add_kernel(where, a0, a1, b0, b1, a_sum, b_sum):
    a_sum[...] = a0[...] + a1[...]
    b_sum[...] = b0[...] + b1[...]


def scatter_end(where, one, two, came, axes, parts=None):
    shapes = (one[1].shape, two[1].shape)
    parts = parts or far
    args = (where, parts(one[1]), came[0][0], parts(two[1]), came[1][0])
    sums = glue(add_kernel, shapes, args, given=lambda array: array, gives=shaped)
    return [(c[1], hop(a, axis)) for c, a, axis in zip(came, sums, axes)]


def gather_at_once(block, axis):
    return [block] + [shift(block, axis, -k) for k in (1, 2, 3)]


def scatter_at_once(parts, axis):
    return [parts[0]] + [shift(parts[k], axis, k) for k in (1, 2, 3)]


def split(value):
    high = value.astype(BF16)
    return high, (value - high.astype(F32)).astype(BF16)


def dot3(left, right, dims=NN):
    def one(a, b):
        return lax.dot_general(a, b, dims, preferred_element_type=F32)

    return one(left[0], right[0]) + one(left[0], right[1]) + one(left[1], right[0])


def normal_parts(values):
    centred = values - jnp.mean(values, axis=-1, keepdims=True)
    spread = jnp.mean(centred * centred, axis=-1, keepdims=True)
    scale = lax.rsqrt(spread + EPSILON)
    return centred * scale, scale


def normal_back(grad, xhat, scale, gain):
    e = grad * gain
    return scale * (
        e
        - jnp.mean(e, axis=-1, keepdims=True)
        - xhat * jnp.mean(e * xhat, axis=-1, keepdims=True)
    )


def normal_cdf(v):
    density = jnp.exp(-0.5 * v * v)
    d = 1.0 + np.float32(0.3275911 * np.sqrt(0.5)) * jnp.abs(v)
    t = pl.reciprocal(d, approx=True)
    t = t * (2.0 - d * t)
    t = t * (2.0 - d * t)
    total = np.float32(0.5 * 1.061405429)
    for c in (-1.453152027, 1.421413741, -0.284496736, 0.254829592):
        total = total * t + np.float32(0.5 * c)
    total = total * t * density
    return jnp.where(v < 0.0, total, 1.0 - total), density * np.float32(1.0 / np.sqrt(2.0 * np.pi))


HALF_ONE, HALF_TWO = 56, 48


def halved(array, c, run):
    count = array.shape[1] // (2 * run)
    return jnp.concatenate(
        [array[:, (2 * i + c) * run : (2 * i + c + 1) * run] for i in range(count)], axis=1
    )


def joined(first, second, run):
    count = first.shape[1] // run
    return jnp.concatenate(
        [h[:, i * run : (i + 1) * run] for i in range(count) for h in (first, second)], axis=1
    )


def pack_one_kernel(where, q, k, v, up, g_one, o_one, g_two, o_two, bias, kept, sent):
    vec = [ref[...] for ref in (g_one, o_one, g_two, o_two, bias)]
    vec = jnp.concatenate(vec + [jnp.zeros((1, 384 - 26), F32)], axis=1)
    both = []
    for c in range(2):
        wide = halved(up[...], c, 192)
        both.append(
            jnp.concatenate(
                [halved(w[...], c, 48) for w in (q, k, v)]
                + [wide[:, 384 * i : 384 * i + 384] for i in range(4)]
                + [jnp.broadcast_to(vec, (6, 384))],
                axis=0,
            )
        )
    first = where[3] == 0
    kept[...] = jnp.where(first, both[0], both[1])
    sent[...] = jnp.where(first, both[1], both[0])


def pack_two_kernel(where, kept, got, out, block):
    first = where[3] == 0
    one = jnp.where(first, kept[...], got[...])
    two = jnp.where(first, got[...], kept[...])

    def rows(i):
        return [one[6 * i : 6 * i + 6], two[6 * i : 6 * i + 6]]

    line = one[42:43, :128] + pltpu.roll(two[42:43, :128], 64, 1)
    block[0:24] = jnp.concatenate(rows(0) + rows(1), axis=0)
    block[24:32] = jnp.concatenate([jnp.broadcast_to(line, (8, 128)), jnp.zeros((8, 256), F32)], axis=1)
    block[32:56] = jnp.concatenate(rows(3) + rows(4), axis=0)
    block[56:80] = jnp.concatenate(rows(2) + [out[:, :384], out[:, 384:]], axis=0)
    block[80:104] = jnp.concatenate(rows(5) + rows(6), axis=0)


def stack_one_kernel(where, p0, p1, p2, p3, one, two):
    for off, ref in enumerate((p0, p1, p2, p3)):
        at = lax.rem(where[2] + off, 4)
        one[at] = ref[:HALF_ONE]
        two[at] = ref[HALF_ONE:]


def at_hops(where, axis, hops):
    return lax.rem(where[axis] + 4 + hops * (1 - 2 * where[3]), 4)


def stack_down_kernel(where, p0, p1, p2, p3, out):
    for hops, ref in zip(FROM, (p0, p1, p2, p3)):
        out[at_hops(where, 0, hops)] = ref[...]


def stack_two_kernel(axis, where, p0, p1, p2, p3, attn, up):
    skip = 8 if axis == 0 else 0
    row = lax.broadcasted_iota(jnp.int32, (8, 128), 0)
    vec = [jnp.zeros((8, 128), F32)] * 3
    for hops, ref in zip(FROM, (p0, p1, p2, p3)):
        at = at_hops(where, axis, hops)
        for z in range(4):
            rows = pl.ds(pl.multiple_of(at * 96 + 24 * z, 8), 24)
            attn[rows] = ref[z, 0:24]
            up[rows] = ref[z, 24 + skip : 48 + skip]
            if skip:
                line = ref[z, 24:32, :128]
                vec[z % 2] = jnp.where(row == at * 2 + z // 2, line, vec[z % 2])
    if skip:
        attn[384:392] = jnp.concatenate(vec, axis=1)


def stack_both_kernel(where, *refs):
    stack_two_kernel(0, where, *refs[:4], *refs[8:10])
    stack_two_kernel(1, where, *refs[4:8], *refs[10:])


def feature_places():
    x, zh, c, y, zl, r = np.indices((4, 2, 2, 4, 2, 6)).reshape(6, -1)
    return [a.astype(np.int32) for a in (y, zl * 8 + x * 2 + zh, x * 4 + zh * 2 + zl, c * 64 + r)]


def offset_places():
    x, zh, c, y, zl, r = np.indices((4, 2, 2, 4, 2, 2)).reshape(6, -1)
    places = []
    for a in (y, zl * 8 + x * 2 + zh, x * 4 + zh * 2 + zl, c * 64 + 24 + r):
        line = np.full((512,), -1000, np.int32)
        line[1:257] = a[::-1]
        places.append(line)
    return places


def place_tables():
    rows = [np.pad(np.stack(t), ((0, 4), (0, 0))) for t in (feature_places(), offset_places())]
    return rows + [np.ascontiguousarray(np.pad(r.T, ((0, 0), (0, 120)))) for r in rows]


def three_parts(value):
    high, rest = split(value)
    rest = value - high.astype(F32)
    return (high, *split(rest))


def pick_dot(left, right):
    return sum(jnp.dot(a, b, preferred_element_type=F32) for a in left for b in right)


def spread_vectors(where, pieces, features, offsets):
    lines = []
    for k in (0, 2, 3, 1):
        last = pieces[k][:, :256]
        lines += [last[:, :128], last[:, 128:]]
    lines = three_parts(jnp.concatenate(lines, axis=0).T)

    def spread(table):
        hops = jnp.bitwise_and((table[0:1, :] + 4 - where[1]) * (1 - 2 * where[3]), 3)
        place = hops * 16 + table[1:2, :]
        chips = lax.broadcasted_iota(jnp.int32, (64, table.shape[1]), 0) == place
        return pick_dot(lines, (chips.astype(F32).astype(BF16),))

    values = spread(features)
    lane = lax.broadcasted_iota(jnp.int32, values.shape, 0)
    picked = [
        jnp.sum(jnp.where(lane == features[3:4, :] + 6 * i, values, 0.0), axis=0, keepdims=True)
        for i in range(4)
    ]
    values = spread(offsets)
    lane = lax.broadcasted_iota(jnp.int32, values.shape, 0)
    base = jnp.sum(jnp.where(lane == offsets[3:4, :], values, 0.0), axis=0, keepdims=True)
    base = jnp.where(offsets[3:4, :] >= 0, jnp.exp(base), 0.0)
    return picked, base


def place_lines(where, smalls, bias, features, offsets, feature_columns, offset_columns):
    def gathered(values, table, columns, lane):
        hops = jnp.bitwise_and((table[0:1, :] + 4 - where[1]) * (1 - 2 * where[3]), 3)
        place = hops * 16 + table[1:2, :]
        chips = lax.broadcasted_iota(jnp.int32, (64, table.shape[1]), 0) == place
        lanes = lax.broadcasted_iota(jnp.int32, (table.shape[1], 128), 1) == columns[:, 3:4] + lane
        return pick_dot(
            three_parts(jnp.where(chips, values, 0.0)), (lanes.astype(F32).astype(BF16),)
        )

    total = gathered(bias, offsets[...], offset_columns[...], 0)
    for i, small in enumerate(smalls):
        total += gathered(small, features[...], feature_columns[...], 6 * i)
    return total


def ring_copies(where, axis, places, parts, whole, sems, rows=384):
    return [
        (p.at[pl.ds(0, rows)], whole.at[at_hops(where, axis, hops), pl.ds(0, rows)], sems.at[i])
        for i, (hops, p) in enumerate(zip(places, parts))
    ]


def bring(where, ones, twos, one, two, sems):
    copies = ring_copies(where, 1, FROM, ones, one, sems.at[0])
    copies += ring_copies(where, 0, FROM, twos, two, sems.at[1])
    copies = [pltpu.make_async_copy(*c) for c in copies]
    for copy in copies:
        copy.start()
    return copies


def send(where, axis, parts, whole, sems, rows=384):
    copies = ring_copies(where, axis, range(4), parts, whole, sems, rows)
    copies = [pltpu.make_async_copy(place, part, sem) for part, place, sem in copies]
    for copy in copies:
        copy.start()
    return copies


def by_group(one, two, group):
    x, zh = group // 2, lax.rem(group, 2)
    held = ([], [])
    for y in range(4):
        for zl in range(2):
            z = zh * 2 + zl
            held[0].append(one[y, pl.ds(pl.multiple_of((x * 4 + z) * 24, 8), 24)])
            held[1].append(two[x, pl.ds(pl.multiple_of((y * 4 + z) * 24, 8), 24)])
    return held


def unpack_attn(one, two, q_hi, q_lo, kv_hi, kv_lo, o_hi, o_lo):
    def step(group, carry):
        held = by_group(one, two, group)

        def rows(part, first):
            return jnp.concatenate([h[first : first + 6] for h in held[part]], axis=0)

        for c in range(2):
            at = pl.ds(pl.multiple_of(group * 96 + c * 48, 16), 48)
            q_hi[at, :], q_lo[at, :] = split(rows(0, 6 * c))
            kv_hi[at, :384], kv_lo[at, :384] = split(rows(0, 12 + 6 * c))
            kv_hi[at, 384:], kv_lo[at, 384:] = split(rows(1, 6 * c))
            at = pl.ds(pl.multiple_of(group * 48, 16), 48)
            lanes = pl.ds(384 * c, 384)
            o_hi[at, lanes], o_lo[at, lanes] = split(rows(1, 12 + 6 * c))
        return carry

    lax.fori_loop(0, 8, step, 0)


def unpack_up(one, two, up_hi, up_lo):
    def step(group, carry):
        held = by_group(one, two, group)
        for c in range(2):
            at = pl.ds(pl.multiple_of(group * 96 + c * 48, 16), 48)
            for part in range(2):
                for b in range(2):
                    first = 12 * b + 6 * c
                    rows = jnp.concatenate([h[first : first + 6] for h in held[part]], axis=0)
                    lanes = pl.ds(768 * part + 384 * b, 384)
                    up_hi[at, lanes], up_lo[at, lanes] = split(rows)
        return carry

    lax.fori_loop(0, 8, step, 0)


def place_in_blocks(one, two, first, second):
    for group in range(8):
        x, zh = group // 2, group % 2
        for y in range(4):
            for zl in range(2):
                z, j = zh * 2 + zl, y * 2 + zl

                def rows(array):
                    at = [group * 96 + 48 * c + 6 * j for c in range(2)]
                    return [array[a : a + 6] for a in at]

                if first is not None:
                    one[y, (x * 4 + z) * 24 : (x * 4 + z) * 24 + 24] = jnp.concatenate(
                        rows(first[0]) + rows(first[1]), axis=0
                    )
                if second is not None:
                    ends = second[1]
                    if ends.shape[0] == 768:
                        ends = rows(ends)
                    else:
                        ends = ends[group * 48 + 6 * j : group * 48 + 6 * j + 6]
                        ends = [ends[:, :384], ends[:, 384:]]
                    two[x, (y * 4 + z) * 24 : (y * 4 + z) * 24 + 24] = jnp.concatenate(
                        rows(second[0]) + ends, axis=0
                    )


def sum_kernel(where, a0, a1, b0, b1, b2, a_sum, b_sum):
    a_sum[...] = a0[...] + a1[...]
    b_sum[...] = b0[...] + b1[...] + b2[...]


def part_one_kernel(axis, where, a0, a1, b0, *more):
    skip = 8 if axis == 0 else 0
    if skip:
        lines = a0[384:392, :256] + a1[384:392, :256]
        row = lax.broadcasted_iota(jnp.int32, (8, 128), 0)
    for hops, out in enumerate(more[-4:]):
        at = at_hops(where, axis, hops)
        for z in range(4):
            rows = pl.ds(pl.multiple_of(at * 96 + 24 * z, 8), 24)
            out[z, 0:24] = a0[rows] + a1[rows]
            if skip:
                line = lines[:, 128 * (z % 2) : 128 * (z % 2) + 128]
                line = jnp.sum(jnp.where(row == at * 2 + z // 2, line, 0.0), axis=0, keepdims=True)
                out[z, 24:32] = jnp.concatenate(
                    [jnp.broadcast_to(line, (8, 128)), jnp.zeros((8, 256), F32)], axis=1
                )
            out[z, 24 + skip : 48 + skip] = b0[rows]


def part_down_kernel(axis, where, down, *outs):
    for hops, out in enumerate(outs):
        out[...] = down[at_hops(where, axis, hops)]


def add_one_kernel(where, a0, a1, total):
    total[...] = a0[...] + a1[...]


def part_two_kernel(where, a0, a1, a2, b0, b1, b2, o0, o1, o2, o3):
    for k, out in enumerate((o0, o1, o2, o3)):
        z = lax.rem(where[2] + k, 4)
        out[:HALF_ONE] = a0[z] + a1[z] + a2[z]
        out[HALF_ONE:] = b0[z] + b1[z] + b2[z]


def sum_three_kernel(where, a0, a1, a2, a3, out, kept, sent):
    block = (a0[...] + a1[...]) + (a2[...] + a3[...])
    out[...] = jnp.concatenate([block[68:74], block[74:80]], axis=1)
    line = block[24:25, :128]
    both = []
    for c in range(2):
        rows = [block[at + 6 * c : at + 6 * c + 6] for at in (0, 12, 56, 32, 44, 80, 92)]
        vec = line if c == 0 else pltpu.roll(line, 64, 1)
        vec = jnp.concatenate([jnp.broadcast_to(vec, (6, 128)), jnp.zeros((6, 256), F32)], axis=1)
        both.append(jnp.concatenate(rows + [vec], axis=0))
    first = where[3] == 0
    kept[...] = jnp.where(first, both[0], both[1])
    sent[...] = jnp.where(first, both[1], both[0])


def finish_kernel(where, kept, got, q, k, v, up, *vectors):
    first = where[3] == 0
    one = jnp.where(first, kept[...], got[...])
    two = jnp.where(first, got[...], kept[...])
    for i, ref in enumerate((q, k, v)):
        ref[...] = joined(one[6 * i : 6 * i + 6], two[6 * i : 6 * i + 6], 48)
    wide = [
        jnp.concatenate([h[18 + 6 * i : 24 + 6 * i] for i in range(4)], axis=1) for h in (one, two)
    ]
    up[...] = joined(wide[0], wide[1], 192)
    line = one[42:43, :128] + two[42:43, :128]
    for i, ref in enumerate(vectors):
        ref[...] = line[:, 6 * i : 6 * i + ref.shape[1]]


def toeplitz(base):
    return pltpu.roll(jnp.broadcast_to(base, (TOK, 2 * TOK)), 0, 1, stride=1, stride_axis=0)


def fetch_pair(where, mine, other, held, first, sems):
    core = where[3]
    return fetch(
        (mine, other),
        [held.at[pl.ds(pl.multiple_of(first + c * TOK, TOK), TOK)] for c in (core, 1 - core)],
        sems,
    )


def fetch(refs, held, sems):
    copies = [pltpu.make_async_copy(r, h, sems.at[i]) for i, (r, h) in enumerate(zip(refs, held))]
    for copy in copies:
        copy.start()
    return copies


def wait(copies):
    for copy in copies:
        copy.wait()


ATTN_HELD = (
    (((768, 384), BF16),) * 2
    + (((768, 768), BF16),) * 2
    + (((384, 768), BF16),) * 2
    + (((512, 384), F32),) * 3
    + (((768, 384), F32),) * 2
)


def norm_kernel(where, halo, tokens, others, xhat_ref, xt_hi_far, xt_lo_far, x_ref, xt_hi, xt_lo, sems):
    fetched = fetch((halo,), (x_ref.at[pl.ds(0, TOK)],), sems)
    fetched += fetch_pair(where, tokens, others, x_ref, TOK, sems.at[pl.ds(1, 2)])
    wait(fetched)
    xhat, _ = normal_parts(x_ref[...])
    xhat_ref[...] = xhat
    xt_hi[...], xt_lo[...] = split(xhat.T)
    wait(fetch((xt_hi, xt_lo), (xt_hi_far, xt_lo_far), sems.at[pl.ds(3, 2)]))


def attn_kernel(
    where, xhat_ref, valid_ref, features, offsets, a0, a1, a2, a3, b0, b1, b2, b3,
    part_far, vec_ref, base_ref, *more,
):
    outs, held = more[:11], more[11:22]
    part_ref, one, two, lines, sems, out_sems, half_sems, line_sems = more[22:]
    q_hi, q_lo, kv_hi, kv_lo, o_hi, o_lo, sig_ref, ratio_ref, below_ref, w_ref, v_ref = held

    def keep(first, count):
        at = slice(first, first + count)
        return fetch(held[at], outs[at], out_sems.at[pl.ds(first, count)])

    fetched = fetch(
        [a.at[pl.ds(384, 8)] for a in (a0, a1, a2, a3)], [lines.at[k] for k in range(4)], line_sems
    )
    copies = bring(where, (a0, a1, a2, a3), (b0, b1, b2, b3), one, two, sems)
    wait(fetched)
    picked, base = spread_vectors(where, [lines[k] for k in range(4)], features[...], offsets[...])
    vec_ref[...] = jnp.concatenate(picked + [jnp.zeros((4, 768), F32)], axis=0)
    base_ref[...] = jnp.broadcast_to(base, (8, 512))
    wait(copies)
    unpack_attn(one, two, q_hi, q_lo, kv_hi, kv_lo, o_hi, o_lo)
    kept = keep(0, 6)
    gain, offset = picked[:2]
    parts = split(xhat_ref[...] * gain + offset)
    own = tuple(p[TOK:] for p in parts)
    keys = dot3(parts, (kv_hi[...], kv_lo[...]))
    sig_ref[...] = jax.nn.sigmoid(dot3(own, (q_hi[...], q_lo[...])))
    w = jnp.exp(keys[:, :384])
    w_ref[:TOK] = jnp.where(valid_ref[0] > 0.0, w[:TOK], 0.0)
    w_ref[TOK:] = w[TOK:]
    v_ref[...] = keys[:, 384:]
    kept += keep(6, 1) + keep(9, 2)
    w = w_ref[...]
    sums = split(jnp.concatenate([w * v_ref[...], w], axis=1))
    band = split(toeplitz(base))
    for i in range(2):
        at, half = slice(TOK * i, TOK * i + TOK), pl.ds(TOK * i, TOK)
        seen = tuple(s[TOK * i : TOK * i + 2 * TOK] for s in sums)
        mixed = dot3(band, seen)
        below_ref[at] = mixed[:, 384:]
        ratio_ref[at] = mixed[:, :384] / mixed[:, 384:]
        for j in (7, 8):
            kept += fetch((held[j].at[half],), (outs[j].at[half],), half_sems.at[i, pl.ds(j - 7, 1)])
        mixed = split(sig_ref[at] * ratio_ref[at])
        part_ref[at] = dot3(mixed, (o_hi[...], o_lo[...]))
        kept += fetch((part_ref.at[half],), (part_far.at[half],), half_sems.at[i, pl.ds(2, 1)])
    wait(kept)


def fetch_down(down_far, down, sems):
    return fetch([down_far.at[z] for z in range(4)], [down.at[z] for z in range(4)], sems)


def unpack_down(fetched, down, down_hi, down_lo):
    for zh in range(2):
        wait(fetched[2 * zh : 2 * zh + 2])
        for x in range(4):
            for y in range(4):
                rows = jnp.concatenate([down[2 * zh + zl, y, x] for zl in range(2)], axis=0)
                at = pl.ds(((x * 2 + zh) * 4 + y) * 48, 48)
                down_hi[at, :], down_lo[at, :] = split(rows)


def ffn_early_kernel(
    where, down_far, mine, other, gh_ref, down, down_hi, down_lo, cot_ref, cot_sems, in_sems
):
    kept = fetch_down(down_far, down, in_sems)
    fetched = fetch_pair(where, mine, other, cot_ref, 0, cot_sems)
    unpack_down(kept, down, down_hi, down_lo)
    wait(fetched)
    cot = split(cot_ref[...])
    for i in range(2):
        at = slice(768 * i, 768 * i + 768)
        gh_ref[:, at] = dot3(cot, (down_hi[at], down_lo[at]), NT)


def ffn_kernel(
    where, tokens, others, mine_far, theirs_ref, vec_ref, gh_ref, a0, a1, a2, a3, b0, b1, b2, b3,
    middle_far, middle_own, nt_hi, nt_lo, h_hi, h_lo, g_hi, g_lo, back_far,
    middle_ref, back_ref, x_ref, mine_ref, one, two, up_hi, up_lo, sems, in_sems, out_sems,
):
    fetched = fetch((mine_far,), (mine_ref,), in_sems)
    fetched += fetch_pair(where, tokens, others, x_ref, 0, in_sems.at[pl.ds(2, 2)])
    wait(bring(where, (a0, a1, a2, a3), (b0, b1, b2, b3), one, two, sems))
    unpack_up(one, two, up_hi, up_lo)
    wait(fetched)
    middle_ref[...] = x_ref[...] + (mine_ref[...] + theirs_ref[...])
    own = pl.ds(pl.multiple_of(where[3] * TOK, TOK), TOK)
    sent = fetch((middle_ref, middle_ref.at[own]), (middle_far, middle_own), out_sems)
    xhat, _ = normal_parts(middle_ref[...])
    normed = xhat * vec_ref[2:3, :] + vec_ref[3:4, :]
    parts = split(normed)
    nt_hi[...], nt_lo[...] = split(normed.T)
    halves = [pl.ds(TOK * c, TOK) for c in range(2)]
    for c, rows in enumerate((slice(0, TOK), slice(TOK, 2 * TOK))):
        for i in range(6):
            at = slice(256 * i, 256 * i + 256)
            preact = dot3(tuple(p[rows] for p in parts), (up_hi[:, at], up_lo[:, at]))
            lower, density = normal_cdf(preact)
            slope = lower + preact * density
            h_hi[rows, at], h_lo[rows, at] = split(preact * lower)
            g_hi[rows, at], g_lo[rows, at] = split(gh_ref[rows, at] * slope)
        back_ref[rows] = dot3((g_hi[rows], g_lo[rows]), (up_hi[...], up_lo[...]), NT)
        sent += fetch((back_ref.at[halves[c]],), (back_far.at[halves[c]],), out_sems.at[pl.ds(2 + c, 1)])
    wait(sent)


def ffn_late_kernel(
    where, cot_mine, cot_other, nt_hi, nt_lo, h_hi, h_lo, g_hi, g_lo,
    down_grad_far, a0, a1, a2, a3, b0, b1, b2, b3, one, two, sems, cot_ref, down_grad,
    in_sems, out_sems,
):
    fetched = fetch_pair(where, cot_mine, cot_other, cot_ref, 0, in_sems)
    nt = (nt_hi[...], nt_lo[...])
    sent = []
    wait(fetched)
    cot = split(cot_ref[...])
    for i in range(2):
        at = slice(768 * i, 768 * i + 768)
        rows = dot3((h_hi[:, at].T, h_lo[:, at].T), cot)
        for chip in range(32):
            x, zh, y, zl = (2 * i + chip // 16), chip // 8 % 2, chip // 2 % 4, chip % 2
            down_grad[2 * zh + zl, y, x] = rows[chip * 24 : chip * 24 + 24]
        for place in range(16):
            part = (place // 4, place % 4, pl.ds(2 * i, 2))
            sem = out_sems.at[i * 16 + place]
            sent.append(pltpu.make_async_copy(down_grad.at[part], down_grad_far.at[part], sem))
            sent[-1].start()
    for i in range(2):
        at = slice(768 * i, 768 * i + 768)
        grad = dot3(nt, (g_hi[:, at], g_lo[:, at]))
        pair = (grad[:, :384], grad[:, 384:])
        place_in_blocks(one, two, *((pair, None) if i == 0 else (None, pair)))
        sent += send(where, 1 - i, ((a0, a1, a2, a3), (b0, b1, b2, b3))[i], (one, two)[i], sems.at[i])
    wait(sent)


def out_kernel(
    where, h_hi_far, h_lo_far, down_far, own, other,
    h_hi, h_lo, down, down_hi, down_lo, out_ref, sems, in_sems, out_sems,
):
    kept = fetch_down(down_far, down, in_sems)
    fetched = fetch((h_hi_far, h_lo_far), (h_hi, h_lo), sems)
    unpack_down(kept, down, down_hi, down_lo)
    wait(fetched)
    for i in range(2):
        at = slice(768 * i, 768 * i + 768)
        out = dot3((h_hi[:, at], h_lo[:, at]), (down_hi[at], down_lo[at]))
        if i == 0:
            out_ref[...] = out
        else:
            out_ref[...] += out
    places = [pl.ds(pl.multiple_of(TOK * c, TOK), TOK) for c in (where[3], 1 - where[3])]
    wait(fetch([out_ref.at[p] for p in places], (own, other), out_sems))


def attn_back_kernel(
    where, vec_ref, base_ref, middle_far, mine_far, theirs_ref, cot_mine, cot_other,
    f0, f1, f2, f3, f4, f5, f6, gmid_own, gq_ref, gkv_ref, out_grad, small_ref, bias_ref,
    middle_ref, mine_ref, cot_ref, gmid_ref,
    o_hi, o_lo, sig_ref, ratio_ref, below_ref, w_ref, v_ref, sems, out_sems,
):
    halves = [pl.ds(TOK * c, TOK) for c in range(2)]
    first = [
        fetch([far.at[p] for p in halves], [ref.at[p] for p in halves], sems.at[pl.ds(9 + 2 * i, 2)])
        for i, (far, ref) in enumerate(((middle_far, middle_ref), (mine_far, mine_ref)))
    ]
    copies = fetch_pair(where, cot_mine, cot_other, cot_ref, 0, sems)
    copies += fetch((f0, f1), (o_hi, o_lo), sems.at[pl.ds(2, 2)])
    wait(first[0])
    xhat, scale = normal_parts(middle_ref[...])
    wait(first[1])
    kept = fetch(
        (f2, f3, f4, f5, f6), (sig_ref, ratio_ref, below_ref, w_ref, v_ref), sems.at[pl.ds(4, 5)]
    )
    mine = mine_ref[...]
    small_ref[2:3, :] = jnp.sum(mine * xhat, axis=0, keepdims=True)
    small_ref[3:4, :] = jnp.sum(mine, axis=0, keepdims=True)
    gmid = normal_back(mine + theirs_ref[...], xhat, scale, vec_ref[2:3, :])
    wait(copies)
    gmid = cot_ref[...] + gmid
    gmid_ref[...] = gmid
    gmid = split(gmid)
    own = pl.ds(pl.multiple_of(where[3] * TOK, TOK), TOK)
    sent = fetch((gmid_ref.at[own],), (gmid_own,), out_sems)
    gmixed = dot3(gmid, (o_hi[...], o_lo[...]), NT)
    wait(kept)
    sig, ratio = sig_ref[...], ratio_ref[...]
    out_grad[...] = dot3(split((sig * ratio).T), gmid)
    gq = gmixed * ratio * sig * (1.0 - sig)
    gq_ref[...] = gq
    gnum = gmixed * sig / below_ref[...]
    gsums = split(jnp.concatenate([gnum, -gnum * ratio], axis=1))
    band = toeplitz(base_ref[0:1, :])
    band_t = split(band.T)
    w, v = w_ref[...], v_ref[...]
    sums = split(jnp.concatenate([w * v, w], axis=1))
    spread, gband = [], None
    for i in range(2):
        here = tuple(g[TOK * i : TOK * i + TOK] for g in gsums)
        seen = tuple(s[TOK * i : TOK * i + 2 * TOK] for s in sums)
        spread.append(dot3(band_t, here))
        term = dot3(here, seen, NT)
        gband = term if gband is None else gband + term
    count = TOK
    while count > 1:
        count //= 2
        gband = gband[:count] + pltpu.roll(gband[count:], 2 * TOK - count, 1)
    bias_ref[...] = jnp.broadcast_to(gband * base_ref[0:1, :], (8, 2 * TOK))
    gseen = jnp.concatenate(
        [spread[0][:TOK], spread[0][TOK:] + spread[1][:TOK], spread[1][TOK:]], axis=0
    )
    gkv = jnp.concatenate([w * (gseen[:, :384] * v + gseen[:, 384:]), gseen[:, :384] * w], axis=1)
    gkv_ref[...] = gkv
    wait(sent)


def attn_grads_kernel(
    where, vec_ref, gq_ref, gkv_ref, out_grad, small_two, bias, features, offsets, feature_columns,
    offset_columns, f0, f1, f2, f3, f4, f5, a0, a1, a2, a3, b0, b1, b2, b3,
    one, two, sems, q_hi, q_lo, kv_hi, kv_lo, xt_hi, xt_lo, in_sems, line_sems,
):
    kept = fetch((f4, f5, f0, f1, f2, f3), (xt_hi, xt_lo, q_hi, q_lo, kv_hi, kv_lo), in_sems)
    gq, gkv = gq_ref[...], gkv_ref[...]
    vec = vec_ref[...].T
    wait(kept[:2])
    small = [0.0, 0.0]

    def grad_of(dots, g):
        total = jnp.sum(g, axis=0, keepdims=True)
        return vec[:, 0:1] * dots + vec[:, 1:2] * total

    def add_small(dots, g, high, low):
        weight = high[...].astype(F32) + low[...].astype(F32)
        total = jnp.sum(g, axis=0, keepdims=True)
        small[0] += jnp.sum(dots * weight, axis=1, keepdims=True)
        small[1] += jnp.sum(total * weight, axis=1, keepdims=True)

    kv_dot = dot3((xt_hi[...], xt_lo[...]), split(gkv))
    kv_grad = grad_of(kv_dot, gkv)
    place_in_blocks(one, two, None, (kv_grad[:, 384:], out_grad[...]))
    sent = send(where, 0, (b0, b1, b2, b3), two, sems.at[1])
    q_dot = dot3((xt_hi[:, TOK:], xt_lo[:, TOK:]), split(gq))
    place_in_blocks(one, two, (grad_of(q_dot, gq), kv_grad[:, :384]), None)
    sent += send(where, 1, (a0, a1, a2, a3), one, sems.at[0], 384)
    wait(kept[2:])
    add_small(kv_dot, gkv, kv_hi, kv_lo)
    add_small(q_dot, gq, q_hi, q_lo)
    small = jnp.concatenate(small + [jnp.zeros((768, 126), F32)], axis=1).T
    smalls = (small[0:1], small[1:2], small_two[2:3, :], small_two[3:4, :])
    lines = place_lines(
        where, smalls, bias[0:1, :], features, offsets, feature_columns, offset_columns
    )
    for k, part in enumerate((a0, a1, a2, a3)):
        line = lines[16 * k : 16 * k + 16]
        place = one.at[at_hops(where, 1, k), pl.ds(384, 8)]
        place[...] = jnp.concatenate([line[:8], line[8:], jnp.zeros((8, 128), F32)], axis=1)
        sent.append(pltpu.make_async_copy(place, part.at[pl.ds(384, 8)], line_sems.at[k]))
        sent[-1].start()
    wait(sent)


def attn_last_kernel(
    where, gq_ref, gkv_ref, f0, f1, f2, f3, own, other, halo_own, halo_other,
    q_hi, q_lo, kv_hi, kv_lo, back_ref, sems, out_sems,
):
    kept = fetch((f2, f3, f0, f1), (kv_hi, kv_lo, q_hi, q_lo), sems)
    gq, gkv = split(gq_ref[...]), split(gkv_ref[...])
    wait(kept)
    back_ref[...] = dot3(gkv, (kv_hi[...], kv_lo[...]), NT)
    back_ref[TOK:] += dot3(gq, (q_hi[...], q_lo[...]), NT)
    core, half = where[3], TOK // 2
    places = [(TOK * (1 + c), TOK) for c in (core, 1 - core)] + [
        (half * c, half) for c in (core, 1 - core)
    ]
    places = [back_ref.at[pl.ds(pl.multiple_of(at, half), n)] for at, n in places]
    wait(fetch(places, (own, other, halo_own, halo_other), out_sems))


def tokens_kernel(
    where, tokens, gmid, back, back_other, halo_low, halo_high, vec_ref, middle, out, out_other,
    out_ref, output_ref,
):
    output_ref[...] = middle[...] + (out[...] + out_other[...])
    back = back[...] + back_other[...]
    halo = jnp.concatenate([halo_low[...], halo_high[...]], axis=0)
    back = back + jnp.where(where[3] == 0, 0.0, halo)
    xhat, scale = normal_parts(tokens[...])
    out_ref[...] = gmid[...] + normal_back(back, xhat, scale, vec_ref[0:1, :])


def shaped(*shape, dtype=F32):
    return jax.ShapeDtypeStruct(shape, dtype)


def kept_near(*shape, dtype=F32):
    return pltpu.VMEM(shape, dtype)


def kept_far(*shape, dtype=F32):
    return pltpu.HBM(shape, dtype)


def near(array):
    return pltpu.with_memory_space_constraint(array, pltpu.VMEM)


def far(array):
    return pltpu.with_memory_space_constraint(array, pltpu.HBM)


def call(kernel, out_shape, args, specs, scratch=(), flops=0, moved=0, vmem=24, **more):
    return pl.pallas_call(
        kernel,
        out_shape=out_shape,
        in_specs=specs,
        scratch_shapes=list(scratch),
        compiler_params=pltpu.CompilerParams(vmem_limit_bytes=vmem * 1024 * 1024),
        cost_estimate=pl.CostEstimate(flops=flops, bytes_accessed=moved, transcendentals=0),
        **more,
    )(*args)


def glue(kernel, shapes, args, axis=None, given=near, gives=kept_near):
    if axis is not None:
        kernel = functools.partial(kernel, axis)
    return call(
        kernel,
        tuple((gives[i] if isinstance(gives, tuple) else gives)(*s) for i, s in enumerate(shapes)),
        (args[0], *map(given, args[1:])),
        [SM] + [VM] * (len(args) - 1),
        vmem=10,
    )


def after(arrays, *others):
    return lax.optimization_barrier((arrays, others))[0]


def phase(*arrays):
    return lax.optimization_barrier(arrays)


def shards(
    inputs, query_weight, key_weight, value_weight, out_weight, up_weight, down_weight,
    gain_one, offset_one, gain_two, offset_two, pos_bias, prefix_len, cotangent,
):
    x, y, core = lax.axis_index("x"), lax.axis_index("y"), lax.axis_index("core")
    zh, zl = lax.axis_index("zh"), lax.axis_index("zl")
    z = zh * 2 + zl
    where = jnp.stack([x, y, z, core]).astype(jnp.int32)
    first_core = core == 0
    dma = lambda *shape: pltpu.SemaphoreType.DMA(shape)
    places = (pltpu.VMEM((4, 384, 384), F32),) * 2 + (dma(2, 4),)
    pair16 = lambda *shape: (kept_near(*shape, dtype=BF16),) * 2
    grad_blocks = (kept_far(384, 384),) * 8
    tables = place_tables()

    with jax.named_scope("pack"):
        near_down = both_ways(down_weight, "x")
        vectors = [a[None] for a in (gain_one, offset_one, gain_two, offset_two, pos_bias)]
        kept, sent = glue(
            pack_one_kernel,
            ((48, 384),) * 2,
            (where, query_weight, key_weight, value_weight, up_weight, *vectors),
            given=far,
        )
        tokens, cot, near_down, sent = phase(inputs[0], cotangent[0], near_down, sent)
        got, far_down = swap_cores(sent), hop(near_down[0], "x")
        (block,) = glue(
            pack_two_kernel,
            ((104, 384),),
            (where, near(kept), near(got), far(out_weight)),
            given=lambda array: array,
        )
    with jax.named_scope("gather_z"):
        block, tokens, cot = phase(block, tokens, cot)
        seq = (x * 2 + zh) * 2 + core
        positions = seq * TOK + jnp.arange(TOK, dtype=jnp.int32)
        cot = cot * (positions >= prefix_len[0]).astype(F32)[:, None]
        block, cot, far_down = phase(gather_at_once(block, "z"), cot, far_down)
        one, two = glue(
            stack_one_kernel,
            ((4, HALF_ONE, 384), (4, HALF_TWO, 384)),
            (where, *block),
            given=lambda array: array,
            gives=shaped,
        )

    with jax.named_scope("gather_mid"):
        one, two, cot, tokens, far_down = phase(one, two, cot, tokens, far_down)
        (down,) = glue(
            stack_down_kernel,
            ((4, 24, 768),),
            (where, down_weight, *near_down, far_down),
            given=lambda array: array,
            gives=kept_far,
        )
        down = lax.all_gather(down, "y", axis=0)
        others = swap_cores(tokens)
        near_one, near_two, others = phase(both_ways(one, "x"), both_ways(two, "y"), others)
        halo = along_row(after(tokens, near_one), 1, (1,), (0,))
        far_one, far_two, halo = phase(hop(near_one[0], "x"), hop(near_two[0], "y"), halo)
        down = lax.all_gather(after(down, far_one), RING["z"], axis=0)
        attn_one, up_one, attn_two, up_two = glue(
            stack_both_kernel,
            ((392, 384), (384, 384), (384, 384), (384, 384)),
            (where, one, *near_one, far_one, two, *near_two, far_two),
            given=lambda array: array,
            gives=kept_far,
        )

    with jax.named_scope("gather_attn"):
        attn_one, attn_two, up_one, up_two = phase(attn_one, attn_two, up_one, up_two)
        near_one, near_two = phase(both_ways(attn_one, "y"), both_ways(attn_two, "x"))
        halo, cot = after((halo, cot), near_one)
        far_one, far_two = hop(near_one[0], "y"), hop(near_two[0], "x")
        cot_other = swap_cores(cot)
        halo = jnp.where(first_core, halo, swap_cores(halo))
        xhat, *xt = call(
            norm_kernel,
            (kept_near(768, 768),) + (kept_far(768, 768, dtype=BF16),) * 2,
            (where, *map(far, (halo, tokens, others))),
            [SM] + [HB] * 3,
            [pltpu.VMEM((768, 768), F32)] + [pltpu.VMEM((768, 768), BF16)] * 2 + [dma(5)],
            vmem=16,
            out_specs=(VM, HB, HB),
        )
        far_one, far_two, xhat, xt, cot_other = phase(far_one, far_two, xhat, xt, cot_other)
        attn_one = (attn_one, *near_one, far_one)
        attn_two = (attn_two, *near_two, far_two)
        valid = jnp.where(x * 2 + zh > 0, 1.0, 0.0).astype(F32).reshape(1)

    with jax.named_scope("attn"):
        attn_one, attn_two, up_one, up_two = phase(attn_one, attn_two, up_one, up_two)
        near_one, near_two = both_ways(up_one, "y"), both_ways(up_two, "x")
        part, vec, base, *held = call(
            attn_kernel,
            (kept_far(512, 768), shaped(8, 768), shaped(8, 512)) + tuple(kept_far(*h, dtype=t) for h, t in ATTN_HELD),
            (where, near(xhat), valid, *tables[:2], *map(far, attn_one + attn_two)),
            [SM, VM, SM, VM, VM] + [HB] * 8,
            [pltpu.VMEM(h, t) for h, t in ATTN_HELD]
            + [pltpu.VMEM((512, 768), F32), *places[:2], pltpu.VMEM((4, 8, 384), F32), places[2]]
            + [dma(11), dma(2, 3), dma(4)],
            flops=5_700_000_000,
            moved=1_000_000,
            vmem=36,
            out_specs=(HB, VM, VM) + (HB,) * 11,
        )
        near_one, near_two, part, held = phase(near_one, near_two, part, held)

    with jax.named_scope("ffn_early"):
        part_other = swap_cores(part)
        far_one, far_two = hop(near_one[0], "y"), hop(near_two[0], "x")
        gh = call(
            ffn_early_kernel,
            kept_near(512, 1536),
            (where, *map(far, (down, cot, cot_other))),
            [SM] + [HB] * 3,
            [pltpu.VMEM((4, 4, 4, 24, 768), F32)]
            + [pltpu.VMEM((1536, 768), BF16)] * 2
            + [pltpu.VMEM((512, 768), F32), dma(2), dma(4)],
            flops=3_600_000_000,
            moved=1_000_000,
            vmem=20,
        )
        down_full = down
        part_other, far_one, far_two, gh = phase(part_other, far_one, far_two, gh)
        up_all = (up_one, *near_one, far_one, up_two, *near_two, far_two)

    with jax.named_scope("ffn"):
        middle, middle_own, *ffn_held, back_part = call(
            ffn_kernel,
            (kept_far(512, 768), kept_far(256, 768))
            + pair16(768, 512)
            + pair16(512, 1536) * 2
            + (kept_far(512, 768),),
            (where, *map(far, (tokens, others, part)), part_other, vec, near(gh))
            + (*map(far, up_all[:3]), up_all[3], *map(far, up_all[4:7]), up_all[7]),
            [SM] + [HB] * 3 + [VM] * 3 + ([HB] * 3 + [ANY]) * 2,
            (pltpu.VMEM((512, 768), F32),) * 4
            + places[:2]
            + (pltpu.VMEM((768, 1536), BF16),) * 2
            + (places[2], dma(4), dma(4)),
            flops=7_200_000_000,
            moved=1_000_000,
            vmem=30,
            out_specs=(HB, HB) + (VM,) * 6 + (HB,),
        )
        back_other = swap_cores(back_part)
        down_grads, *up_grads = call(
            ffn_late_kernel,
            (kept_far(4, 4, 4, 24, 768),) + grad_blocks,
            (where, far(cot), far(cot_other), *map(near, ffn_held)),
            [SM] + [HB] * 2 + [VM] * 6,
            places
            + (pltpu.VMEM((512, 768), F32), pltpu.VMEM((4, 4, 4, 24, 768), F32), dma(2), dma(32)),
            flops=7_300_000_000,
            moved=1_000_000,
            vmem=24,
            out_specs=(HB,) * 9,
        )
        back_other, up_grads, down_grads = phase(back_other, up_grads, down_grads)

    with jax.named_scope("attn_back"):
        up_one, up_two = up_grads[:4], up_grads[4:]
        came = scatter_start(up_one, "y"), scatter_start(up_two, "x")
        q_w, kv_w, o_w, saved = held[:2], held[2:4], held[4:6], held[6:]
        gmid, gq, gkv, out_grad, small_two, bias = call(
            attn_back_kernel,
            (kept_far(256, 768), kept_near(512, 384), kept_near(768, 768), kept_near(384, 768))
            + (shaped(8, 768), shaped(8, 512)),
            (where, vec, base)
            + (far(middle), far(back_part), back_other)
            + tuple(map(far, (cot, cot_other, *o_w, *saved))),
            [SM] + [VM] * 2 + [HB] * 2 + [VM] + [HB] * 9,
            [pltpu.VMEM((512, 768), F32)] * 4
            + [pltpu.VMEM(h, t) for h, t in ATTN_HELD[4:]]
            + [dma(15), dma(1)],
            flops=5_000_000_000,
            moved=1_000_000,
            vmem=32,
            out_specs=(HB,) + (VM,) * 5,
        )
        down = lax.psum_scatter(down_grads, RING["z"], scatter_dimension=0, tiled=True)[0]
        came, gq, gkv, out_grad = phase(came, gq, gkv, out_grad)

    with jax.named_scope("attn_grads"):
        gq, gkv, out_grad = map(near, (gq, gkv, out_grad))
        up_one_came, up_two_came = scatter_end(where, up_one, up_two, came, "yx")
        attn_grads = call(
            attn_grads_kernel,
            (kept_far(392, 384),) * 4 + (kept_far(384, 384),) * 4,
            (where, vec, gq, gkv, out_grad, small_two, bias, *tables)
            + tuple(map(far, (*q_w, *kv_w, *xt))),
            [SM] + [VM] * 10 + [HB] * 6,
            [pltpu.VMEM((4, 392, 384), F32), *places[1:]]
            + [pltpu.VMEM(h, t) for h, t in ATTN_HELD[:4]]
            + [pltpu.VMEM((768, 768), BF16)] * 2
            + [dma(6), dma(4)],
            flops=3_600_000_000,
            moved=1_000_000,
            vmem=32,
            out_specs=(HB,) * 8,
        )
        up_one_came, up_two_came, attn_grads = phase(up_one_came, up_two_came, attn_grads)

    with jax.named_scope("attn_last"):
        attn_one, attn_two = attn_grads[:4], attn_grads[4:]
        came = scatter_start(attn_one, "y"), scatter_start(attn_two, "x")
        back_own, back_other, halo_own, halo_other = call(
            attn_last_kernel,
            (kept_far(256, 768),) * 2 + (kept_far(128, 768),) * 2,
            (where, gq, gkv, *map(far, (*q_w, *kv_w))),
            [SM] + [VM] * 2 + [HB] * 4,
            [pltpu.VMEM(h, t) for h, t in ATTN_HELD[:4]]
            + [pltpu.VMEM((768, 768), F32), dma(4), dma(4)],
            flops=3_600_000_000,
            moved=1_000_000,
            vmem=20,
            out_specs=(HB,) * 4,
        )
        halo_other = swap_cores(halo_other)
        came, back_own, back_other, halo_own, halo_other, down = phase(
            came, back_own, back_other, halo_own, halo_other, down
        )
        down = lax.psum_scatter(down, "y", scatter_dimension=0, tiled=True)[0]

    with jax.named_scope("scatter_attn"):
        attn_one_came, attn_two_came = scatter_end(where, attn_one, attn_two, came, "yx")
        out_own, out_other = call(
            out_kernel,
            (kept_far(256, 768),) * 2,
            (where, *map(far, (*ffn_held[2:4], down_full))),
            [SM] + [HB] * 3,
            [pltpu.VMEM((512, 1536), BF16)] * 2
            + [pltpu.VMEM((4, 4, 4, 24, 768), F32)]
            + [pltpu.VMEM((1536, 768), BF16)] * 2
            + [pltpu.VMEM((512, 768), F32), dma(2), dma(4), dma(2)],
            flops=3_600_000_000,
            moved=1_000_000,
            vmem=24,
            out_specs=(HB,) * 2,
        )
        back_other = swap_cores(back_other)
        halo_high = along_row(halo_own + halo_other, -1, (0, 1), (0, 1))
        sums = [
            glue(
                sum_kernel,
                (attn[0].shape, up[0].shape),
                (where, attn[0], attn_came[0], up[0], *up_came),
                given=far,
                gives=kept_far,
            )
            for attn, attn_came, up, up_came in (
                (attn_one, attn_one_came, up_one, up_one_came),
                (attn_two, attn_two_came, up_two, up_two_came),
            )
        ]
        attn_one_came, attn_two_came, out_own, out_other, halo_high, back_other, sums = phase(
            attn_one_came, attn_two_came, out_own, out_other, halo_high, back_other, sums
        )

    def attn_tail(own, came):
        return far(own), far(came[0]), came[1]

    now_and_later = (kept_far,) * 2 + (shaped,) * 2

    as_is = lambda array: array

    with jax.named_scope("scatter_mid"):
        one = glue(
            part_one_kernel,
            ((4, HALF_ONE, 384),) * 4,
            (where, far(sums[0][0]), attn_one_came[1], far(sums[0][1])),
            0,
            given=as_is,
            gives=now_and_later,
        )
        two = glue(
            part_one_kernel,
            ((4, HALF_TWO, 384),) * 4,
            (where, far(sums[1][0]), attn_two_came[1], far(sums[1][1])),
            1,
            given=as_is,
            gives=now_and_later,
        )
        came = scatter_start(one, "x"), scatter_start(two, "y")
        out_other = swap_cores(out_other)
        came, one, two, down, out_other = phase(came, one, two, down, out_other)

        one_came, two_came = scatter_end(where, one, two, came, "xy")
        down = glue(part_down_kernel, ((24, 768),) * 4, (where, down), 0, given=far)
        down_came = scatter_start(down, "x")
        one_came, two_came, down_came, down = phase(one_came, two_came, down_came, down)

    with jax.named_scope("scatter_z"):
        block = glue(
            part_two_kernel,
            ((104, 384),) * 4,
            (where, *attn_tail(one[0], one_came), *attn_tail(two[0], two_came)),
            given=as_is,
            gives=shaped,
        )
        (next_down,) = glue(add_one_kernel, ((24, 768),), (where, down[1], down_came[0]))
        block, next_down = phase(block, next_down)
        block = scatter_at_once(block, "z")
        next_down = hop(next_down, "x")
        halo_low = swap_cores(halo_high)
        gmid = after(gmid, next_down)
        input_grad, output = glue(
            tokens_kernel,
            ((256, 768),) * 2,
            (where, inputs[0], gmid, back_own, back_other, halo_low, halo_high, vec)
            + (middle_own, out_own, out_other),
            given=as_is,
            gives=shaped,
        )
        down = down[0] + down_came[1] + next_down
        block, down, input_grad, output = phase(block, down, input_grad, output)

    with jax.named_scope("finish"):
        out_grad, kept, sent = glue(
            sum_three_kernel,
            ((6, 768), (48, 384), (48, 384)),
            (where, *block),
            given=as_is,
            gives=(shaped,) * 3,
        )
        got = swap_cores(sent)
        *qkv, up_out = glue(
            finish_kernel,
            ((6, 768),) * 3 + ((6, 3072),) + ((1, 6),) * 4 + ((1, 2),),
            (where, kept, got),
            gives=shaped,
        )
        qkv, up_out, vectors = qkv[:3], qkv[3], [v[0] for v in (*qkv[4:], up_out)]

    return (
        output[None], input_grad[None], *qkv, out_grad, up_out, down,
        *vectors,
    )


def solution(mesh):
    fine = Mesh(mesh.devices.reshape(4, 2, 2, 4, 2), AXES)
    tokens = P(("y", "zl"), ("x", "zh", "core"), None)
    matrix = P(AXES, None)
    vector = P(AXES)
    return jax.shard_map(
        shards,
        mesh=fine,
        in_specs=(tokens,) + (matrix,) * 6 + (vector,) * 5 + (P(("y", "zl")), tokens),
        out_specs=(tokens, tokens) + (matrix,) * 6 + (vector,) * 5,
        check_vma=False,
    )
```

```python
import functools

import jax
import jax.numpy as jnp
import numpy as np
from jax import lax
from jax.experimental import pallas as pl
from jax.experimental.pallas import tpu as pltpu
from jax.sharding import Mesh
from jax.sharding import PartitionSpec as P

EPSILON = 1e-05
AXES = ("x", "zh", "core", "y", "zl")
RING = {"x": "x", "y": "y", "z": ("zh", "zl")}
F32, BF16 = jnp.float32, jnp.bfloat16
TOK = 256
NT = (((1,), (1,)), ((), ()))
NN = (((1,), (0,)), ((), ()))
ANY = pl.BlockSpec(memory_space=pl.ANY)
HB = pl.BlockSpec(memory_space=pltpu.HBM)
VM = pl.BlockSpec(memory_space=pltpu.VMEM)
SM = pl.BlockSpec(memory_space=pltpu.SMEM)


def shift(array, axis, by):
    return lax.ppermute(array, RING[axis], [(i, (i + by) % 4) for i in range(4)])


def swap_cores(array):
    return lax.ppermute(array, "core", [(0, 1), (1, 0)])


def index_of(x, zh, core, y, zl):
    return (((x * 2 + zh) * 2 + core) * 4 + y) * 2 + zl


def along_row(array, by, from_core, to_core):
    pairs = []
    for chip in range(8):
        if 0 <= chip + by < 8:
            for y in range(4):
                for zl in range(2):
                    for a, b in zip(from_core, to_core):
                        pairs.append(
                            (
                                index_of(chip // 2, chip % 2, a, y, zl),
                                index_of((chip + by) // 2, (chip + by) % 2, b, y, zl),
                            )
                        )
    return lax.ppermute(array, AXES, pairs)


def hop(array, axis, by=1):
    pairs = []
    for at in np.ndindex(4, 4, 2, 4):
        to = dict(zip("xzcy", at))
        to[axis] = (to[axis] + by * (1 - 2 * to["c"])) % 4
        pairs.append(
            tuple(index_of(p[0], p[1] // 2, p[2], p[3], p[1] % 2) for p in (at, tuple(to.values())))
        )
    return lax.ppermute(array, AXES, pairs)


FROM = (0, 3, 1, 2)


def both_ways(block, axis):
    return hop(block, axis), hop(block, axis, -1)


def scatter_start(parts, axis):
    return hop(parts[2], axis), hop(parts[3], axis, -1)


def add_kernel(where, a0, a1, b0, b1, a_sum, b_sum):
    a_sum[...] = a0[...] + a1[...]
    b_sum[...] = b0[...] + b1[...]


def add_both_kernel(where, a0, a1, a2, a3, b0, b1, b2, b3, a_own, a_next, b_own, b_next):
    a_own[...] = a0[...] + a3[...]
    a_next[...] = a1[...] + a2[...]
    b_own[...] = b0[...] + b3[...]
    b_next[...] = b1[...] + b2[...]


def scatter_end(where, one, two, came, axes, parts=None):
    shapes = (one[1].shape, two[1].shape)
    parts = parts or far
    args = (where, parts(one[1]), came[0][0], parts(two[1]), came[1][0])
    sums = glue(add_kernel, shapes, args, given=lambda array: array, gives=shaped)
    return [(c[1], hop(a, axis)) for c, a, axis in zip(came, sums, axes)]


def gather_at_once(block, axis):
    return [block] + [shift(block, axis, -k) for k in (1, 2, 3)]


def scatter_at_once(parts, axis):
    return [parts[0]] + [shift(parts[k], axis, k) for k in (1, 2, 3)]


def split(value):
    high = value.astype(BF16)
    return high, (value - high.astype(F32)).astype(BF16)


def dot3(left, right, dims=NN):
    def one(a, b):
        return lax.dot_general(a, b, dims, preferred_element_type=F32)

    return one(left[0], right[0]) + one(left[0], right[1]) + one(left[1], right[0])


def normal_parts(values):
    centred = values - jnp.mean(values, axis=-1, keepdims=True)
    spread = jnp.mean(centred * centred, axis=-1, keepdims=True)
    scale = lax.rsqrt(spread + EPSILON)
    return centred * scale, scale


def normal_back(grad, xhat, scale, gain):
    e = grad * gain
    return scale * (
        e
        - jnp.mean(e, axis=-1, keepdims=True)
        - xhat * jnp.mean(e * xhat, axis=-1, keepdims=True)
    )


def normal_cdf(v):
    density = jnp.exp(-0.5 * v * v)
    d = 1.0 + np.float32(0.3275911 * np.sqrt(0.5)) * jnp.abs(v)
    t = pl.reciprocal(d, approx=True)
    t = t * (2.0 - d * t)
    t = t * (2.0 - d * t)
    total = np.float32(0.5 * 1.061405429)
    for c in (-1.453152027, 1.421413741, -0.284496736, 0.254829592):
        total = total * t + np.float32(0.5 * c)
    total = total * t * density
    return jnp.where(v < 0.0, total, 1.0 - total), density * np.float32(1.0 / np.sqrt(2.0 * np.pi))


HALF_ONE, HALF_TWO = 56, 48


def halved(array, c, run):
    count = array.shape[1] // (2 * run)
    return jnp.concatenate(
        [array[:, (2 * i + c) * run : (2 * i + c + 1) * run] for i in range(count)], axis=1
    )


def joined(first, second, run):
    count = first.shape[1] // run
    return jnp.concatenate(
        [h[:, i * run : (i + 1) * run] for i in range(count) for h in (first, second)], axis=1
    )


def pack_one_kernel(where, q, k, v, up, g_one, o_one, g_two, o_two, bias, kept, sent):
    vec = [ref[...] for ref in (g_one, o_one, g_two, o_two, bias)]
    vec = jnp.concatenate(vec + [jnp.zeros((1, 384 - 26), F32)], axis=1)
    both = []
    for c in range(2):
        wide = halved(up[...], c, 192)
        both.append(
            jnp.concatenate(
                [halved(w[...], c, 48) for w in (q, k, v)]
                + [wide[:, 384 * i : 384 * i + 384] for i in range(4)]
                + [jnp.broadcast_to(vec, (6, 384))],
                axis=0,
            )
        )
    first = where[3] == 0
    kept[...] = jnp.where(first, both[0], both[1])
    sent[...] = jnp.where(first, both[1], both[0])


def pack_two_kernel(where, kept, got, out, block):
    first = where[3] == 0
    one = jnp.where(first, kept[...], got[...])
    two = jnp.where(first, got[...], kept[...])

    def rows(i):
        return [one[6 * i : 6 * i + 6], two[6 * i : 6 * i + 6]]

    line = one[42:43, :128] + pltpu.roll(two[42:43, :128], 64, 1)
    block[0:24] = jnp.concatenate(rows(0) + rows(1), axis=0)
    block[24:32] = jnp.concatenate([jnp.broadcast_to(line, (8, 128)), jnp.zeros((8, 256), F32)], axis=1)
    block[32:56] = jnp.concatenate(rows(3) + rows(4), axis=0)
    block[56:80] = jnp.concatenate(rows(2) + [out[:, :384], out[:, 384:]], axis=0)
    block[80:104] = jnp.concatenate(rows(5) + rows(6), axis=0)


def stack_one_kernel(where, p0, p1, p2, p3, one, two):
    for off, ref in enumerate((p0, p1, p2, p3)):
        at = lax.rem(where[2] + off, 4)
        one[at] = ref[:HALF_ONE]
        two[at] = ref[HALF_ONE:]


def at_hops(where, axis, hops):
    return lax.rem(where[axis] + 4 + hops * (1 - 2 * where[3]), 4)


def stack_down_kernel(where, p0, p1, p2, p3, out):
    for hops, ref in zip(FROM, (p0, p1, p2, p3)):
        out[at_hops(where, 0, hops)] = ref[...]


def stack_two_kernel(axis, where, p0, p1, p2, p3, attn, up):
    skip = 8 if axis == 0 else 0
    row = lax.broadcasted_iota(jnp.int32, (8, 128), 0)
    vec = [jnp.zeros((8, 128), F32)] * 3
    for hops, ref in zip(FROM, (p0, p1, p2, p3)):
        at = at_hops(where, axis, hops)
        for z in range(4):
            rows = pl.ds(pl.multiple_of(at * 96 + 24 * z, 8), 24)
            attn[rows] = ref[z, 0:24]
            up[rows] = ref[z, 24 + skip : 48 + skip]
            if skip:
                line = ref[z, 24:32, :128]
                vec[z % 2] = jnp.where(row == at * 2 + z // 2, line, vec[z % 2])
    if skip:
        attn[384:392] = jnp.concatenate(vec, axis=1)


def stack_both_kernel(where, *refs):
    stack_two_kernel(0, where, *refs[:4], *refs[8:10])
    stack_two_kernel(1, where, *refs[4:8], *refs[10:])


def feature_places():
    x, zh, c, y, zl, r = np.indices((4, 2, 2, 4, 2, 6)).reshape(6, -1)
    return [a.astype(np.int32) for a in (y, zl * 8 + x * 2 + zh, x * 4 + zh * 2 + zl, c * 64 + r)]


def offset_places():
    x, zh, c, y, zl, r = np.indices((4, 2, 2, 4, 2, 2)).reshape(6, -1)
    places = []
    for a in (y, zl * 8 + x * 2 + zh, x * 4 + zh * 2 + zl, c * 64 + 24 + r):
        line = np.full((512,), -1000, np.int32)
        line[1:257] = a[::-1]
        places.append(line)
    return places


def place_tables():
    rows = [np.pad(np.stack(t), ((0, 4), (0, 0))) for t in (feature_places(), offset_places())]
    return rows + [np.ascontiguousarray(np.pad(r.T, ((0, 0), (0, 120)))) for r in rows]


def three_parts(value):
    high, rest = split(value)
    rest = value - high.astype(F32)
    return (high, *split(rest))


def pick_dot(left, right):
    return sum(jnp.dot(a, b, preferred_element_type=F32) for a in left for b in right)


def spread_vectors(where, pieces, features, offsets):
    lines = []
    for k in (0, 2, 3, 1):
        last = pieces[k][:, :256]
        lines += [last[:, :128], last[:, 128:]]
    lines = three_parts(jnp.concatenate(lines, axis=0).T)

    def spread(table):
        hops = jnp.bitwise_and((table[0:1, :] + 4 - where[1]) * (1 - 2 * where[3]), 3)
        place = hops * 16 + table[1:2, :]
        chips = lax.broadcasted_iota(jnp.int32, (64, table.shape[1]), 0) == place
        return pick_dot(lines, (chips.astype(F32).astype(BF16),))

    values = spread(features)
    lane = lax.broadcasted_iota(jnp.int32, values.shape, 0)
    picked = [
        jnp.sum(jnp.where(lane == features[3:4, :] + 6 * i, values, 0.0), axis=0, keepdims=True)
        for i in range(4)
    ]
    values = spread(offsets)
    lane = lax.broadcasted_iota(jnp.int32, values.shape, 0)
    base = jnp.sum(jnp.where(lane == offsets[3:4, :], values, 0.0), axis=0, keepdims=True)
    base = jnp.where(offsets[3:4, :] >= 0, jnp.exp(base), 0.0)
    return picked, base


def place_lines(where, smalls, bias, features, offsets, feature_columns, offset_columns):
    def gathered(values, table, columns, lane):
        hops = jnp.bitwise_and((table[0:1, :] + 4 - where[1]) * (1 - 2 * where[3]), 3)
        place = hops * 16 + table[1:2, :]
        chips = lax.broadcasted_iota(jnp.int32, (64, table.shape[1]), 0) == place
        lanes = lax.broadcasted_iota(jnp.int32, (table.shape[1], 128), 1) == columns[:, 3:4] + lane
        return pick_dot(
            three_parts(jnp.where(chips, values, 0.0)), (lanes.astype(F32).astype(BF16),)
        )

    total = gathered(bias, offsets[...], offset_columns[...], 0)
    for i, small in enumerate(smalls):
        total += gathered(small, features[...], feature_columns[...], 6 * i)
    return total


def ring_copies(where, axis, places, parts, whole, sems, rows=384):
    return [
        (p.at[pl.ds(0, rows)], whole.at[at_hops(where, axis, hops), pl.ds(0, rows)], sems.at[i])
        for i, (hops, p) in enumerate(zip(places, parts))
    ]


def bring(where, ones, twos, one, two, sems):
    copies = ring_copies(where, 1, FROM, ones, one, sems.at[0])
    copies += ring_copies(where, 0, FROM, twos, two, sems.at[1])
    copies = [pltpu.make_async_copy(*c) for c in copies]
    for copy in copies:
        copy.start()
    return copies


def send(where, axis, parts, whole, sems, rows=384):
    copies = ring_copies(where, axis, range(4), parts, whole, sems, rows)
    copies = [pltpu.make_async_copy(place, part, sem) for part, place, sem in copies]
    for copy in copies:
        copy.start()
    return copies


def by_group(one, two, group):
    x, zh = group // 2, lax.rem(group, 2)
    held = ([], [])
    for y in range(4):
        for zl in range(2):
            z = zh * 2 + zl
            held[0].append(one[y, pl.ds(pl.multiple_of((x * 4 + z) * 24, 8), 24)])
            held[1].append(two[x, pl.ds(pl.multiple_of((y * 4 + z) * 24, 8), 24)])
    return held


def unpack_attn(one, two, q_hi, q_lo, kv_hi, kv_lo, o_hi, o_lo):
    def step(group, carry):
        held = by_group(one, two, group)

        def rows(part, first):
            return jnp.concatenate([h[first : first + 6] for h in held[part]], axis=0)

        for c in range(2):
            at = pl.ds(pl.multiple_of(group * 96 + c * 48, 16), 48)
            q_hi[at, :], q_lo[at, :] = split(rows(0, 6 * c))
            kv_hi[at, :384], kv_lo[at, :384] = split(rows(0, 12 + 6 * c))
            kv_hi[at, 384:], kv_lo[at, 384:] = split(rows(1, 6 * c))
            at = pl.ds(pl.multiple_of(group * 48, 16), 48)
            lanes = pl.ds(384 * c, 384)
            o_hi[at, lanes], o_lo[at, lanes] = split(rows(1, 12 + 6 * c))
        return carry

    lax.fori_loop(0, 8, step, 0)


def unpack_up(one, two, up_hi, up_lo):
    def step(group, carry):
        held = by_group(one, two, group)
        for c in range(2):
            at = pl.ds(pl.multiple_of(group * 96 + c * 48, 16), 48)
            for part in range(2):
                for b in range(2):
                    first = 12 * b + 6 * c
                    rows = jnp.concatenate([h[first : first + 6] for h in held[part]], axis=0)
                    lanes = pl.ds(768 * part + 384 * b, 384)
                    up_hi[at, lanes], up_lo[at, lanes] = split(rows)
        return carry

    lax.fori_loop(0, 8, step, 0)


def place_in_blocks(one, two, first, second):
    for group in range(8):
        x, zh = group // 2, group % 2
        for y in range(4):
            for zl in range(2):
                z, j = zh * 2 + zl, y * 2 + zl

                def rows(array):
                    at = [group * 96 + 48 * c + 6 * j for c in range(2)]
                    return [array[a : a + 6] for a in at]

                if first is not None:
                    one[y, (x * 4 + z) * 24 : (x * 4 + z) * 24 + 24] = jnp.concatenate(
                        rows(first[0]) + rows(first[1]), axis=0
                    )
                if second is not None:
                    ends = second[1]
                    if ends.shape[0] == 768:
                        ends = rows(ends)
                    else:
                        ends = ends[group * 48 + 6 * j : group * 48 + 6 * j + 6]
                        ends = [ends[:, :384], ends[:, 384:]]
                    two[x, (y * 4 + z) * 24 : (y * 4 + z) * 24 + 24] = jnp.concatenate(
                        rows(second[0]) + ends, axis=0
                    )


def sum_kernel(where, a0, a1, b0, b1, b2, a_sum, b_sum):
    a_sum[...] = a0[...] + a1[...]
    b_sum[...] = b0[...] + b1[...] + b2[...]


def part_one_kernel(axis, where, a0, a1, b0, *more):
    skip = 8 if axis == 0 else 0
    if skip:
        lines = a0[384:392, :256] + a1[384:392, :256]
        row = lax.broadcasted_iota(jnp.int32, (8, 128), 0)
    for hops, out in enumerate(more[-4:]):
        at = at_hops(where, axis, hops)
        for z in range(4):
            rows = pl.ds(pl.multiple_of(at * 96 + 24 * z, 8), 24)
            out[z, 0:24] = a0[rows] + a1[rows]
            if skip:
                line = lines[:, 128 * (z % 2) : 128 * (z % 2) + 128]
                line = jnp.sum(jnp.where(row == at * 2 + z // 2, line, 0.0), axis=0, keepdims=True)
                out[z, 24:32] = jnp.concatenate(
                    [jnp.broadcast_to(line, (8, 128)), jnp.zeros((8, 256), F32)], axis=1
                )
            out[z, 24 + skip : 48 + skip] = b0[rows]


def part_down_kernel(axis, where, down, *outs):
    for hops, out in enumerate(outs):
        out[...] = down[at_hops(where, axis, hops)]


def add_one_kernel(where, a0, a1, total):
    total[...] = a0[...] + a1[...]


def part_two_kernel(where, a0, a1, b0, b1, o0, o1, o2, o3):
    for k, out in enumerate((o0, o1, o2, o3)):
        z = lax.rem(where[2] + k, 4)
        out[:HALF_ONE] = a0[z] + a1[z]
        out[HALF_ONE:] = b0[z] + b1[z]


def sum_three_kernel(where, a0, a1, a2, a3, out, kept, sent):
    block = (a0[...] + a1[...]) + (a2[...] + a3[...])
    out[...] = jnp.concatenate([block[68:74], block[74:80]], axis=1)
    line = block[24:25, :128]
    both = []
    for c in range(2):
        rows = [block[at + 6 * c : at + 6 * c + 6] for at in (0, 12, 56, 32, 44, 80, 92)]
        vec = line if c == 0 else pltpu.roll(line, 64, 1)
        vec = jnp.concatenate([jnp.broadcast_to(vec, (6, 128)), jnp.zeros((6, 256), F32)], axis=1)
        both.append(jnp.concatenate(rows + [vec], axis=0))
    first = where[3] == 0
    kept[...] = jnp.where(first, both[0], both[1])
    sent[...] = jnp.where(first, both[1], both[0])


def finish_kernel(where, kept, got, q, k, v, up, *vectors):
    first = where[3] == 0
    one = jnp.where(first, kept[...], got[...])
    two = jnp.where(first, got[...], kept[...])
    for i, ref in enumerate((q, k, v)):
        ref[...] = joined(one[6 * i : 6 * i + 6], two[6 * i : 6 * i + 6], 48)
    wide = [
        jnp.concatenate([h[18 + 6 * i : 24 + 6 * i] for i in range(4)], axis=1) for h in (one, two)
    ]
    up[...] = joined(wide[0], wide[1], 192)
    line = one[42:43, :128] + two[42:43, :128]
    for i, ref in enumerate(vectors):
        ref[...] = line[:, 6 * i : 6 * i + ref.shape[1]]


def toeplitz(base):
    return pltpu.roll(jnp.broadcast_to(base, (TOK, 2 * TOK)), 0, 1, stride=1, stride_axis=0)


def fetch_pair(where, mine, other, held, first, sems):
    core = where[3]
    return fetch(
        (mine, other),
        [held.at[pl.ds(pl.multiple_of(first + c * TOK, TOK), TOK)] for c in (core, 1 - core)],
        sems,
    )


def fetch(refs, held, sems):
    copies = [pltpu.make_async_copy(r, h, sems.at[i]) for i, (r, h) in enumerate(zip(refs, held))]
    for copy in copies:
        copy.start()
    return copies


def wait(copies):
    for copy in copies:
        copy.wait()


ATTN_HELD = (
    (((768, 384), BF16),) * 2
    + (((768, 768), BF16),) * 2
    + (((384, 768), BF16),) * 2
    + (((512, 384), F32),) * 3
    + (((768, 384), F32),) * 2
)


def norm_kernel(where, halo, tokens, others, xhat_ref, xt_hi_far, xt_lo_far, x_ref, xt_hi, xt_lo, sems):
    fetched = fetch((halo,), (x_ref.at[pl.ds(0, TOK)],), sems)
    fetched += fetch_pair(where, tokens, others, x_ref, TOK, sems.at[pl.ds(1, 2)])
    wait(fetched)
    xhat, _ = normal_parts(x_ref[...])
    xhat_ref[...] = xhat
    xt_hi[...], xt_lo[...] = split(xhat.T)
    wait(fetch((xt_hi, xt_lo), (xt_hi_far, xt_lo_far), sems.at[pl.ds(3, 2)]))


def attn_kernel(
    where, xhat_ref, valid_ref, features, offsets, a0, a1, a2, a3, b0, b1, b2, b3,
    part_far, vec_ref, base_ref, *more,
):
    outs, held = more[:11], more[11:22]
    part_ref, one, two, lines, sems, out_sems, half_sems, line_sems = more[22:]
    q_hi, q_lo, kv_hi, kv_lo, o_hi, o_lo, sig_ref, ratio_ref, below_ref, w_ref, v_ref = held

    def keep(first, count):
        at = slice(first, first + count)
        return fetch(held[at], outs[at], out_sems.at[pl.ds(first, count)])

    fetched = fetch(
        [a.at[pl.ds(384, 8)] for a in (a0, a1, a2, a3)], [lines.at[k] for k in range(4)], line_sems
    )
    copies = bring(where, (a0, a1, a2, a3), (b0, b1, b2, b3), one, two, sems)
    wait(fetched)
    picked, base = spread_vectors(where, [lines[k] for k in range(4)], features[...], offsets[...])
    vec_ref[...] = jnp.concatenate(picked + [jnp.zeros((4, 768), F32)], axis=0)
    base_ref[...] = jnp.broadcast_to(base, (8, 512))
    wait(copies)
    unpack_attn(one, two, q_hi, q_lo, kv_hi, kv_lo, o_hi, o_lo)
    kept = keep(0, 6)
    gain, offset = picked[:2]
    parts = split(xhat_ref[...] * gain + offset)
    own = tuple(p[TOK:] for p in parts)
    keys = dot3(parts, (kv_hi[...], kv_lo[...]))
    sig_ref[...] = jax.nn.sigmoid(dot3(own, (q_hi[...], q_lo[...])))
    w = jnp.exp(keys[:, :384])
    w_ref[:TOK] = jnp.where(valid_ref[0] > 0.0, w[:TOK], 0.0)
    w_ref[TOK:] = w[TOK:]
    v_ref[...] = keys[:, 384:]
    kept += keep(6, 1) + keep(9, 2)
    w = w_ref[...]
    sums = split(jnp.concatenate([w * v_ref[...], w], axis=1))
    band = split(toeplitz(base))
    for i in range(2):
        at, half = slice(TOK * i, TOK * i + TOK), pl.ds(TOK * i, TOK)
        seen = tuple(s[TOK * i : TOK * i + 2 * TOK] for s in sums)
        mixed = dot3(band, seen)
        below_ref[at] = mixed[:, 384:]
        ratio_ref[at] = mixed[:, :384] / mixed[:, 384:]
        for j in (7, 8):
            kept += fetch((held[j].at[half],), (outs[j].at[half],), half_sems.at[i, pl.ds(j - 7, 1)])
        mixed = split(sig_ref[at] * ratio_ref[at])
        part_ref[at] = dot3(mixed, (o_hi[...], o_lo[...]))
        kept += fetch((part_ref.at[half],), (part_far.at[half],), half_sems.at[i, pl.ds(2, 1)])
    wait(kept)


def fetch_down(down_far, down, sems):
    return fetch([down_far.at[z] for z in range(4)], [down.at[z] for z in range(4)], sems)


def unpack_down(fetched, down, down_hi, down_lo):
    for zh in range(2):
        wait(fetched[2 * zh : 2 * zh + 2])
        for x in range(4):
            for y in range(4):
                rows = jnp.concatenate([down[2 * zh + zl, y, x] for zl in range(2)], axis=0)
                at = pl.ds(((x * 2 + zh) * 4 + y) * 48, 48)
                down_hi[at, :], down_lo[at, :] = split(rows)


def ffn_early_kernel(
    where, down_far, mine, other, gh_ref, down, down_hi, down_lo, cot_ref, cot_sems, in_sems
):
    kept = fetch_down(down_far, down, in_sems)
    fetched = fetch_pair(where, mine, other, cot_ref, 0, cot_sems)
    unpack_down(kept, down, down_hi, down_lo)
    wait(fetched)
    cot = split(cot_ref[...])
    for i in range(2):
        at = slice(768 * i, 768 * i + 768)
        gh_ref[:, at] = dot3(cot, (down_hi[at], down_lo[at]), NT)


def ffn_kernel(
    where, tokens, others, mine_far, theirs_ref, vec_ref, gh_ref, a0, a1, a2, a3, b0, b1, b2, b3,
    middle_far, middle_own, nt_hi, nt_lo, h_hi, h_lo, g_hi, g_lo, back_far,
    middle_ref, back_ref, x_ref, mine_ref, one, two, up_hi, up_lo, sems, in_sems, out_sems,
):
    fetched = fetch((mine_far,), (mine_ref,), in_sems)
    fetched += fetch_pair(where, tokens, others, x_ref, 0, in_sems.at[pl.ds(2, 2)])
    wait(bring(where, (a0, a1, a2, a3), (b0, b1, b2, b3), one, two, sems))
    unpack_up(one, two, up_hi, up_lo)
    wait(fetched)
    middle_ref[...] = x_ref[...] + (mine_ref[...] + theirs_ref[...])
    own = pl.ds(pl.multiple_of(where[3] * TOK, TOK), TOK)
    sent = fetch((middle_ref, middle_ref.at[own]), (middle_far, middle_own), out_sems)
    xhat, _ = normal_parts(middle_ref[...])
    normed = xhat * vec_ref[2:3, :] + vec_ref[3:4, :]
    parts = split(normed)
    nt_hi[...], nt_lo[...] = split(normed.T)
    halves = [pl.ds(TOK * c, TOK) for c in range(2)]
    for c, rows in enumerate((slice(0, TOK), slice(TOK, 2 * TOK))):
        for i in range(6):
            at = slice(256 * i, 256 * i + 256)
            preact = dot3(tuple(p[rows] for p in parts), (up_hi[:, at], up_lo[:, at]))
            lower, density = normal_cdf(preact)
            slope = lower + preact * density
            h_hi[rows, at], h_lo[rows, at] = split(preact * lower)
            g_hi[rows, at], g_lo[rows, at] = split(gh_ref[rows, at] * slope)
        back_ref[rows] = dot3((g_hi[rows], g_lo[rows]), (up_hi[...], up_lo[...]), NT)
        sent += fetch((back_ref.at[halves[c]],), (back_far.at[halves[c]],), out_sems.at[pl.ds(2 + c, 1)])
    wait(sent)


def ffn_late_kernel(
    where, cot_mine, cot_other, nt_hi, nt_lo, h_hi, h_lo, g_hi, g_lo,
    down_grad_far, a0, a1, a2, a3, b0, b1, b2, b3, one, two, sems, cot_ref, down_grad,
    in_sems, out_sems,
):
    fetched = fetch_pair(where, cot_mine, cot_other, cot_ref, 0, in_sems)
    nt = (nt_hi[...], nt_lo[...])
    sent = []
    wait(fetched)
    cot = split(cot_ref[...])
    for i in range(2):
        at = slice(768 * i, 768 * i + 768)
        rows = dot3((h_hi[:, at].T, h_lo[:, at].T), cot)
        for chip in range(32):
            x, zh, y, zl = (2 * i + chip // 16), chip // 8 % 2, chip // 2 % 4, chip % 2
            down_grad[2 * zh + zl, y, x] = rows[chip * 24 : chip * 24 + 24]
        for place in range(16):
            part = (place // 4, place % 4, pl.ds(2 * i, 2))
            sem = out_sems.at[i * 16 + place]
            sent.append(pltpu.make_async_copy(down_grad.at[part], down_grad_far.at[part], sem))
            sent[-1].start()
    for i in range(2):
        at = slice(768 * i, 768 * i + 768)
        grad = dot3(nt, (g_hi[:, at], g_lo[:, at]))
        pair = (grad[:, :384], grad[:, 384:])
        place_in_blocks(one, two, *((pair, None) if i == 0 else (None, pair)))
        sent += send(where, 1 - i, ((a0, a1, a2, a3), (b0, b1, b2, b3))[i], (one, two)[i], sems.at[i])
    wait(sent)


def out_kernel(
    where, h_hi_far, h_lo_far, down_far, own, other,
    h_hi, h_lo, down, down_hi, down_lo, out_ref, sems, in_sems, out_sems,
):
    kept = fetch_down(down_far, down, in_sems)
    fetched = fetch((h_hi_far, h_lo_far), (h_hi, h_lo), sems)
    unpack_down(kept, down, down_hi, down_lo)
    wait(fetched)
    for i in range(2):
        at = slice(768 * i, 768 * i + 768)
        out = dot3((h_hi[:, at], h_lo[:, at]), (down_hi[at], down_lo[at]))
        if i == 0:
            out_ref[...] = out
        else:
            out_ref[...] += out
    places = [pl.ds(pl.multiple_of(TOK * c, TOK), TOK) for c in (where[3], 1 - where[3])]
    wait(fetch([out_ref.at[p] for p in places], (own, other), out_sems))


def attn_back_kernel(
    where, vec_ref, base_ref, middle_far, mine_far, theirs_ref, cot_mine, cot_other,
    f0, f1, f2, f3, f4, f5, f6, gmid_own, gq_ref, gkv_ref, out_grad, small_ref, bias_ref,
    middle_ref, mine_ref, cot_ref, gmid_ref,
    o_hi, o_lo, sig_ref, ratio_ref, below_ref, w_ref, v_ref, sems, out_sems,
):
    halves = [pl.ds(TOK * c, TOK) for c in range(2)]
    first = [
        fetch([far.at[p] for p in halves], [ref.at[p] for p in halves], sems.at[pl.ds(9 + 2 * i, 2)])
        for i, (far, ref) in enumerate(((middle_far, middle_ref), (mine_far, mine_ref)))
    ]
    copies = fetch_pair(where, cot_mine, cot_other, cot_ref, 0, sems)
    copies += fetch((f0, f1), (o_hi, o_lo), sems.at[pl.ds(2, 2)])
    wait(first[0])
    xhat, scale = normal_parts(middle_ref[...])
    wait(first[1])
    kept = fetch(
        (f2, f3, f4, f5, f6), (sig_ref, ratio_ref, below_ref, w_ref, v_ref), sems.at[pl.ds(4, 5)]
    )
    mine = mine_ref[...]
    small_ref[2:3, :] = jnp.sum(mine * xhat, axis=0, keepdims=True)
    small_ref[3:4, :] = jnp.sum(mine, axis=0, keepdims=True)
    gmid = normal_back(mine + theirs_ref[...], xhat, scale, vec_ref[2:3, :])
    wait(copies)
    gmid = cot_ref[...] + gmid
    gmid_ref[...] = gmid
    gmid = split(gmid)
    own = pl.ds(pl.multiple_of(where[3] * TOK, TOK), TOK)
    sent = fetch((gmid_ref.at[own],), (gmid_own,), out_sems)
    gmixed = dot3(gmid, (o_hi[...], o_lo[...]), NT)
    wait(kept)
    sig, ratio = sig_ref[...], ratio_ref[...]
    out_grad[...] = dot3(split((sig * ratio).T), gmid)
    gq = gmixed * ratio * sig * (1.0 - sig)
    gq_ref[...] = gq
    gnum = gmixed * sig / below_ref[...]
    gsums = split(jnp.concatenate([gnum, -gnum * ratio], axis=1))
    band = toeplitz(base_ref[0:1, :])
    band_t = split(band.T)
    w, v = w_ref[...], v_ref[...]
    sums = split(jnp.concatenate([w * v, w], axis=1))
    spread, gband = [], None
    for i in range(2):
        here = tuple(g[TOK * i : TOK * i + TOK] for g in gsums)
        seen = tuple(s[TOK * i : TOK * i + 2 * TOK] for s in sums)
        spread.append(dot3(band_t, here))
        term = dot3(here, seen, NT)
        gband = term if gband is None else gband + term
    count = TOK
    while count > 1:
        count //= 2
        gband = gband[:count] + pltpu.roll(gband[count:], 2 * TOK - count, 1)
    bias_ref[...] = jnp.broadcast_to(gband * base_ref[0:1, :], (8, 2 * TOK))
    gseen = jnp.concatenate(
        [spread[0][:TOK], spread[0][TOK:] + spread[1][:TOK], spread[1][TOK:]], axis=0
    )
    gkv = jnp.concatenate([w * (gseen[:, :384] * v + gseen[:, 384:]), gseen[:, :384] * w], axis=1)
    gkv_ref[...] = gkv
    wait(sent)


def attn_grads_kernel(
    where, vec_ref, gq_ref, gkv_ref, out_grad, small_two, bias, features, offsets, feature_columns,
    offset_columns, f0, f1, f2, f3, f4, f5, a0, a1, a2, a3, b0, b1, b2, b3,
    one, two, sems, q_hi, q_lo, kv_hi, kv_lo, xt_hi, xt_lo, in_sems, line_sems,
):
    kept = fetch((f4, f5, f0, f1, f2, f3), (xt_hi, xt_lo, q_hi, q_lo, kv_hi, kv_lo), in_sems)
    gq, gkv = gq_ref[...], gkv_ref[...]
    vec = vec_ref[...].T
    wait(kept[:2])
    small = [0.0, 0.0]

    def grad_of(dots, g):
        total = jnp.sum(g, axis=0, keepdims=True)
        return vec[:, 0:1] * dots + vec[:, 1:2] * total

    def add_small(dots, g, high, low):
        weight = high[...].astype(F32) + low[...].astype(F32)
        total = jnp.sum(g, axis=0, keepdims=True)
        small[0] += jnp.sum(dots * weight, axis=1, keepdims=True)
        small[1] += jnp.sum(total * weight, axis=1, keepdims=True)

    kv_dot = dot3((xt_hi[...], xt_lo[...]), split(gkv))
    kv_grad = grad_of(kv_dot, gkv)
    place_in_blocks(one, two, None, (kv_grad[:, 384:], out_grad[...]))
    sent = send(where, 0, (b0, b1, b2, b3), two, sems.at[1])
    q_dot = dot3((xt_hi[:, TOK:], xt_lo[:, TOK:]), split(gq))
    place_in_blocks(one, two, (grad_of(q_dot, gq), kv_grad[:, :384]), None)
    sent += send(where, 1, (a0, a1, a2, a3), one, sems.at[0], 384)
    wait(kept[2:])
    add_small(kv_dot, gkv, kv_hi, kv_lo)
    add_small(q_dot, gq, q_hi, q_lo)
    small = jnp.concatenate(small + [jnp.zeros((768, 126), F32)], axis=1).T
    smalls = (small[0:1], small[1:2], small_two[2:3, :], small_two[3:4, :])
    lines = place_lines(
        where, smalls, bias[0:1, :], features, offsets, feature_columns, offset_columns
    )
    for k, part in enumerate((a0, a1, a2, a3)):
        line = lines[16 * k : 16 * k + 16]
        place = one.at[at_hops(where, 1, k), pl.ds(384, 8)]
        place[...] = jnp.concatenate([line[:8], line[8:], jnp.zeros((8, 128), F32)], axis=1)
        sent.append(pltpu.make_async_copy(place, part.at[pl.ds(384, 8)], line_sems.at[k]))
        sent[-1].start()
    wait(sent)


def attn_last_kernel(
    where, gq_ref, gkv_ref, f0, f1, f2, f3, own, other, halo_own, halo_other,
    q_hi, q_lo, kv_hi, kv_lo, back_ref, sems, out_sems,
):
    kept = fetch((f2, f3, f0, f1), (kv_hi, kv_lo, q_hi, q_lo), sems)
    gq, gkv = split(gq_ref[...]), split(gkv_ref[...])
    wait(kept)
    back_ref[...] = dot3(gkv, (kv_hi[...], kv_lo[...]), NT)
    back_ref[TOK:] += dot3(gq, (q_hi[...], q_lo[...]), NT)
    core, half = where[3], TOK // 2
    places = [(TOK * (1 + c), TOK) for c in (core, 1 - core)] + [
        (half * c, half) for c in (core, 1 - core)
    ]
    places = [back_ref.at[pl.ds(pl.multiple_of(at, half), n)] for at, n in places]
    wait(fetch(places, (own, other, halo_own, halo_other), out_sems))


def tokens_kernel(
    where, tokens, gmid, back, back_other, halo_low, halo_high, vec_ref, middle, out, out_other,
    out_ref, output_ref,
):
    output_ref[...] = middle[...] + (out[...] + out_other[...])
    back = back[...] + back_other[...]
    halo = jnp.concatenate([halo_low[...], halo_high[...]], axis=0)
    back = back + jnp.where(where[3] == 0, 0.0, halo)
    xhat, scale = normal_parts(tokens[...])
    out_ref[...] = gmid[...] + normal_back(back, xhat, scale, vec_ref[0:1, :])


def shaped(*shape, dtype=F32):
    return jax.ShapeDtypeStruct(shape, dtype)


def kept_near(*shape, dtype=F32):
    return pltpu.VMEM(shape, dtype)


def kept_far(*shape, dtype=F32):
    return pltpu.HBM(shape, dtype)


def near(array):
    return pltpu.with_memory_space_constraint(array, pltpu.VMEM)


def far(array):
    return pltpu.with_memory_space_constraint(array, pltpu.HBM)


def call(kernel, out_shape, args, specs, scratch=(), flops=0, moved=0, vmem=24, **more):
    return pl.pallas_call(
        kernel,
        out_shape=out_shape,
        in_specs=specs,
        scratch_shapes=list(scratch),
        compiler_params=pltpu.CompilerParams(vmem_limit_bytes=vmem * 1024 * 1024),
        cost_estimate=pl.CostEstimate(flops=flops, bytes_accessed=moved, transcendentals=0),
        **more,
    )(*args)


def glue(kernel, shapes, args, axis=None, given=near, gives=kept_near):
    if axis is not None:
        kernel = functools.partial(kernel, axis)
    return call(
        kernel,
        tuple((gives[i] if isinstance(gives, tuple) else gives)(*s) for i, s in enumerate(shapes)),
        (args[0], *map(given, args[1:])),
        [SM] + [VM] * (len(args) - 1),
        vmem=10,
    )


def after(arrays, *others):
    return lax.optimization_barrier((arrays, others))[0]


def phase(*arrays):
    return lax.optimization_barrier(arrays)


def shards(
    inputs, query_weight, key_weight, value_weight, out_weight, up_weight, down_weight,
    gain_one, offset_one, gain_two, offset_two, pos_bias, prefix_len, cotangent,
):
    x, y, core = lax.axis_index("x"), lax.axis_index("y"), lax.axis_index("core")
    zh, zl = lax.axis_index("zh"), lax.axis_index("zl")
    z = zh * 2 + zl
    where = jnp.stack([x, y, z, core]).astype(jnp.int32)
    first_core = core == 0
    dma = lambda *shape: pltpu.SemaphoreType.DMA(shape)
    places = (pltpu.VMEM((4, 384, 384), F32),) * 2 + (dma(2, 4),)
    pair16 = lambda *shape: (kept_near(*shape, dtype=BF16),) * 2
    grad_blocks = (kept_far(384, 384),) * 8
    tables = place_tables()

    with jax.named_scope("pack"):
        near_down = both_ways(down_weight, "x")
        vectors = [a[None] for a in (gain_one, offset_one, gain_two, offset_two, pos_bias)]
        kept, sent = glue(
            pack_one_kernel,
            ((48, 384),) * 2,
            (where, query_weight, key_weight, value_weight, up_weight, *vectors),
            given=far,
        )
        tokens, cot, near_down, sent = phase(inputs[0], cotangent[0], near_down, sent)
        got, far_down = swap_cores(sent), hop(near_down[0], "x")
        (block,) = glue(
            pack_two_kernel,
            ((104, 384),),
            (where, near(kept), near(got), far(out_weight)),
            given=lambda array: array,
        )
    with jax.named_scope("gather_z"):
        block, tokens, cot = phase(block, tokens, cot)
        seq = (x * 2 + zh) * 2 + core
        positions = seq * TOK + jnp.arange(TOK, dtype=jnp.int32)
        cot = cot * (positions >= prefix_len[0]).astype(F32)[:, None]
        block, cot, far_down = phase(gather_at_once(block, "z"), cot, far_down)
        one, two = glue(
            stack_one_kernel,
            ((4, HALF_ONE, 384), (4, HALF_TWO, 384)),
            (where, *block),
            given=lambda array: array,
            gives=shaped,
        )

    with jax.named_scope("gather_mid"):
        one, two, cot, tokens, far_down = phase(one, two, cot, tokens, far_down)
        (down,) = glue(
            stack_down_kernel,
            ((4, 24, 768),),
            (where, down_weight, *near_down, far_down),
            given=lambda array: array,
            gives=kept_far,
        )
        down = lax.all_gather(down, "y", axis=0)
        others = swap_cores(tokens)
        near_one, near_two, others = phase(both_ways(one, "x"), both_ways(two, "y"), others)
        halo = along_row(after(tokens, near_one), 1, (1,), (0,))
        far_one, far_two, halo = phase(hop(near_one[0], "x"), hop(near_two[0], "y"), halo)
        down = lax.all_gather(after(down, far_one), RING["z"], axis=0)
        attn_one, up_one, attn_two, up_two = glue(
            stack_both_kernel,
            ((392, 384), (384, 384), (384, 384), (384, 384)),
            (where, one, *near_one, far_one, two, *near_two, far_two),
            given=lambda array: array,
            gives=kept_far,
        )

    with jax.named_scope("gather_attn"):
        attn_one, attn_two, up_one, up_two = phase(attn_one, attn_two, up_one, up_two)
        near_one, near_two = phase(both_ways(attn_one, "y"), both_ways(attn_two, "x"))
        halo, cot = after((halo, cot), near_one)
        far_one, far_two = hop(near_one[0], "y"), hop(near_two[0], "x")
        cot_other = swap_cores(cot)
        halo = jnp.where(first_core, halo, swap_cores(halo))
        xhat, *xt = call(
            norm_kernel,
            (kept_near(768, 768),) + (kept_far(768, 768, dtype=BF16),) * 2,
            (where, *map(far, (halo, tokens, others))),
            [SM] + [HB] * 3,
            [pltpu.VMEM((768, 768), F32)] + [pltpu.VMEM((768, 768), BF16)] * 2 + [dma(5)],
            vmem=16,
            out_specs=(VM, HB, HB),
        )
        far_one, far_two, xhat, xt, cot_other = phase(far_one, far_two, xhat, xt, cot_other)
        attn_one = (attn_one, *near_one, far_one)
        attn_two = (attn_two, *near_two, far_two)
        valid = jnp.where(x * 2 + zh > 0, 1.0, 0.0).astype(F32).reshape(1)

    with jax.named_scope("attn"):
        attn_one, attn_two, up_one, up_two = phase(attn_one, attn_two, up_one, up_two)
        near_one, near_two = both_ways(up_one, "y"), both_ways(up_two, "x")
        part, vec, base, *held = call(
            attn_kernel,
            (kept_far(512, 768), shaped(8, 768), shaped(8, 512)) + tuple(kept_far(*h, dtype=t) for h, t in ATTN_HELD),
            (where, near(xhat), valid, *tables[:2], *map(far, attn_one + attn_two)),
            [SM, VM, SM, VM, VM] + [HB] * 8,
            [pltpu.VMEM(h, t) for h, t in ATTN_HELD]
            + [pltpu.VMEM((512, 768), F32), *places[:2], pltpu.VMEM((4, 8, 384), F32), places[2]]
            + [dma(11), dma(2, 3), dma(4)],
            flops=5_700_000_000,
            moved=1_000_000,
            vmem=36,
            out_specs=(HB, VM, VM) + (HB,) * 11,
        )
        near_one, near_two, part, held = phase(near_one, near_two, part, held)

    with jax.named_scope("ffn_early"):
        part_other = swap_cores(part)
        far_one, far_two = hop(near_one[0], "y"), hop(near_two[0], "x")
        gh = call(
            ffn_early_kernel,
            kept_near(512, 1536),
            (where, *map(far, (down, cot, cot_other))),
            [SM] + [HB] * 3,
            [pltpu.VMEM((4, 4, 4, 24, 768), F32)]
            + [pltpu.VMEM((1536, 768), BF16)] * 2
            + [pltpu.VMEM((512, 768), F32), dma(2), dma(4)],
            flops=3_600_000_000,
            moved=1_000_000,
            vmem=20,
        )
        down_full = down
        part_other, far_one, far_two, gh = phase(part_other, far_one, far_two, gh)
        up_all = (up_one, *near_one, far_one, up_two, *near_two, far_two)

    with jax.named_scope("ffn"):
        middle, middle_own, *ffn_held, back_part = call(
            ffn_kernel,
            (kept_far(512, 768), kept_far(256, 768))
            + pair16(768, 512)
            + pair16(512, 1536) * 2
            + (kept_far(512, 768),),
            (where, *map(far, (tokens, others, part)), part_other, vec, near(gh))
            + (*map(far, up_all[:3]), up_all[3], *map(far, up_all[4:7]), up_all[7]),
            [SM] + [HB] * 3 + [VM] * 3 + ([HB] * 3 + [ANY]) * 2,
            (pltpu.VMEM((512, 768), F32),) * 4
            + places[:2]
            + (pltpu.VMEM((768, 1536), BF16),) * 2
            + (places[2], dma(4), dma(4)),
            flops=7_200_000_000,
            moved=1_000_000,
            vmem=30,
            out_specs=(HB, HB) + (VM,) * 6 + (HB,),
        )
        back_other = swap_cores(back_part)
        down_grads, *up_grads = call(
            ffn_late_kernel,
            (kept_far(4, 4, 4, 24, 768),) + grad_blocks,
            (where, far(cot), far(cot_other), *map(near, ffn_held)),
            [SM] + [HB] * 2 + [VM] * 6,
            places
            + (pltpu.VMEM((512, 768), F32), pltpu.VMEM((4, 4, 4, 24, 768), F32), dma(2), dma(32)),
            flops=7_300_000_000,
            moved=1_000_000,
            vmem=24,
            out_specs=(HB,) * 9,
        )
        back_other, up_grads, down_grads = phase(back_other, up_grads, down_grads)

    with jax.named_scope("attn_back"):
        up_one, up_two = up_grads[:4], up_grads[4:]
        came = scatter_start(up_one, "y"), scatter_start(up_two, "x")
        q_w, kv_w, o_w, saved = held[:2], held[2:4], held[4:6], held[6:]
        gmid, gq, gkv, out_grad, small_two, bias = call(
            attn_back_kernel,
            (kept_far(256, 768), kept_near(512, 384), kept_near(768, 768), kept_near(384, 768))
            + (shaped(8, 768), shaped(8, 512)),
            (where, vec, base)
            + (far(middle), far(back_part), back_other)
            + tuple(map(far, (cot, cot_other, *o_w, *saved))),
            [SM] + [VM] * 2 + [HB] * 2 + [VM] + [HB] * 9,
            [pltpu.VMEM((512, 768), F32)] * 4
            + [pltpu.VMEM(h, t) for h, t in ATTN_HELD[4:]]
            + [dma(15), dma(1)],
            flops=5_000_000_000,
            moved=1_000_000,
            vmem=32,
            out_specs=(HB,) + (VM,) * 5,
        )
        down = lax.psum_scatter(down_grads, RING["z"], scatter_dimension=0, tiled=True)[0]
        came, gq, gkv, out_grad = phase(came, gq, gkv, out_grad)

    with jax.named_scope("attn_grads"):
        gq, gkv, out_grad = map(near, (gq, gkv, out_grad))
        up_one_came, up_two_came = scatter_end(where, up_one, up_two, came, "yx")
        attn_grads = call(
            attn_grads_kernel,
            (kept_far(392, 384),) * 4 + (kept_far(384, 384),) * 4,
            (where, vec, gq, gkv, out_grad, small_two, bias, *tables)
            + tuple(map(far, (*q_w, *kv_w, *xt))),
            [SM] + [VM] * 10 + [HB] * 6,
            [pltpu.VMEM((4, 392, 384), F32), *places[1:]]
            + [pltpu.VMEM(h, t) for h, t in ATTN_HELD[:4]]
            + [pltpu.VMEM((768, 768), BF16)] * 2
            + [dma(6), dma(4)],
            flops=3_600_000_000,
            moved=1_000_000,
            vmem=32,
            out_specs=(HB,) * 8,
        )
        up_one_came, up_two_came, attn_grads = phase(up_one_came, up_two_came, attn_grads)

    with jax.named_scope("attn_last"):
        attn_one, attn_two = attn_grads[:4], attn_grads[4:]
        came = scatter_start(attn_one, "y"), scatter_start(attn_two, "x")
        back_own, back_other, halo_own, halo_other = call(
            attn_last_kernel,
            (kept_far(256, 768),) * 2 + (kept_far(128, 768),) * 2,
            (where, gq, gkv, *map(far, (*q_w, *kv_w))),
            [SM] + [VM] * 2 + [HB] * 4,
            [pltpu.VMEM(h, t) for h, t in ATTN_HELD[:4]]
            + [pltpu.VMEM((768, 768), F32), dma(4), dma(4)],
            flops=3_600_000_000,
            moved=1_000_000,
            vmem=20,
            out_specs=(HB,) * 4,
        )
        halo_other = swap_cores(halo_other)
        came, back_own, back_other, halo_own, halo_other, down = phase(
            came, back_own, back_other, halo_own, halo_other, down
        )
        down = lax.psum_scatter(down, "y", scatter_dimension=0, tiled=True)[0]

    with jax.named_scope("scatter_attn"):
        attn_one_came, attn_two_came = scatter_end(where, attn_one, attn_two, came, "yx")
        out_own, out_other = call(
            out_kernel,
            (kept_far(256, 768),) * 2,
            (where, *map(far, (*ffn_held[2:4], down_full))),
            [SM] + [HB] * 3,
            [pltpu.VMEM((512, 1536), BF16)] * 2
            + [pltpu.VMEM((4, 4, 4, 24, 768), F32)]
            + [pltpu.VMEM((1536, 768), BF16)] * 2
            + [pltpu.VMEM((512, 768), F32), dma(2), dma(4), dma(2)],
            flops=3_600_000_000,
            moved=1_000_000,
            vmem=24,
            out_specs=(HB,) * 2,
        )
        back_other = swap_cores(back_other)
        halo_high = along_row(halo_own + halo_other, -1, (0, 1), (0, 1))
        sums = [
            glue(
                sum_kernel,
                (attn[0].shape, up[0].shape),
                (where, attn[0], attn_came[0], up[0], *up_came),
                given=far,
                gives=kept_far,
            )
            for attn, attn_came, up, up_came in (
                (attn_one, attn_one_came, up_one, up_one_came),
                (attn_two, attn_two_came, up_two, up_two_came),
            )
        ]
        attn_one_came, attn_two_came, out_own, out_other, halo_high, back_other, sums = phase(
            attn_one_came, attn_two_came, out_own, out_other, halo_high, back_other, sums
        )

    now_and_later = (kept_far,) * 2 + (shaped,) * 2

    as_is = lambda array: array

    with jax.named_scope("scatter_mid"):
        one = glue(
            part_one_kernel,
            ((4, HALF_ONE, 384),) * 4,
            (where, far(sums[0][0]), attn_one_came[1], far(sums[0][1])),
            0,
            given=as_is,
            gives=now_and_later,
        )
        two = glue(
            part_one_kernel,
            ((4, HALF_TWO, 384),) * 4,
            (where, far(sums[1][0]), attn_two_came[1], far(sums[1][1])),
            1,
            given=as_is,
            gives=now_and_later,
        )
        came = scatter_start(one, "x"), scatter_start(two, "y")
        out_other = swap_cores(out_other)
        came, one, two, down, out_other = phase(came, one, two, down, out_other)

        one_own, one_next, two_own, two_next = glue(
            add_both_kernel,
            (one[0].shape,) * 2 + (two[0].shape,) * 2,
            (where, far(one[0]), far(one[1]), *came[0], far(two[0]), far(two[1]), *came[1]),
            given=as_is,
            gives=(kept_far, shaped) * 2,
        )
        one_came, two_came = hop(one_next, "x"), hop(two_next, "y")
        down = glue(part_down_kernel, ((24, 768),) * 4, (where, down), 0, given=far)
        down_came = scatter_start(down, "x")
        one_came, two_came, down_came, down, one_own, two_own = phase(
            one_came, two_came, down_came, down, one_own, two_own
        )

    with jax.named_scope("scatter_z"):
        block = glue(
            part_two_kernel,
            ((104, 384),) * 4,
            (where, far(one_own), one_came, far(two_own), two_came),
            given=as_is,
            gives=shaped,
        )
        (next_down,) = glue(add_one_kernel, ((24, 768),), (where, down[1], down_came[0]))
        block, next_down = phase(block, next_down)
        block = scatter_at_once(block, "z")
        next_down = hop(next_down, "x")
        halo_low = swap_cores(halo_high)
        gmid = after(gmid, next_down)
        input_grad, output = glue(
            tokens_kernel,
            ((256, 768),) * 2,
            (where, inputs[0], gmid, back_own, back_other, halo_low, halo_high, vec)
            + (middle_own, out_own, out_other),
            given=as_is,
            gives=shaped,
        )
        down = down[0] + down_came[1] + next_down
        block, down, input_grad, output = phase(block, down, input_grad, output)

    with jax.named_scope("finish"):
        out_grad, kept, sent = glue(
            sum_three_kernel,
            ((6, 768), (48, 384), (48, 384)),
            (where, *block),
            given=as_is,
            gives=(shaped,) * 3,
        )
        got = swap_cores(sent)
        *qkv, up_out = glue(
            finish_kernel,
            ((6, 768),) * 3 + ((6, 3072),) + ((1, 6),) * 4 + ((1, 2),),
            (where, kept, got),
            gives=shaped,
        )
        qkv, up_out, vectors = qkv[:3], qkv[3], [v[0] for v in (*qkv[4:], up_out)]

    return (
        output[None], input_grad[None], *qkv, out_grad, up_out, down,
        *vectors,
    )


def solution(mesh):
    fine = Mesh(mesh.devices.reshape(4, 2, 2, 4, 2), AXES)
    tokens = P(("y", "zl"), ("x", "zh", "core"), None)
    matrix = P(AXES, None)
    vector = P(AXES)
    return jax.shard_map(
        shards,
        mesh=fine,
        in_specs=(tokens,) + (matrix,) * 6 + (vector,) * 5 + (P(("y", "zl")), tokens),
        out_specs=(tokens, tokens) + (matrix,) * 6 + (vector,) * 5,
        check_vma=False,
    )
```
